128 devices in a mesh: dp: 16 (over x, z), row: 4 (over y_lo, core), col: 2 (over y_hi).
Axes of the slice: x: 4, y: 4 (y_hi: 2, y_lo: 2; y = y_hi * 2 + y_lo), z: 4, core: 2. Of those that a mesh axis runs over, the one named last changes fastest.
Arguments:
- tokens: bfloat16 [16, 1024, 1536], P('dp', 'col', 'row'), may hold values from -6 to 6
- gain1: float32 [1536], P('row'), may hold values from 0.1 to 1.9
- w_query: bfloat16 [1536, 1536], P('row', 'col'), may hold values from -0.15625 to 0.15625
- w_keyval: bfloat16 [1536, 1536], P('row', 'col'), may hold values from -0.15625 to 0.15625
- w_out: bfloat16 [1536, 1536], P('col', 'row'), may hold values from -0.4375 to 0.4375
- gain2: float32 [1536], P('row'), may hold values from 0.1 to 1.9
- w_gate: bfloat16 [1536, 4096], P('row', 'col'), may hold values from -0.15625 to 0.15625
- w_up: bfloat16 [1536, 4096], P('row', 'col'), may hold values from -0.15625 to 0.15625
- w_down: bfloat16 [4096, 1536], P('col', 'row'), may hold values from -0.09375 to 0.09375
- grad_out: bfloat16 [16, 1024, 1536], P('dp', 'col', 'row'), may hold values from -6 to 6
- segments: int32 [16, 1024], P('dp'), may hold values from 0 to 3, as said below
Outputs:
- output: bfloat16 [16, 1024, 1536], P('dp', 'col', 'row')
- grad_in: float32 [16, 1024, 1536], P('dp', 'col', 'row')
- grad_gain1: float32 [1536], P('row')
- grad_w_query: float32 [1536, 1536], P('row', 'col')
- grad_w_keyval: float32 [1536, 1536], P('row', 'col')
- grad_w_out: float32 [1536, 1536], P('col', 'row')
- grad_gain2: float32 [1536], P('row')
- gate_weight_gradient: float32 [1536, 4096], P('row', 'col')
- up_weight_gradient: float32 [1536, 4096], P('row', 'col')
- grad_w_down: float32 [4096, 1536], P('col', 'row')
The draws below stay inside these ranges and needn't reach their ends.
Inputs may be any that keep to these rules, and one draw needn't show every extreme that they name: `segments`: in each sequence the numbers start at 0, never fall and rise by one at each document start; each sequence holds 4 documents, which start at multiples of 64 and never at 512.
All inputs are finite; a program needn't handle non-finite values.
Results may differ from the reference program's by a relative error of at most 0.025.
Values may be sent and summed in bfloat16 or wider, within the bound.
No kernel may reach another device: no remote copies, remote signals or barrier semaphores. Data moves between devices by JAX's collectives and lax.ppermute only.
A program may use at most 128 MiB of HBM per device.

```python
import jax
import jax.numpy as jnp
import numpy as np
from jax import lax

D = 1536
Q = 16
KV = 8
HD = 96
FF = 4096
SEQ_LEN = 1024
NDOC = 4
QBLK = 512
GQ = 2
BATCH = 16


def draw_segments(key, part):
    key = jax.random.fold_in(key, 11)
    spacing = SEQ_LEN // 16
    places = jnp.arange(SEQ_LEN, dtype=jnp.int32)
    candidates = jnp.array(np.array([1, 2, 3, 4, 5, 6, 7, 9, 10, 11, 12, 13, 14, 15], dtype=np.int32))

    def one_sequence(subkey):
        order = jax.random.permutation(subkey, 14)
        bounds = candidates[order[:NDOC - 1]] * spacing
        return jnp.sum((places[:, None] >= bounds[None, :]).astype(jnp.int32), axis=1).astype(jnp.int32)
    return jax.vmap(one_sequence)(jax.random.split(key, BATCH))


def block_scale(stream_key, extent, cuts, smallest, largest):
    def one(position, blocks):
        heights = jax.random.uniform(jax.random.fold_in(jax.random.fold_in(stream_key, 6), position), (blocks,), jnp.float32, smallest / len(cuts), largest / len(cuts))
        return jnp.repeat(jnp.exp(heights), extent[position] // blocks).reshape((-1,) + (1,) * (len(extent) - position - 1))

    factor_of = one(*cuts[0])
    for cut in cuts[1:]:
        factor_of = factor_of * one(*cut)
    return factor_of


def centred(own_key, shape, spread, bound, pieces=(), held_as=jnp.bfloat16):
    drawn = spread * jax.random.normal(own_key, shape, jnp.float32)
    if pieces:
        drawn = drawn * block_scale(own_key, shape, pieces, -0.22, 0.18)
    return jnp.clip(drawn, -bound, bound).astype(held_as)


def setup_inputs(seed: int = 0) -> dict:
    key_of = jax.random.split(jax.random.key(seed), 12)
    return {
        "tokens": centred(key_of[0], (BATCH, SEQ_LEN, D), 1.0, 6.0, ((0, 16), (1, 2), (2, 4))),
        "gain1": jnp.clip(1.0 + 0.18 * jax.random.normal(key_of[1], (D,), jnp.float32), 0.1, 1.9),
        "w_query": centred(key_of[2], (D, Q * HD), D ** -0.5, 0.15625, ((0, 4), (1, 2))),
        "w_keyval": centred(key_of[3], (D, 2 * KV * HD), D ** -0.5, 0.15625, ((0, 4), (1, 2))),
        "w_out": centred(key_of[4], (Q * HD, D), (Q * HD // 8) ** -0.5, 0.4375, ((0, 2), (1, 4))),
        "gain2": jnp.clip(1.0 + 0.18 * jax.random.normal(key_of[5], (D,), jnp.float32), 0.1, 1.9),
        "w_gate": centred(key_of[6], (D, FF), D ** -0.5, 0.15625, ((0, 4), (1, 2))),
        "w_up": centred(key_of[7], (D, FF), D ** -0.5, 0.15625, ((0, 4), (1, 2))),
        "w_down": centred(key_of[8], (FF, D), FF ** -0.5, 0.09375, ((0, 2), (1, 4))),
        "grad_out": centred(key_of[9], (BATCH, SEQ_LEN, D), 1.0, 6.0, ((0, 16), (1, 2), (2, 4))),
        "segments": draw_segments(jax.random.fold_in(key_of[11], 71), 0),
    }


EPS = 1e-05
THETA = 100000.0

@jax.custom_vjp
def low(v):
    return lax.optimization_barrier(v.astype(jnp.bfloat16)).astype(jnp.float32)

@jax.custom_vjp
def low_back(v):
    return v

def low_keep(v):
    return (low(v), None)

def low_pass(kept, grad):
    return (grad,)

def back_keep(v):
    return (v, None)

def back_low(kept, grad):
    return (low(grad),)
low.defvjp(low_keep, low_pass)
low_back.defvjp(back_keep, back_low)

def highest(left, right):
    return jnp.dot(left, right, precision=lax.Precision.HIGHEST, preferred_element_type=jnp.float32)

def rms_norm(values, gain):
    scaled = values * lax.rsqrt(lax.optimization_barrier(jnp.mean(values * values, axis=-1, keepdims=True)) + EPS)
    return scaled * gain

def rope_tables(segment_ids):
    places = jnp.arange(SEQ_LEN, dtype=jnp.int32)
    starts = jnp.concatenate([jnp.ones((1,), dtype=bool), segment_ids[1:] != segment_ids[:-1]])
    leading_factor = lax.cummax(jnp.where(starts, places, 0), axis=0)
    rates = THETA ** (-jnp.arange(HD // 2, dtype=jnp.float32) * 2.0 / HD)
    angles = (places - leading_factor).astype(jnp.float32)[:, None] * rates[None, :]
    return (jnp.cos(angles), jnp.sin(angles))

def rotate(values, cosine, sine, sign):
    halfway = values.shape[-1] // 2
    front = values[..., :halfway]
    behind = values[..., halfway:]
    return jnp.concatenate([front * cosine - sign * behind * sine, behind * cosine + sign * front * sine], axis=-1)

def attention(queries, keys, values, segment_ids):
    blocks = SEQ_LEN // QBLK
    scale = HD ** (-0.5)
    columns = jnp.arange(SEQ_LEN, dtype=jnp.int32)

    def attend(inputs):
        query_block, segment_block, row_block = inputs
        logits = low_back(jnp.einsum('qkgd,tkd->kgqt', query_block, keys, precision=lax.Precision.HIGHEST) * scale)
        allowed = (segment_block[:, None] == segment_ids[None, :]) & (columns[None, :] <= row_block[:, None])
        logits = jnp.where(allowed, logits, -1e+30)
        peak = lax.optimization_barrier(jnp.max(logits, axis=-1, keepdims=True))
        weights = jnp.exp(logits - peak)
        probs = weights / lax.optimization_barrier(jnp.sum(weights, axis=-1, keepdims=True))
        return jnp.einsum('kgqt,tkd->qkgd', low(probs), values, precision=lax.Precision.HIGHEST)
    outputs = lax.map(jax.checkpoint(attend), (queries.reshape(blocks, QBLK, KV, GQ, HD), segment_ids.reshape(blocks, QBLK), columns.reshape(blocks, QBLK)))
    return outputs.reshape(SEQ_LEN, Q * HD)

def layer(tokens, gain1, w_query, w_keyval, w_out, gain2, w_gate, w_up, w_down, segment_ids):
    cosine, sine = rope_tables(segment_ids)
    normed = low(rms_norm(tokens, gain1))
    queries = low_back(highest(normed, w_query)).reshape(SEQ_LEN, KV, GQ, HD)
    keyval = low_back(highest(normed, w_keyval)).reshape(SEQ_LEN, KV, 2, HD)
    queries = low(rotate(queries, cosine[:, None, None], sine[:, None, None], 1.0))
    keys = low(rotate(keyval[:, :, 0], cosine[:, None], sine[:, None], 1.0))
    values = low(keyval[:, :, 1])
    heads = low_back(low(attention(queries, keys, values, segment_ids)))
    mixed = tokens + low_back(highest(heads, w_out))
    normed_two = low(rms_norm(mixed, gain2))
    gate = low_back(highest(normed_two, w_gate))
    upward = low_back(highest(normed_two, w_up))
    hidden = low(jax.nn.silu(gate) * upward)
    return mixed + low_back(highest(hidden, w_down))

def reference(tokens, gain1, w_query, w_keyval, w_out, gain2, w_gate, w_up, w_down, grad_out, segments):
    params = (gain1.astype(jnp.float32), w_query.astype(jnp.float32), w_keyval.astype(jnp.float32), w_out.astype(jnp.float32), gain2.astype(jnp.float32), w_gate.astype(jnp.float32), w_up.astype(jnp.float32), w_down.astype(jnp.float32))

    def one_sequence(totals, inputs):
        seq_tokens, seq_grad, seq_ids = inputs

        def forward(values, *weights):
            return layer(values, *weights, seq_ids)
        result, pull = jax.vjp(forward, seq_tokens.astype(jnp.float32), *params)
        grads = pull(seq_grad.astype(jnp.float32))
        totals = tuple((total + grad for total, grad in zip(totals, grads[1:])))
        return (totals, (result.astype(jnp.bfloat16), grads[0]))
    start = tuple((jnp.zeros(param.shape, jnp.float32) for param in params))
    totals, (output, grad_in) = lax.scan(one_sequence, start, (tokens, grad_out, segments))
    return (output, grad_in, totals[0], totals[1], totals[2], totals[3], totals[4], totals[5], totals[6], totals[7])
```

```python
import jax
import jax.numpy as jnp
from jax import lax
from jax.experimental import pallas as pl
from jax.experimental.pallas import tpu as pltpu
from jax.sharding import Mesh
from jax.sharding import PartitionSpec as P

D = 1536
HD = 96
HALF = HD // 2
EPS = 1e-05
THETA = 100000.0
NEGATIVE = -1e30
SCALE = HD**-0.5
LOG2E = 1.4426950408889634
F32 = jnp.float32
BF16 = jnp.bfloat16
QUARTER = 256
YS = ("yhi", "ylo")


def dot(a, b, dims):
    return lax.dot_general(a, b, (dims, ((), ())), preferred_element_type=F32)


NN = ((1,), (0,))
NT = ((1,), (1,))
TN = ((0,), (0,))


def swap(value, axis, step=1):
    count = lax.axis_size(axis)
    return lax.ppermute(value, axis, [(i, i ^ step) for i in range(count)])


def from_peers(value, axis):
    return [value] + [swap(value, axis, k) for k in range(1, lax.axis_size(axis))]


def placed(parts, axis):
    count = len(parts)
    if count == 1:
        return parts[0][None]
    me = lax.axis_index(axis)
    out = jnp.zeros((count, *parts[0].shape), parts[0].dtype)
    for k, part in enumerate(parts):
        out = lax.dynamic_update_index_in_dim(out, part, me ^ k, 0)
    return out


def sum_scatter(value, axis):
    count = lax.axis_size(axis)
    me = lax.axis_index(axis)

    def entry(k):
        return lax.dynamic_index_in_dim(value, me ^ k, 0, keepdims=False)

    total = entry(0).astype(F32)
    got = [swap(entry(k).astype(BF16), axis, k) for k in range(1, count)]
    for g in got:
        total = total + g.astype(F32)
    return total


def gather_dp(first, second):
    a = placed(from_peers(first, "x"), "x")
    b = placed(from_peers(second, "z"), "z")
    a = placed(from_peers(a, "z"), "z")
    b = placed(from_peers(b, "x"), "x")
    return jnp.swapaxes(a, 0, 1), b


def scatter_dp(first, second):
    a = sum_scatter(first, "x").astype(BF16)
    b = sum_scatter(jnp.swapaxes(second, 0, 1), "z").astype(BF16)
    a = sum_scatter(a, "z").astype(BF16)
    b = sum_scatter(b, "x").astype(BF16)
    return a, b


def over_y(value):
    return lax.all_to_all(value, YS, 0, 0, tiled=True)


def gather_y(value):
    return over_y(jnp.broadcast_to(value[None], (4, *value.shape)))


def small_sum(value):
    for axis in ("core", "ylo", "yhi", "x", "z"):
        parts = from_peers(value, axis)
        value = sum(parts[1:], parts[0])
    return value


def key_blocks(block):
    return (0, 2) if block == 0 else (0, 1, 2, 3)


def allowed_keys(offs_ref, key, place, low):
    at = offs_ref[key] + lax.broadcasted_iota(jnp.int32, (QUARTER, place.shape[1]), 0)
    return (at >= low) & (at <= place)


def two_heads(ref, group, block):
    lanes = pl.ds(block * QUARTER, QUARTER)
    return jnp.concatenate(
        [ref[pl.ds((2 * group + h) * HD, HD), lanes] for h in range(2)], axis=1
    )


def twice(ref, block):
    row = ref[:, pl.ds(block * QUARTER, QUARTER)]
    return jnp.concatenate([row, row], axis=1)


def forward_kernel(offs_ref, q_ref, own_ref, oth_ref, place_ref, low_ref, out_ref, lse_ref):
    factor = SCALE * LOG2E
    for group in range(2):
        keys = []
        vals = []
        for ref in (own_ref, oth_ref):
            for half in range(2):
                lanes = pl.ds(half * QUARTER, QUARTER)
                keys.append(ref[pl.ds(group * 2 * HD, HD), lanes].T)
                vals.append(ref[pl.ds(group * 2 * HD + HD, HD), lanes])
        for block in range(2):
            q = two_heads(q_ref, group, block)
            place, low = twice(place_ref, block), twice(low_ref, block)
            scores = []
            for key in key_blocks(block):
                s = dot(keys[key], q, NN)
                scores.append(jnp.where(allowed_keys(offs_ref, key, place, low), s, NEGATIVE))
            peak = scores[0].max(axis=0, keepdims=True)
            for s in scores[1:]:
                peak = jnp.maximum(peak, s.max(axis=0, keepdims=True))
            shift = peak * factor
            total = jnp.zeros_like(peak)
            acc = jnp.zeros((HD, 2 * QUARTER), F32)
            for key, s in zip(key_blocks(block), scores):
                p = jnp.exp2(s * factor - shift)
                total = total + p.sum(axis=0, keepdims=True)
                acc = acc + dot(vals[key], p.astype(BF16), NN)
            acc = (acc / total).astype(BF16)
            lse = shift + jnp.log2(total)
            for h in range(2):
                lanes = pl.ds(block * QUARTER, QUARTER)
                cut = slice(h * QUARTER, (h + 1) * QUARTER)
                out_ref[pl.ds((2 * group + h) * HD, HD), lanes] = acc[:, cut]
                lse_ref[pl.ds(2 * group + h, 1), lanes] = lse[:, cut]


def backward_kernel(
    offs_ref, q_ref, own_ref, oth_ref, do_ref, o_ref, lse_ref, place_ref, low_ref,
    dq_ref, down_ref, doth_ref,
):
    factor = SCALE * LOG2E
    for group in range(2):
        keys, vals, keyst = [], [], []
        for ref in (own_ref, oth_ref):
            for half in range(2):
                lanes = pl.ds(half * QUARTER, QUARTER)
                kt = ref[pl.ds(group * 2 * HD, HD), lanes]
                keyst.append(kt)
                keys.append(kt.T)
                vals.append(ref[pl.ds(group * 2 * HD + HD, HD), lanes].T)
        dks = [jnp.zeros((HD, QUARTER), F32) for _ in range(4)]
        dvs = [jnp.zeros((HD, QUARTER), F32) for _ in range(4)]
        for block in range(2):
            lanes = pl.ds(block * QUARTER, QUARTER)
            q = two_heads(q_ref, group, block)
            do = two_heads(do_ref, group, block)
            o = two_heads(o_ref, group, block)
            place, low = twice(place_ref, block), twice(low_ref, block)
            lse = jnp.concatenate(
                [lse_ref[pl.ds(2 * group + h, 1), lanes] for h in range(2)], axis=1
            )
            delta = (do.astype(F32) * o.astype(F32)).sum(axis=0, keepdims=True)
            dq = jnp.zeros((HD, 2 * QUARTER), F32)
            for key in key_blocks(block):
                s = dot(keys[key], q, NN)
                p = jnp.exp2(s * factor - lse)
                p = jnp.where(allowed_keys(offs_ref, key, place, low), p, 0.0)
                dp = dot(vals[key], do, NN)
                ds = (p * (dp - delta)).astype(BF16)
                dvs[key] = dvs[key] + dot(do, p.astype(BF16), NT)
                dks[key] = dks[key] + dot(q, ds, NT)
                dq = dq + dot(keyst[key], ds, NN)
            dq = dq * SCALE
            for h in range(2):
                cut = slice(h * QUARTER, (h + 1) * QUARTER)
                dq_ref[pl.ds((2 * group + h) * HD, HD), lanes] = dq[:, cut]
        for i, ref in enumerate((down_ref, doth_ref)):
            for half in range(2):
                lanes = pl.ds(half * QUARTER, QUARTER)
                rows = group * 2 * HD
                ref[pl.ds(rows, HD), lanes] = (dks[2 * i + half] * SCALE).astype(ref.dtype)
                ref[pl.ds(rows + HD, HD), lanes] = dvs[2 * i + half].astype(ref.dtype)


def vmem():
    return pl.BlockSpec(memory_space=pltpu.VMEM)


def attend(offs, queries, own, other, place, low):
    n, length = queries.shape
    return pl.pallas_call(
        forward_kernel,
        out_shape=(
            jax.ShapeDtypeStruct((n, length), BF16),
            jax.ShapeDtypeStruct((n // HD, length), F32),
        ),
        in_specs=[pl.BlockSpec(memory_space=pltpu.SMEM)] + [vmem()] * 5,
        out_specs=(vmem(), vmem()),
        compiler_params=pltpu.CompilerParams(vmem_limit_bytes=48 << 20),
        cost_estimate=pl.CostEstimate(
            flops=4 * 4 * HD * QUARTER * QUARTER * 6, bytes_accessed=4 << 20, transcendentals=1 << 20
        ),
        name="attend_forward",
    )(offs, queries, own, other, place, low)


def attend_back(offs, queries, own, other, grads, outs, lse, place, low):
    n, length = queries.shape
    return pl.pallas_call(
        backward_kernel,
        out_shape=(
            jax.ShapeDtypeStruct((n, length), F32),
            jax.ShapeDtypeStruct((n, length), F32),
            jax.ShapeDtypeStruct((n, length), BF16),
        ),
        in_specs=[pl.BlockSpec(memory_space=pltpu.SMEM)] + [vmem()] * 8,
        out_specs=(vmem(), vmem(), vmem()),
        compiler_params=pltpu.CompilerParams(vmem_limit_bytes=48 << 20),
        cost_estimate=pl.CostEstimate(
            flops=10 * 4 * HD * QUARTER * QUARTER * 6, bytes_accessed=6 << 20, transcendentals=1 << 20
        ),
        name="attend_backward",
    )(offs, queries, own, other, grads, outs, lse, place, low)


def rotate(values, cosine, sine, sign):
    front, behind = values[:, 0], values[:, 1]
    return jnp.stack(
        [front * cosine - sign * behind * sine, behind * cosine + sign * front * sine], axis=1
    )


def body(tokens, gain1, w_query, w_keyval, w_out, gain2, w_gate, w_up, w_down, grad_out, segments):
    core, yh, yl = lax.axis_index("core"), lax.axis_index("yhi"), lax.axis_index("ylo")
    nx, nz = lax.axis_size("x"), lax.axis_size("z")
    ndp = nx * nz
    dp = lax.axis_index("x") * nz + lax.axis_index("z")
    y = 2 * yh + yl
    mine = core ^ yh
    shard = D // 4

    def pick(first_is_mine, own, other):
        return jnp.where(first_is_mine, own, other), jnp.where(first_is_mine, other, own)

    def whole_rows(value):
        own = lax.dynamic_slice_in_dim(value, mine * QUARTER, QUARTER, 0)
        other = lax.dynamic_slice_in_dim(value, (1 - mine) * QUARTER, QUARTER, 0)
        pair = jnp.stack(pick(core == 0, own, swap(other, "core")))
        got = gather_y(pair).reshape(2, 2, 2, QUARTER, shard)
        return got.transpose(0, 3, 1, 2, 4).reshape(2 * QUARTER, D)

    def exchanged(slab):
        send = lax.dynamic_index_in_dim(slab, 1 - yl, 0, keepdims=False)
        keep = lax.dynamic_index_in_dim(slab, yl, 0, keepdims=False)
        return pick(yl == 0, keep, swap(send, "ylo"))

    def both_cores(left, right):
        pair = jnp.stack([left, right])
        first, second = pick(core == 0, pair, swap(pair, "core"))
        return jnp.concatenate([first[0], second[0], first[1], second[1]], axis=1)

    def part_of(value, dim):
        size = value.shape[dim] // ndp
        return lax.dynamic_slice_in_dim(value, dp * size, size, dim)

    def rows_first(weight):
        return weight.reshape(shard, 2, -1).transpose(1, 2, 0)

    x_rows = whole_rows(tokens[0])

    wide = jnp.concatenate([rows_first(w_query), rows_first(w_keyval)], axis=1)
    left, right = gather_dp(*exchanged(part_of(wide, 1)))
    w_qkv = both_cores(left.reshape(-1, shard), right.reshape(-1, shard))

    piece = gather_y(part_of(w_out, 0))
    piece = piece.reshape(2, 2, *piece.shape[1:])
    left, right = gather_dp(piece[:, 0], piece[:, 1])

    def head_rows(v):
        return v.transpose(2, 0, 1, 3, 4).reshape(-1, shard)

    w_o = both_cores(head_rows(left), head_rows(right))
    w_o_mine = lax.dynamic_slice_in_dim(w_o, y * shard, shard, 0)

    def hidden_slab(weight):
        units = weight.shape[0] // (2 * ndp)
        return part_of(weight, 0).reshape(2, units, shard)

    slabs = [hidden_slab(w_gate.T), hidden_slab(w_up.T), hidden_slab(w_down)]
    units = slabs[0].shape[1]
    left, right = gather_dp(*exchanged(jnp.concatenate(slabs, axis=1)))

    def hidden_rows(v, k):
        return v.reshape(ndp, 3, units, shard)[:, k].reshape(-1, shard)

    w_g, w_u, w_d = [both_cores(hidden_rows(left, k), hidden_rows(right, k)) for k in range(3)]

    gains = gather_small(gain1, gain2)
    gain1, gain2 = gains[0][None, :], gains[1][None, :]

    ids = segments[0]
    low_all = jnp.sum((ids[None, :] < ids[:, None]).astype(jnp.int32), axis=1)
    low = jnp.concatenate(
        [
            lax.dynamic_slice_in_dim(low_all, core * QUARTER, QUARTER),
            lax.dynamic_slice_in_dim(low_all, (3 - core) * QUARTER, QUARTER),
        ]
    )
    step = jnp.arange(QUARTER, dtype=jnp.int32)
    place = jnp.concatenate([core * QUARTER + step, (3 - core) * QUARTER + step])
    rates = THETA ** (-jnp.arange(HALF, dtype=F32) * 2.0 / HD)
    angles = rates[:, None] * (place - low).astype(F32)[None, :]
    cosine, sine = jnp.cos(angles), jnp.sin(angles)
    place, low = place[None, :], low[None, :]
    offs = (jnp.stack([core, 3 - core, 1 - core, 2 + core]) * QUARTER).astype(jnp.int32)

    inputs = x_rows.astype(F32)
    inverse_one = lax.rsqrt(jnp.mean(inputs * inputs, axis=-1, keepdims=True) + EPS)
    normed_one = inputs * inverse_one
    h_one = (normed_one * gain1).astype(BF16)
    raw = dot(w_qkv, h_one, NT)
    queries = rotate(raw[:shard].reshape(4, 2, HALF, -1), cosine, sine, 1.0)
    queries = queries.astype(BF16).reshape(shard, -1)
    keyval = raw[shard:].reshape(2, 2, 2, HALF, -1)
    keys = rotate(keyval[:, 0], cosine, sine, 1.0)
    keyval = jnp.stack([keys, keyval[:, 1]], axis=1).astype(BF16).reshape(shard, -1)
    keyval_other = swap(keyval, "core")
    heads, lse = attend(offs, queries, keyval, keyval_other, place, low)
    heads_all = gather_y(heads).reshape(-1, heads.shape[1])
    mixed = inputs + dot(heads_all, w_o, TN)

    inverse_two = lax.rsqrt(jnp.mean(mixed * mixed, axis=-1, keepdims=True) + EPS)
    h_two = (mixed * inverse_two * gain2).astype(BF16)
    gate = dot(h_two, w_g, NT)
    upward = dot(h_two, w_u, NT)
    sigma = jax.nn.sigmoid(gate)
    hidden = (gate * sigma * upward).astype(BF16)
    top = whole_rows(grad_out[0])
    grad_hidden = dot(top, w_d, NT)
    grad_gate = (grad_hidden * upward * sigma * (1.0 + gate * (1.0 - sigma))).astype(BF16)
    grad_up = (grad_hidden * gate * sigma).astype(BF16)
    part = dot(grad_gate, w_g, NN) + dot(grad_up, w_u, NN)
    got = over_y(part.astype(BF16).reshape(4, 128, D))
    grad_two = got.astype(F32).sum(axis=0)

    def my_rows(value):
        return lax.dynamic_slice_in_dim(value, y * 128, 128, 0)

    inv_two = my_rows(inverse_two)
    normed_two = my_rows(mixed) * inv_two
    gain2_part = (grad_two * normed_two).sum(axis=0)
    scaled = grad_two * gain2
    inner = jnp.mean(scaled * normed_two, axis=-1, keepdims=True)
    grad_mixed = my_rows(top).astype(F32) + inv_two * (scaled - normed_two * inner)
    residual = gather_y(grad_mixed.astype(BF16)).reshape(-1, D)

    grad_heads = dot(w_o_mine, residual, NT).astype(BF16)
    dq, dkv, dkv_other = attend_back(
        offs, queries, keyval, keyval_other, grad_heads, heads, lse, place, low
    )
    dkv = dkv + swap(dkv_other, "core").astype(F32)
    dq = rotate(dq.reshape(4, 2, HALF, -1), cosine, sine, -1.0).reshape(shard, -1)
    dkv = dkv.reshape(2, 2, 2, HALF, -1)
    dk = rotate(dkv[:, 0], cosine, sine, -1.0)
    dkv = jnp.stack([dk, dkv[:, 1]], axis=1).reshape(shard, -1)
    grad_raw = jnp.concatenate([dq, dkv]).astype(BF16)
    part = dot(grad_raw, w_qkv, TN)
    gain1_part = (part * normed_one).sum(axis=0)
    inner = (part * normed_one * gain1).sum(axis=-1)
    got = over_y(blocks(part.astype(BF16)))
    inner = over_y(jnp.broadcast_to(inner.reshape(2, 1, QUARTER), (2, 2, QUARTER)).reshape(4, -1))
    inner = inner.sum(axis=0)[:, None] / D

    def my_block(value):
        return lax.dynamic_slice(value, (yh * QUARTER, yl * D // 2), (QUARTER, D // 2))

    gain1_mine = lax.dynamic_slice(gain1, (0, yl * D // 2), (1, D // 2))
    inv_one = lax.dynamic_slice_in_dim(inverse_one, yh * QUARTER, QUARTER, 0)
    normed_block = my_block(x_rows).astype(F32) * inv_one
    scaled = got.astype(F32).sum(axis=0) * gain1_mine
    grad_in = my_block(residual).astype(F32) + inv_one * (scaled - normed_block * inner)

    def to_home(block):
        own = lax.dynamic_slice_in_dim(block, core * shard, shard, 1)
        other = lax.dynamic_slice_in_dim(block, (1 - core) * shard, shard, 1)
        return jnp.concatenate(pick(mine == 0, own, swap(other, "core")))

    grad_in = to_home(grad_in)
    mlp = over_y(blocks(dot(hidden, w_d, NN).astype(BF16)))
    output = to_home((my_block(mixed) + mlp.astype(F32).sum(axis=0)).astype(BF16))

    def for_core(value, who):
        cut = value.reshape(-1, 2, 2, shard)
        return lax.dynamic_index_in_dim(cut, who, 2, keepdims=False).reshape(-1, 2 * shard)

    def weight_grad(left_dims, rows, columns):
        send = dot(rows, for_core(columns, 1 - core), left_dims).astype(BF16)
        return dot(rows, for_core(columns, core), left_dims) + swap(send, "core").astype(F32)

    def reduced(total):
        total = total.astype(BF16)
        cut = total.reshape(nx, nz, -1, 2 * shard)
        left, right = scatter_dp(cut[..., :shard], cut[..., shard:])
        send = jnp.where(yl == 0, right, left)
        keep = jnp.where(yl == 0, left, right)
        first, second = gather_dp(*pick(yl == 0, keep, swap(send, "ylo")))
        return first.reshape(ndp, -1, shard), second.reshape(ndp, -1, shard)

    grad_d = weight_grad(TN, hidden, top)
    grad_g = weight_grad(TN, grad_gate, h_two)
    grad_u = weight_grad(TN, grad_up, h_two)
    total = jnp.stack([v.reshape(ndp, units, -1) for v in (grad_g, grad_u, grad_d)], axis=1)
    first, second = reduced(total.reshape(-1, 2 * shard))

    def hidden_grad(k):
        cut = [v.reshape(ndp, 3, units, shard)[:, k] for v in (first, second)]
        return jnp.stack(cut, axis=1).reshape(-1, shard).astype(F32)

    grad_w_gate, grad_w_up, grad_w_down = hidden_grad(0).T, hidden_grad(1).T, hidden_grad(2)

    grad_o = weight_grad(NN, heads, residual)
    grad_qkv = weight_grad(NN, grad_raw, h_one)
    total = jnp.concatenate([grad_qkv, grad_o])
    first, second = reduced(total)
    both = jnp.stack([v.reshape(-1, shard) for v in (first, second)]).astype(F32)
    grad_w_query = both[:, :shard].reshape(-1, shard).T
    grad_w_keyval = both[:, shard : 2 * shard].reshape(-1, shard).T
    grad_w_out = both[:, 2 * shard :].reshape(-1, shard)

    gains = small_sum(jnp.stack([gain1_part, gain2_part]))
    home = (yl * 2 + core) * shard
    gains = lax.dynamic_slice(gains, (0, home), (2, shard))
    return (
        output[None],
        grad_in[None],
        gains[0],
        grad_w_query,
        grad_w_keyval,
        grad_w_out,
        gains[1],
        grad_w_gate,
        grad_w_up,
        grad_w_down,
    )


def blocks(value):
    return value.reshape(2, QUARTER, 2, D // 2).transpose(0, 2, 1, 3).reshape(4, QUARTER, D // 2)


def gather_small(gain1, gain2):
    pair = jnp.stack([gain1, gain2])
    first = placed(from_peers(pair, "core"), "core")
    both = placed(from_peers(first, "ylo"), "ylo")
    return both.transpose(2, 0, 1, 3).reshape(2, D)


def solution(mesh):
    dp = mesh.shape["dp"]
    side = int(round(dp**0.5))
    fine = Mesh(
        mesh.devices.reshape(side, dp // side, 2, 2, 2), ("x", "z", "ylo", "core", "yhi")
    )
    seq, row, col = ("x", "z"), ("ylo", "core"), "yhi"
    return jax.shard_map(
        body,
        mesh=fine,
        in_specs=(
            P(seq, col, row),
            P(row),
            P(row, col),
            P(row, col),
            P(col, row),
            P(row),
            P(row, col),
            P(row, col),
            P(col, row),
            P(seq, col, row),
            P(seq, None),
        ),
        out_specs=(
            P(seq, col, row),
            P(seq, col, row),
            P(row),
            P(row, col),
            P(row, col),
            P(col, row),
            P(row),
            P(row, col),
            P(row, col),
            P(col, row),
        ),
        check_vma=False,
    )
```

```python
import jax
import jax.numpy as jnp
from jax import lax
from jax.experimental import pallas as pl
from jax.experimental.pallas import tpu as pltpu
from jax.sharding import Mesh
from jax.sharding import PartitionSpec as P

D = 1536
HD = 96
HALF = HD // 2
EPS = 1e-05
THETA = 100000.0
NEGATIVE = -1e30
SCALE = HD**-0.5
LOG2E = 1.4426950408889634
F32 = jnp.float32
BF16 = jnp.bfloat16
QUARTER = 256
TOKENS = 2 * QUARTER
CHUNK = 128
WIDE = D // 2
SHARD = D // 4
YS = ("yhi", "ylo")
DP = ("x", "z")

NN = ((1,), (0,))
NT = ((1,), (1,))
TN = ((0,), (0,))


def dot(a, b, dims):
    return lax.dot_general(a, b, (dims, ((), ())), preferred_element_type=F32)


def swap(value, axis, step=1):
    count = lax.axis_size(axis)
    return lax.ppermute(value, axis, [(i, i ^ step) for i in range(count)])


def swap_y(value, k):
    return swap(value, ("ylo", "yhi"), 2 * (k & 1) + (k >> 1))


def peers_y(value):
    return [value] + [swap_y(value, k) for k in (1, 2, 3)]


def to_peers_y(values):
    return [values[0]] + [swap_y(values[k], k) for k in (1, 2, 3)]


def gather_dp(value):
    return lax.all_gather(value, DP, axis=0)


def scatter_dp(value):
    got = lax.all_to_all(value, DP, 0, 0, tiled=True)
    return got.astype(F32).sum(axis=0).astype(BF16)


def gather_dp_now(value):
    count = lax.axis_size(DP)
    return lax.all_to_all(jnp.broadcast_to(value[None], (count, *value.shape)), DP, 0, 0, tiled=True)


def gather_y_now(value):
    return lax.all_to_all(jnp.broadcast_to(value[None], (4, *value.shape)), YS, 0, 0, tiled=True)


def small_sum(value):
    for axis in ("core", "ylo", "yhi", "x", "z"):
        parts = [value] + [swap(value, axis, k) for k in range(1, lax.axis_size(axis))]
        value = sum(parts[1:], parts[0])
    return value


def vmem():
    return pl.BlockSpec(memory_space=pltpu.VMEM)


def smem():
    return pl.BlockSpec(memory_space=pltpu.SMEM)


def shape(dims, dtype):
    return jax.ShapeDtypeStruct(dims, dtype)


def cost(flops, nbytes):
    return pl.CostEstimate(flops=int(flops), bytes_accessed=int(nbytes), transcendentals=0)


def params(mib):
    return pltpu.CompilerParams(vmem_limit_bytes=mib << 20)


def peer(spot, k):
    high = jnp.bitwise_xor(spot[0], k >> 1)
    low = jnp.bitwise_xor(spot[1], k & 1)
    return high, low, 2 * high + low


def place_pieces(spot, pieces, out):
    for k, piece in enumerate(pieces):
        high, low, _ = peer(spot, k)
        rows = pl.ds(pl.multiple_of(high * QUARTER, QUARTER), QUARTER)
        for j in range(2):
            lanes = pl.ds(pl.multiple_of(low * SHARD + j * WIDE, 128), SHARD)
            out[rows, lanes] = piece[j]


def cut_pieces(spot, value, outs):
    for k, out in enumerate(outs):
        high, low, _ = peer(spot, k)
        rows = pl.ds(pl.multiple_of(high * QUARTER, QUARTER), QUARTER)
        for j in range(2):
            lanes = pl.ds(pl.multiple_of(low * SHARD + j * WIDE, 128), SHARD)
            out[j] = value[rows, lanes].astype(out.dtype)


def turn(front, behind, cosine, sine):
    return front * cosine - behind * sine, behind * cosine + front * sine


def qkv_kernel(spot, p0, p1, p2, p3, gain, own, oth, cosine, sine, x, h, inv, q, kv):
    place_pieces(spot, (p0, p1, p2, p3), x)
    for i in range(4):
        rows = pl.ds(i * CHUNK, CHUNK)
        value = x[rows].astype(F32)
        inverse = lax.rsqrt((value * value).sum(axis=-1, keepdims=True) / D + EPS)
        inv[rows] = inverse
        h[rows] = (value * inverse * gain[...]).astype(BF16)
    cos, sin = cosine[...], sine[...]
    for i in range(4):
        rows = pl.ds(i * 2 * HD, 2 * HD)
        raw = dot(own[rows], h[:, :WIDE], NT) + dot(oth[rows], h[:, WIDE:], NT)
        out, base = (q, i * 2 * HD) if i < 2 else (kv, (i - 2) * 2 * HD)
        for head in range(2):
            front, behind = raw[head * HD : head * HD + HALF], raw[head * HD + HALF : (head + 1) * HD]
            if i < 2 or head == 0:
                front, behind = turn(front, behind, cos, sin)
            out[pl.ds(base + head * HD, HALF)] = front.astype(BF16)
            out[pl.ds(base + head * HD + HALF, HALF)] = behind.astype(BF16)


def project(spot, pieces, gain, own, oth, cosine, sine):
    return pl.pallas_call(
        qkv_kernel,
        out_shape=(
            shape((TOKENS, D), BF16),
            shape((TOKENS, D), BF16),
            shape((TOKENS, 1), F32),
            shape((SHARD, TOKENS), BF16),
            shape((SHARD, TOKENS), BF16),
        ),
        in_specs=[smem()] + [vmem()] * 9,
        out_specs=(vmem(),) * 5,
        compiler_params=params(32),
        cost_estimate=cost(2 * TOKENS * D * WIDE, 8 << 20),
        name="project",
    )(spot, *pieces, gain, own, oth, cosine, sine)


def key_blocks(block):
    return (0, 2) if block == 0 else (0, 1, 2, 3)


def allowed_keys(spot, key, place, low):
    at = spot[4 + key] + lax.broadcasted_iota(jnp.int32, (QUARTER, place.shape[1]), 0)
    return (at >= low) & (at <= place)


def two_heads(ref, group, block):
    lanes = pl.ds(block * QUARTER, QUARTER)
    return jnp.concatenate(
        [ref[pl.ds((2 * group + h) * HD, HD), lanes] for h in range(2)], axis=1
    )


def twice(ref, block):
    row = ref[:, pl.ds(block * QUARTER, QUARTER)]
    return jnp.concatenate([row, row], axis=1)


def forward_kernel(spot, q_ref, own_ref, oth_ref, place_ref, low_ref, outt_ref, out_ref, lse_ref):
    factor = SCALE * LOG2E
    for group in range(2):
        keys = []
        vals = []
        for ref in (own_ref, oth_ref):
            for half in range(2):
                lanes = pl.ds(half * QUARTER, QUARTER)
                keys.append(ref[pl.ds(group * 2 * HD, HD), lanes].T)
                vals.append(ref[pl.ds(group * 2 * HD + HD, HD), lanes])
        for block in range(2):
            q = two_heads(q_ref, group, block)
            place, low = twice(place_ref, block), twice(low_ref, block)
            scores = []
            for key in key_blocks(block):
                s = dot(keys[key], q, NN)
                scores.append(jnp.where(allowed_keys(spot, key, place, low), s, NEGATIVE))
            peak = scores[0].max(axis=0, keepdims=True)
            for s in scores[1:]:
                peak = jnp.maximum(peak, s.max(axis=0, keepdims=True))
            shift = peak * factor
            total = jnp.zeros_like(peak)
            acc = jnp.zeros((HD, 2 * QUARTER), F32)
            for key, s in zip(key_blocks(block), scores):
                p = jnp.exp2(s * factor - shift)
                total = total + p.sum(axis=0, keepdims=True)
                acc = acc + dot(vals[key], p.astype(BF16), NN)
            acc = (acc / total).astype(BF16)
            lse = shift + jnp.log2(total)
            for h in range(2):
                lanes = pl.ds(block * QUARTER, QUARTER)
                cut = slice(h * QUARTER, (h + 1) * QUARTER)
                outt_ref[pl.ds((2 * group + h) * HD, HD), lanes] = acc[:, cut]
                lse_ref[pl.ds(2 * group + h, 1), lanes] = lse[:, cut]
    out_ref[...] = outt_ref[...].T


def attend(spot, queries, own, other, place, low):
    return pl.pallas_call(
        forward_kernel,
        out_shape=(
            shape((SHARD, TOKENS), BF16),
            shape((TOKENS, SHARD), BF16),
            shape((4, TOKENS), F32),
        ),
        in_specs=[smem()] + [vmem()] * 5,
        out_specs=(vmem(),) * 3,
        compiler_params=params(40),
        cost_estimate=cost(4 * 4 * HD * QUARTER * QUARTER * 6, 4 << 20),
        name="attend_forward",
    )(spot, queries, own, other, place, low)


def mix_kernel(spot, x, h0, h1, h2, h3, own, oth, gain, mixed, h, inv, heads):
    for k, piece in enumerate((h0, h1, h2, h3)):
        _, _, y = peer(spot, k)
        heads[:, pl.ds(pl.multiple_of(y * SHARD, 128), SHARD)] = piece[...]
    for i in range(2):
        rows = pl.ds(i * QUARTER, QUARTER)
        square = jnp.zeros((QUARTER, 1), F32)
        for j, w in enumerate((own, oth)):
            lanes = pl.ds(j * WIDE, WIDE)
            value = x[rows, lanes].astype(F32)
            for half in range(2):
                block = w[:, half].reshape(WIDE, WIDE)
                value = value + dot(heads[rows, pl.ds(half * WIDE, WIDE)], block, NN)
            mixed[rows, lanes] = value
            square = square + (value * value).sum(axis=-1, keepdims=True)
        inverse = lax.rsqrt(square / D + EPS)
        inv[rows] = inverse
        h[rows] = (mixed[rows] * inverse * gain[...]).astype(BF16)


def mix(spot, x, pieces, own, oth, gain):
    return pl.pallas_call(
        mix_kernel,
        out_shape=(
            shape((TOKENS, D), F32),
            shape((TOKENS, D), BF16),
            shape((TOKENS, 1), F32),
        ),
        in_specs=[smem()] + [vmem()] * 8,
        out_specs=(vmem(),) * 3,
        scratch_shapes=[pltpu.VMEM((TOKENS, D), BF16)],
        compiler_params=params(40),
        cost_estimate=cost(2 * TOKENS * D * D, 12 << 20),
        name="mix",
    )(spot, x, *pieces, own, oth, gain)


def units_of(ref, k):
    return ref[:, k].reshape(-1, WIDE)


def feed_kernel(spot, h, g0, g1, g2, g3, own, oth, top, act, dgate, dup, o0, o1, o2, o3, acc):
    step = pl.program_id(0)

    @pl.when(step == 0)
    def _():
        place_pieces(spot, (g0, g1, g2, g3), top)
        acc[...] = jnp.zeros_like(acc)

    def hidden(k, columns):
        return dot(units_of(own, k), columns[:, :WIDE], NT) + dot(
            units_of(oth, k), columns[:, WIDE:], NT
        )

    gate, up, grad = hidden(0, h), hidden(1, h), hidden(2, top)
    sigma = jax.nn.sigmoid(gate)
    silu = gate * sigma
    act[...] = (silu * up).astype(BF16)
    grad_gate = (grad * up * sigma * (1.0 + gate * (1.0 - sigma))).astype(BF16)
    grad_up = (grad * silu).astype(BF16)
    dgate[...] = grad_gate
    dup[...] = grad_up
    grad_gate, grad_up = grad_gate.T, grad_up.T
    for j, w in enumerate((own, oth)):
        lanes = pl.ds(j * WIDE, WIDE)
        acc[:, lanes] += dot(grad_gate, units_of(w, 0), NN) + dot(grad_up, units_of(w, 1), NN)

    @pl.when(step == pl.num_programs(0) - 1)
    def _():
        for k, out in enumerate((o0, o1, o2, o3)):
            _, _, y = peer(spot, k)
            out[...] = acc[pl.ds(pl.multiple_of(y * CHUNK, CHUNK), CHUNK)].astype(BF16)


def whole(dims):
    return pl.BlockSpec(dims, lambda *_: (0,) * len(dims))


def feed(spot, h, pieces, own, oth):
    steps = 4
    units = own.shape[0] * own.shape[2]
    group = own.shape[0] // steps
    rows = units // steps
    weights = pl.BlockSpec((group, *own.shape[1:]), lambda i, _: (i, 0, 0, 0))
    block = pl.BlockSpec((rows, TOKENS), lambda i, _: (i, 0))
    return pl.pallas_call(
        feed_kernel,
        out_shape=(
            shape((TOKENS, D), BF16),
            *(shape((units, TOKENS), BF16),) * 3,
            *(shape((CHUNK, D), BF16),) * 4,
        ),
        grid_spec=pltpu.PrefetchScalarGridSpec(
            num_scalar_prefetch=1,
            grid=(steps,),
            in_specs=[whole((TOKENS, D))]
            + [whole((2, QUARTER, SHARD))] * 4
            + [weights, weights],
            out_specs=(whole((TOKENS, D)), block, block, block, *(whole((CHUNK, D)),) * 4),
            scratch_shapes=[pltpu.VMEM((TOKENS, D), F32)],
        ),
        compiler_params=params(48),
        cost_estimate=cost(10 * TOKENS * D * units, 20 << 20),
        name="feed",
    )(spot, h, *pieces, own, oth)


def down_kernel(spot, act, own, oth, o0, o1, o2, o3, acc):
    step = pl.program_id(0)

    @pl.when(step == 0)
    def _():
        acc[...] = jnp.zeros_like(acc)

    hidden = act[...].T
    for j, w in enumerate((own, oth)):
        acc[:, pl.ds(j * WIDE, WIDE)] += dot(hidden, w[...].reshape(-1, WIDE), NN)

    @pl.when(step == pl.num_programs(0) - 1)
    def _():
        cut_pieces(spot, acc, (o0, o1, o2, o3))


def down(spot, act, own, oth):
    steps = 4
    group = own.shape[0] // steps
    rows = act.shape[0] // steps
    weights = pl.BlockSpec((group, 1, *own.shape[2:]), lambda i, _: (i, 2, 0, 0))
    return pl.pallas_call(
        down_kernel,
        out_shape=(shape((2, QUARTER, SHARD), BF16),) * 4,
        grid_spec=pltpu.PrefetchScalarGridSpec(
            num_scalar_prefetch=1,
            grid=(steps,),
            in_specs=[pl.BlockSpec((rows, TOKENS), lambda i, _: (i, 0)), weights, weights],
            out_specs=(whole((2, QUARTER, SHARD)),) * 4,
            scratch_shapes=[pltpu.VMEM((TOKENS, D), F32)],
        ),
        compiler_params=params(24),
        cost_estimate=cost(2 * TOKENS * D * act.shape[0], 8 << 20),
        name="down",
    )(spot, act, own, oth)


def residual_kernel(spot, r0, r1, r2, r3, mixed, inv, top, gain, out, part):
    grad = r0[...].astype(F32) + r1[...].astype(F32) + r2[...].astype(F32) + r3[...].astype(F32)
    inverse = inv[...]
    normed = mixed[...] * inverse
    part[...] = (grad * normed).sum(axis=0, keepdims=True)
    scaled = grad * gain[...]
    inner = (scaled * normed).sum(axis=-1, keepdims=True) / D
    out[...] = (top[...].astype(F32) + inverse * (scaled - normed * inner)).astype(BF16)


def residual(spot, pieces, mixed, inv, top, gain):
    mine = lambda width: pl.BlockSpec((CHUNK, width), lambda i, s: (2 * s[0] + s[1], 0))
    return pl.pallas_call(
        residual_kernel,
        out_shape=(shape((CHUNK, D), BF16), shape((1, D), F32)),
        grid_spec=pltpu.PrefetchScalarGridSpec(
            num_scalar_prefetch=1,
            grid=(1,),
            in_specs=[whole((CHUNK, D))] * 4 + [mine(D), mine(1), mine(D), whole((1, D))],
            out_specs=(whole((CHUNK, D)), whole((1, D))),
        ),
        compiler_params=params(16),
        cost_estimate=cost(CHUNK * D * 20, 4 << 20),
        name="residual",
    )(spot, *pieces, mixed, inv, top, gain)


def backward_kernel(
    spot, r0, r1, r2, r3, wown, woth, q_ref, own_ref, oth_ref, o_ref, lse_ref, place_ref, low_ref,
    cosine, sine, rows_ref, dq_ref, down_ref, doth_ref, do_ref,
):
    for k, piece in enumerate((r0, r1, r2, r3)):
        _, _, y = peer(spot, k)
        rows_ref[pl.ds(pl.multiple_of(y * CHUNK, CHUNK), CHUNK)] = piece[...]
    do_ref[...] = (
        dot(wown[...].reshape(SHARD, WIDE), rows_ref[:, :WIDE], NT)
        + dot(woth[...].reshape(SHARD, WIDE), rows_ref[:, WIDE:], NT)
    ).astype(BF16)
    factor = SCALE * LOG2E
    for group in range(2):
        keys, vals, keyst = [], [], []
        for ref in (own_ref, oth_ref):
            for half in range(2):
                lanes = pl.ds(half * QUARTER, QUARTER)
                kt = ref[pl.ds(group * 2 * HD, HD), lanes]
                keyst.append(kt)
                keys.append(kt.T)
                vals.append(ref[pl.ds(group * 2 * HD + HD, HD), lanes].T)
        dks = [jnp.zeros((HD, QUARTER), F32) for _ in range(4)]
        dvs = [jnp.zeros((HD, QUARTER), F32) for _ in range(4)]
        for block in range(2):
            lanes = pl.ds(block * QUARTER, QUARTER)
            q = two_heads(q_ref, group, block)
            do = two_heads(do_ref, group, block)
            o = two_heads(o_ref, group, block)
            place, low = twice(place_ref, block), twice(low_ref, block)
            lse = jnp.concatenate(
                [lse_ref[pl.ds(2 * group + h, 1), lanes] for h in range(2)], axis=1
            )
            delta = (do.astype(F32) * o.astype(F32)).sum(axis=0, keepdims=True)
            dq = jnp.zeros((HD, 2 * QUARTER), F32)
            for key in key_blocks(block):
                s = dot(keys[key], q, NN)
                p = jnp.exp2(s * factor - lse)
                p = jnp.where(allowed_keys(spot, key, place, low), p, 0.0)
                dp = dot(vals[key], do, NN)
                ds = (p * (dp - delta)).astype(BF16)
                dvs[key] = dvs[key] + dot(do, p.astype(BF16), NT)
                dks[key] = dks[key] + dot(q, ds, NT)
                dq = dq + dot(keyst[key], ds, NN)
            dq = dq * SCALE
            cos, sin = twice(cosine, block), twice(sine, block)
            front, behind = turn(dq[:HALF], dq[HALF:], cos, -sin)
            for h in range(2):
                cut = slice(h * QUARTER, (h + 1) * QUARTER)
                base = (2 * group + h) * HD
                dq_ref[pl.ds(base, HALF), lanes] = front[:, cut].astype(BF16)
                dq_ref[pl.ds(base + HALF, HALF), lanes] = behind[:, cut].astype(BF16)
        for i, ref in enumerate((down_ref, doth_ref)):
            for half in range(2):
                lanes = pl.ds(half * QUARTER, QUARTER)
                rows = group * 2 * HD
                ref[pl.ds(rows, HD), lanes] = (dks[2 * i + half] * SCALE).astype(ref.dtype)
                ref[pl.ds(rows + HD, HD), lanes] = dvs[2 * i + half].astype(ref.dtype)


def attend_back(spot, pieces, wown, woth, queries, own, other, outs, lse, place, low, cosine, sine):
    half = wown.shape[0] // 2
    weights = pl.BlockSpec((half, 1, *wown.shape[2:]), lambda i, s: (s[1], s[0], 0, 0))
    flat = whole((SHARD, TOKENS))
    row = whole((1, TOKENS))
    return pl.pallas_call(
        backward_kernel,
        out_shape=(
            shape((TOKENS, D), BF16),
            shape((SHARD, TOKENS), BF16),
            shape((SHARD, TOKENS), F32),
            shape((SHARD, TOKENS), BF16),
        ),
        grid_spec=pltpu.PrefetchScalarGridSpec(
            num_scalar_prefetch=1,
            grid=(1,),
            in_specs=[whole((CHUNK, D))] * 4
            + [weights, weights, flat, flat, flat, flat, whole((4, TOKENS)), row, row]
            + [whole((HALF, TOKENS))] * 2,
            out_specs=(whole((TOKENS, D)), flat, flat, flat),
            scratch_shapes=[pltpu.VMEM((SHARD, TOKENS), BF16)],
        ),
        compiler_params=params(48),
        cost_estimate=cost(10 * 4 * HD * QUARTER * QUARTER * 6 + 2 * TOKENS * D * SHARD, 8 << 20),
        name="attend_backward",
    )(spot, *pieces, wown, woth, queries, own, other, outs, lse, place, low, cosine, sine)


def input_kernel(
    spot, dq, mine, got, cosine, sine, own, oth, x, inv, raw, o0, o1, o2, o3, part, acc
):
    raw[:SHARD] = dq[...]
    total = mine[...] + got[...].astype(F32)
    cos, sin = cosine[...], -sine[...]
    for group in range(2):
        base = group * 2 * HD
        front, behind = turn(total[base : base + HALF], total[base + HALF : base + HD], cos, sin)
        raw[pl.ds(SHARD + base, HALF)] = front.astype(BF16)
        raw[pl.ds(SHARD + base + HALF, HALF)] = behind.astype(BF16)
        raw[pl.ds(SHARD + base + HD, HD)] = total[base + HD : base + 2 * HD].astype(BF16)
    grads = raw[...].T
    for j, w in enumerate((own, oth)):
        lanes = pl.ds(j * WIDE, WIDE)
        value = dot(grads, w[...], NN)
        acc[:, lanes] = value.astype(BF16)
        part[:, lanes] = (value * (x[:, lanes].astype(F32) * inv[...])).sum(axis=0, keepdims=True)
    cut_pieces(spot, acc, (o0, o1, o2, o3))


def input_grad(spot, dq, mine, got, cosine, sine, own, oth, x, inv):
    return pl.pallas_call(
        input_kernel,
        out_shape=(
            shape((WIDE, TOKENS), BF16),
            *(shape((2, QUARTER, SHARD), BF16),) * 4,
            shape((1, D), F32),
        ),
        in_specs=[smem()] + [vmem()] * 9,
        out_specs=(vmem(),) * 6,
        scratch_shapes=[pltpu.VMEM((TOKENS, D), BF16)],
        compiler_params=params(32),
        cost_estimate=cost(2 * TOKENS * D * WIDE, 8 << 20),
        name="input_grad",
    )(spot, dq, mine, got, cosine, sine, own, oth, x, inv)


def units_grad_kernel(dgate, dup, act, h, top, *rest):
    out = rest[-1]
    for k, (rows, columns) in enumerate(((dgate, h), (dup, h), (act, top))):
        value = dot(rows[...], columns[...], NN).reshape(out.shape[0], -1, WIDE)
        if len(rest) == 2:
            value = value + rest[0][:, k].astype(F32)
        out[:, k] = value.astype(BF16)


def units_grad(dgate, dup, act, h, top, half, got, ndp):
    steps = 4
    units = dgate.shape[0]
    block = pl.BlockSpec((units // steps, TOKENS), lambda i: (i, 0))
    columns = pl.BlockSpec((TOKENS, WIDE), lambda i: (0, half))
    dims = (ndp, 3, units // ndp, WIDE)
    result = pl.BlockSpec((ndp // steps, *dims[1:]), lambda i: (i, 0, 0, 0))
    extra = [] if got is None else [got]
    return pl.pallas_call(
        units_grad_kernel,
        grid=(steps,),
        out_shape=shape(dims, BF16),
        in_specs=[block, block, block, columns, columns] + [result] * len(extra),
        out_specs=result,
        compiler_params=params(32),
        cost_estimate=cost(6 * TOKENS * WIDE * units, 12 << 20),
        name="units_grad",
    )(dgate, dup, act, h, top, *extra)


def heads_grad_kernel(raw, heads, h, rows, *rest):
    out = rest[-1]
    for i, (left, right) in enumerate(((raw[:SHARD], h), (raw[SHARD:], h), (heads[...], rows))):
        value = dot(left, right[...], NN)
        cut = pl.ds(i * SHARD, SHARD)
        if len(rest) == 2:
            value = value + rest[0][cut].astype(F32)
        out[cut] = value.astype(BF16)


def heads_grad(raw, heads, h, rows, half, got):
    columns = pl.BlockSpec((TOKENS, WIDE), lambda i: (0, half))
    extra = [] if got is None else [got]
    result = whole((3 * SHARD, WIDE))
    return pl.pallas_call(
        heads_grad_kernel,
        grid=(1,),
        out_shape=shape((3 * SHARD, WIDE), BF16),
        in_specs=[whole((WIDE, TOKENS)), whole((SHARD, TOKENS)), columns, columns]
        + [result] * len(extra),
        out_specs=result,
        compiler_params=params(24),
        cost_estimate=cost(6 * TOKENS * WIDE * SHARD, 6 << 20),
        name="heads_grad",
    )(raw, heads, h, rows, *extra)


def finish_units_kernel(value, gate, up, lower):
    for k, out in enumerate((gate, up)):
        out[...] = value[0, :, k].reshape(-1, SHARD).astype(F32).T
    lower[...] = value[0, :, 2].reshape(-1, SHARD).astype(F32)


def finish_units(value):
    ndp, _, _, units, _ = value.shape
    total = 2 * units * ndp
    across = pl.BlockSpec((SHARD, 2 * units), lambda i: (0, i))
    return pl.pallas_call(
        finish_units_kernel,
        grid=(ndp,),
        out_shape=(shape((SHARD, total), F32),) * 2 + (shape((total, SHARD), F32),),
        in_specs=[pl.BlockSpec((1, *value.shape[1:]), lambda i: (i, 0, 0, 0, 0))],
        out_specs=(across, across, pl.BlockSpec((2 * units, SHARD), lambda i: (i, 0))),
        compiler_params=params(16),
        cost_estimate=cost(0, 14 << 20),
        name="finish_units",
    )(value)


def body(tokens, gain1, w_query, w_keyval, w_out, gain2, w_gate, w_up, w_down, grad_out, segments):
    core, yh, yl = lax.axis_index("core"), lax.axis_index("yhi"), lax.axis_index("ylo")
    ndp = lax.axis_size(DP)
    dp = lax.axis_index(DP)
    mine = core ^ yh
    spot = jnp.stack(
        [yh, yl, 2 * yh + yl, core]
        + [place * QUARTER for place in (core, 3 - core, 1 - core, 2 + core)]
    ).astype(jnp.int32)

    def pick(first_is_mine, own, other):
        return jnp.where(first_is_mine, own, other), jnp.where(first_is_mine, other, own)

    def whole_rows(value):
        own = lax.dynamic_slice_in_dim(value, mine * QUARTER, QUARTER, 0)
        other = lax.dynamic_slice_in_dim(value, (1 - mine) * QUARTER, QUARTER, 0)
        return peers_y(jnp.stack([own, swap(other, "core")]))

    x_pieces = whole_rows(tokens[0])

    gains = jnp.stack([gain1, gain2])
    gains = jnp.stack([gains, swap(gains, "core")], axis=1)
    gains = jnp.stack(pick(yl == 0, gains, swap(gains, "ylo")), axis=2).reshape(2, 1, D)

    def part_of(value, dim):
        size = value.shape[dim] // ndp
        return lax.dynamic_slice_in_dim(value, dp * size, size, dim)

    def exchanged(slab):
        send = lax.dynamic_index_in_dim(slab, 1 - yl, 0, keepdims=False)
        keep = lax.dynamic_index_in_dim(slab, yl, 0, keepdims=False)
        return jnp.concatenate(pick(yl == 0, keep, swap(send, "ylo")), axis=-1)

    def rows_first(weight):
        return weight.T.reshape(2, -1, SHARD)

    qkv_own = exchanged(jnp.concatenate([rows_first(w_query), rows_first(w_keyval)], axis=1))
    qkv_oth = swap(qkv_own, "core")

    piece = gather_y_now(part_of(w_out, 0)).reshape(2, 2, -1, SHARD)
    piece = piece.transpose(0, 2, 1, 3).reshape(2, -1, WIDE)
    out_own = gather_dp_now(piece)
    out_oth = swap(out_own, "core")

    slabs = [part_of(w_gate, 1).T, part_of(w_up, 1).T, part_of(w_down, 0)]
    slab = jnp.stack([s.reshape(2, -1, SHARD) for s in slabs], axis=1)
    feed_own = gather_dp(exchanged(slab))
    feed_oth = swap(feed_own, "core")

    ids = segments[0]
    low_all = jnp.sum((ids[None, :] < ids[:, None]).astype(jnp.int32), axis=1)
    low = jnp.concatenate(
        [
            lax.dynamic_slice_in_dim(low_all, core * QUARTER, QUARTER),
            lax.dynamic_slice_in_dim(low_all, (3 - core) * QUARTER, QUARTER),
        ]
    )
    step = jnp.arange(QUARTER, dtype=jnp.int32)
    place = jnp.concatenate([core * QUARTER + step, (3 - core) * QUARTER + step])
    rates = THETA ** (-jnp.arange(HALF, dtype=F32) * 2.0 / HD)
    angles = rates[:, None] * (place - low).astype(F32)[None, :]
    cosine, sine = jnp.cos(angles), jnp.sin(angles)
    place, low = place[None, :], low[None, :]

    x, h_one, inv_one, queries, keyval = project(
        spot, x_pieces, gains[0], qkv_own, qkv_oth, cosine, sine
    )
    keyval_oth = swap(keyval, "core")
    heads_t, heads, lse = attend(spot, queries, keyval, keyval_oth, place, low)
    mixed, h_two, inv_two = mix(spot, x, peers_y(heads), out_own, out_oth, gains[1])

    top_pieces = whole_rows(grad_out[0])
    top, act, dgate, dup, *parts = feed(spot, h_two, top_pieces, feed_own, feed_oth)
    rows, gain2_part = residual(spot, to_peers_y(parts), mixed, inv_two, top, gains[1])

    row_all, dq, dkv, dkv_oth = attend_back(
        spot, peers_y(rows), out_own, out_oth, queries, keyval, keyval_oth, heads_t, lse, place, low,
        cosine, sine,
    )
    raw, *parts, gain1_part = input_grad(
        spot, dq, dkv, swap(dkv_oth, "core"), cosine, sine, qkv_own, qkv_oth, x, inv_one
    )
    got = sum([g.astype(F32) for g in to_peers_y(parts)])

    def my_block(value):
        return jnp.stack(
            [
                lax.dynamic_slice(value, (yh * QUARTER, j * WIDE + yl * SHARD), (QUARTER, SHARD))
                for j in range(2)
            ]
        )

    def to_home(block):
        return jnp.concatenate(pick(mine == 0, block[0], swap(block[1], "core")))

    gain = jnp.stack(
        [lax.dynamic_slice(gains[0], (0, j * WIDE + yl * SHARD), (1, SHARD)) for j in range(2)]
    )
    inverse = lax.dynamic_slice_in_dim(inv_one, yh * QUARTER, QUARTER, 0)
    normed = my_block(x).astype(F32) * inverse
    scaled = got * gain
    inner = (scaled * normed).sum(axis=(0, 2))
    inner = (inner + swap(inner, "ylo"))[:, None] / D
    grad_in = to_home(my_block(row_all).astype(F32) + inverse * (scaled - normed * inner))

    parts = to_peers_y(down(spot, act, feed_own, feed_oth))
    output = my_block(mixed) + sum([g.astype(F32) for g in parts])
    output = to_home(output.astype(BF16))

    def exchanged_back(value):
        keep = lax.dynamic_slice_in_dim(value, yl * SHARD, SHARD, value.ndim - 1)
        send = lax.dynamic_slice_in_dim(value, (1 - yl) * SHARD, SHARD, value.ndim - 1)
        return jnp.stack(pick(yl == 0, keep, swap(send, "ylo")))

    send = units_grad(dgate, dup, act, h_two, top, 1, None, ndp)
    total = units_grad(dgate, dup, act, h_two, top, 0, swap(send, "core"), ndp)
    total = gather_dp(exchanged_back(scatter_dp(total)))
    grad_w_gate, grad_w_up, grad_w_down = finish_units(total)

    send = heads_grad(raw, heads_t, h_one, row_all, 1, None)
    total = heads_grad(raw, heads_t, h_one, row_all, 0, swap(send, "core"))
    total = exchanged_back(scatter_dp(total.reshape(ndp, -1, WIDE)))
    total = gather_dp_now(total)
    both = total.reshape(ndp, 2, -1, SHARD).transpose(1, 0, 2, 3).reshape(2, -1, SHARD).astype(F32)
    grad_w_query = both[:, :SHARD].reshape(-1, SHARD).T
    grad_w_keyval = both[:, SHARD : 2 * SHARD].reshape(-1, SHARD).T
    grad_w_out = both[:, 2 * SHARD :].reshape(-1, SHARD)

    parts = small_sum(relative_to_absolute(core, jnp.concatenate([gain1_part, gain2_part])))
    parts = lax.dynamic_slice(parts, (0, core * WIDE + yl * SHARD), (2, SHARD))
    return (
        output[None],
        grad_in[None],
        parts[0],
        grad_w_query,
        grad_w_keyval,
        grad_w_out,
        parts[1],
        grad_w_gate,
        grad_w_up,
        grad_w_down,
    )


def relative_to_absolute(core, value):
    turned = jnp.concatenate([value[:, WIDE:], value[:, :WIDE]], axis=1)
    return jnp.where(core == 0, value, turned)


def solution(mesh):
    dp = mesh.shape["dp"]
    side = int(round(dp**0.5))
    fine = Mesh(
        mesh.devices.reshape(side, dp // side, 2, 2, 2), ("x", "z", "ylo", "core", "yhi")
    )
    seq, row, col = DP, ("ylo", "core"), "yhi"
    return jax.shard_map(
        body,
        mesh=fine,
        in_specs=(
            P(seq, col, row),
            P(row),
            P(row, col),
            P(row, col),
            P(col, row),
            P(row),
            P(row, col),
            P(row, col),
            P(col, row),
            P(seq, col, row),
            P(seq, None),
        ),
        out_specs=(
            P(seq, col, row),
            P(seq, col, row),
            P(row),
            P(row, col),
            P(row, col),
            P(col, row),
            P(row),
            P(row, col),
            P(row, col),
            P(col, row),
        ),
        check_vma=False,
    )
```

```python
import functools

import jax
import jax.numpy as jnp
from jax import lax
from jax.experimental import pallas as pl
from jax.experimental.pallas import tpu as pltpu
from jax.sharding import Mesh
from jax.sharding import PartitionSpec as P

D = 1536
HD = 96
HALF = HD // 2
EPS = 1e-05
THETA = 100000.0
NEGATIVE = -1e30
SCALE = HD**-0.5
LOG2E = 1.4426950408889634
F32 = jnp.float32
BF16 = jnp.bfloat16
QUARTER = 256
TOKENS = 2 * QUARTER
CHUNK = 128
WIDE = D // 2
SHARD = D // 4
DP = ("x", "z")

NN = ((1,), (0,))
NT = ((1,), (1,))
TN = ((0,), (0,))


def dot(a, b, dims):
    return lax.dot_general(a, b, (dims, ((), ())), preferred_element_type=F32)


def swap(value, axis, step=1):
    count = lax.axis_size(axis)
    return lax.ppermute(value, axis, [(i, i ^ step) for i in range(count)])


def swap_y(value, k):
    return swap(value, ("ylo", "yhi"), 2 * (k & 1) + (k >> 1))


def peers_y(value):
    return [value] + [swap_y(value, k) for k in (1, 2, 3)]


def to_peers_y(values):
    return [values[0]] + [swap_y(values[k], k) for k in (1, 2, 3)]


def from_peers(value, axis):
    return [value] + [swap(value, axis, k) for k in range(1, lax.axis_size(axis))]


def over_y(value):
    return lax.all_to_all(value, ("yhi", "ylo"), 0, 0, tiled=True)


def gather_y(value):
    return over_y(jnp.broadcast_to(value[None], (4, *value.shape)))


def to_peers(values, axis):
    return [values[0]] + [swap(values[k], axis, k) for k in range(1, lax.axis_size(axis))]


def scatter_dp(value):
    return lax.all_to_all(value, DP, 0, 0, tiled=True)


def gather_dp(value):
    return lax.all_gather(value, DP, axis=0)


def gather_dp_now(value):
    count = lax.axis_size(DP)
    return scatter_dp(jnp.broadcast_to(value[None], (count, *value.shape)))


def together(*values):
    return lax.optimization_barrier(values)


def after(value, *others):
    return lax.optimization_barrier((value, *others))[0]


def shape(dims, dtype):
    return jax.ShapeDtypeStruct(dims, dtype)


def cost(flops, nbytes):
    return pl.CostEstimate(flops=1, bytes_accessed=1, transcendentals=0)


def params(mib=16):
    return pltpu.CompilerParams(vmem_limit_bytes=mib << 20)


def whole(dims):
    return pl.BlockSpec(dims, lambda *_: (0,) * len(dims))


def stage(kernel, name, spot, inputs, outs, flops, scratch=(), mib=16):
    nbytes = sum(v.size * v.dtype.itemsize for v in (*inputs, *outs))
    return pl.pallas_call(
        kernel,
        out_shape=tuple(outs),
        grid_spec=pltpu.PrefetchScalarGridSpec(
            num_scalar_prefetch=1,
            grid=(1,),
            in_specs=[whole(v.shape) for v in inputs],
            out_specs=tuple(whole(v.shape) for v in outs),
            scratch_shapes=scratch,
        ),
        compiler_params=params(mib),
        cost_estimate=cost(flops, nbytes),
        name=name,
    )(spot, *inputs)


def peer(spot, k):
    high = jnp.bitwise_xor(spot[0], k >> 1)
    low = jnp.bitwise_xor(spot[1], k & 1)
    return high, low, 2 * high + low


def place_pieces(spot, pieces, out):
    for k, piece in enumerate(pieces):
        high, low, _ = peer(spot, k)
        rows = pl.ds(pl.multiple_of(high * QUARTER, QUARTER), QUARTER)
        for j in range(2):
            lanes = pl.ds(pl.multiple_of(low * SHARD + j * WIDE, 128), SHARD)
            out[rows, lanes] = piece[pl.ds(j * QUARTER, QUARTER)]


def cut_pieces(spot, value, outs):
    for k, out in enumerate(outs):
        high, low, _ = peer(spot, k)
        rows = pl.ds(pl.multiple_of(high * QUARTER, QUARTER), QUARTER)
        for j in range(2):
            lanes = pl.ds(pl.multiple_of(low * SHARD + j * WIDE, 128), SHARD)
            out[j] = value[rows, lanes].astype(out.dtype)


def turn(front, behind, cosine, sine):
    return front * cosine - behind * sine, behind * cosine + front * sine


def prepare_kernel(
    spot, query, keyval, gate, up, lower, outer, mine, send, units_send, out_send, turned, part
):
    low = spot[1]
    for i, w in enumerate((query, keyval)):
        value = w[...].T
        turned[0, pl.ds(i * SHARD, SHARD)] = value[:SHARD]
        turned[1, pl.ds(i * SHARD, SHARD)] = value[SHARD:]
    mine[...] = turned[low]
    send[...] = turned[1 - low]
    units = part.shape[0] // 2
    for k, value in enumerate((gate[...].T, up[...].T, lower[...])):
        part[...] = value
        units_send[pl.ds(k * units, units)] = part[
            pl.ds(pl.multiple_of((1 - low) * units, 64), units)
        ]
    units_send[3 * units :] = outer[...]
    out_send[...] = outer[...]


def prepare(spot, query, keyval, gate, up, lower, outer, ndp):
    cols = gate.shape[1] // ndp
    across = pl.BlockSpec((SHARD, cols), lambda i, s: (0, s[10]))
    count = WIDE // ndp
    dims = ((WIDE, SHARD), (WIDE, SHARD), (3 * cols // 2 + count, SHARD), (count, SHARD))
    return pl.pallas_call(
        prepare_kernel,
        out_shape=tuple(shape(d, BF16) for d in dims),
        grid_spec=pltpu.PrefetchScalarGridSpec(
            num_scalar_prefetch=1,
            grid=(1,),
            in_specs=[whole(query.shape), whole(keyval.shape), across, across]
            + [pl.BlockSpec((cols, SHARD), lambda i, s: (s[10], 0))]
            + [pl.BlockSpec((count, SHARD), lambda i, s: (s[10], 0))],
            out_specs=tuple(whole(d) for d in dims),
            scratch_shapes=[pltpu.VMEM((2, WIDE, SHARD), BF16), pltpu.VMEM((cols, SHARD), BF16)],
        ),
        compiler_params=params(60),
        cost_estimate=cost(0, 4 << 20),
        name="prepare",
    )(spot, query, keyval, gate, up, lower, outer)


def join_rows(spot, mine, got, out):
    out[:, pl.ds(pl.multiple_of(spot[1] * SHARD, 128), SHARD)] = mine[...]
    out[:, pl.ds(pl.multiple_of((1 - spot[1]) * SHARD, 128), SHARD)] = got[...]


def out_rows_kernel(spot, mine, value, out):
    rows = pl.ds(pl.multiple_of(spot[0] * WIDE, 64), WIDE)
    out[rows, pl.ds(pl.multiple_of(spot[1] * SHARD, 128), SHARD)] = mine[...]
    ndp = value.shape[0]
    count = WIDE // ndp
    base = value.shape[1] - 3 * count
    for i in range(ndp):
        for k in (1, 2, 3):
            high, low, _ = peer(spot, k)
            rows = pl.ds(pl.multiple_of(high * WIDE + i * count, 16), count)
            lanes = pl.ds(pl.multiple_of(low * SHARD, 128), SHARD)
            out[rows, lanes] = value[i, pl.ds(base + (k - 1) * count, count)]


def out_rows(spot, mine, value):
    outs = (shape((D, WIDE), BF16),)
    return stage(out_rows_kernel, "out_rows", spot, (mine, value), outs, 0, mib=60)[0]


def unit_rows_kernel(spot, gate, up, lower, other, out, turned):
    low = spot[1]
    units = out.shape[2]
    for k, value in enumerate((gate[...].T, up[...].T, lower[...])):
        turned[k] = value
    for j in range(out.shape[0]):
        for k in range(3):
            rows = pl.ds(pl.multiple_of((2 * j + low) * units, 64), units)
            out[j, k, :, pl.ds(pl.multiple_of(low * SHARD, 128), SHARD)] = turned[k, rows]
            out[j, k, :, pl.ds(pl.multiple_of((1 - low) * SHARD, 128), SHARD)] = other[
                j, pl.ds(k * units, units)
            ]


def unit_rows(spot, gate, up, lower, other, steps=4):
    ndp, rows, _ = other.shape
    cols = gate.shape[1] // steps
    units = gate.shape[1] // (2 * ndp)
    across = pl.BlockSpec((SHARD, cols), lambda i, s: (0, i))
    dims = (ndp, 3, units, WIDE)
    return pl.pallas_call(
        unit_rows_kernel,
        out_shape=shape(dims, BF16),
        grid_spec=pltpu.PrefetchScalarGridSpec(
            num_scalar_prefetch=1,
            grid=(steps,),
            in_specs=[across, across, pl.BlockSpec((cols, SHARD), lambda i, s: (i, 0))]
            + [pl.BlockSpec((ndp // steps, rows, SHARD), lambda i, s: (i, 0, 0))],
            out_specs=pl.BlockSpec((ndp // steps, *dims[1:]), lambda i, s: (i, 0, 0, 0)),
            scratch_shapes=[pltpu.VMEM((3, cols, SHARD), BF16)],
        ),
        compiler_params=params(60),
        cost_estimate=cost(0, 12 << 20),
        name="unit_rows",
    )(spot, gate, up, lower, other)


def qkv_kernel(
    spot, p0, p1, p2, p3, gain, mine, got, mine_oth, got_oth, cosine, sine,
    x, h, inv, q, kv, own, oth,
):
    place_pieces(spot, (p0, p1, p2, p3), x)
    join_rows(spot, mine, got, own)
    join_rows(spot, mine_oth, got_oth, oth)
    for i in range(4):
        rows = pl.ds(i * CHUNK, CHUNK)
        value = x[rows].astype(F32)
        inverse = lax.rsqrt((value * value).sum(axis=-1, keepdims=True) / D + EPS)
        inv[rows] = inverse
        h[rows] = (value * inverse * gain[...]).astype(BF16)
    cos, sin = cosine[...], sine[...]
    for i in range(4):
        rows = pl.ds(i * 2 * HD, 2 * HD)
        raw = dot(own[rows], h[:, :WIDE], NT) + dot(oth[rows], h[:, WIDE:], NT)
        out, base = (q, i * 2 * HD) if i < 2 else (kv, (i - 2) * 2 * HD)
        for head in range(2):
            front, behind = raw[head * HD : head * HD + HALF], raw[head * HD + HALF : (head + 1) * HD]
            if i < 2 or head == 0:
                front, behind = turn(front, behind, cos, sin)
            out[pl.ds(base + head * HD, HALF)] = front.astype(BF16)
            out[pl.ds(base + head * HD + HALF, HALF)] = behind.astype(BF16)


def project(spot, pieces, gain, rows, cosine, sine):
    outs = (
        shape((TOKENS, D), BF16),
        shape((TOKENS, D), BF16),
        shape((TOKENS, 1), F32),
        shape((SHARD, TOKENS), BF16),
        shape((SHARD, TOKENS), BF16),
        shape((WIDE, WIDE), BF16),
        shape((WIDE, WIDE), BF16),
    )
    inputs = (*pieces, gain, *rows, cosine, sine)
    return stage(qkv_kernel, "project", spot, inputs, outs, 2 * TOKENS * D * WIDE, mib=60)


def key_blocks(block):
    return (0, 2) if block == 0 else (0, 1, 2, 3)


def allowed_keys(spot, key, place, low):
    at = spot[4 + key] + lax.broadcasted_iota(jnp.int32, (QUARTER, place.shape[1]), 0)
    return (at >= low) & (at <= place)


def two_heads(ref, group, block):
    lanes = pl.ds(block * QUARTER, QUARTER)
    return jnp.concatenate(
        [ref[pl.ds((2 * group + h) * HD, HD), lanes] for h in range(2)], axis=1
    )


def twice(ref, block):
    row = ref[:, pl.ds(block * QUARTER, QUARTER)]
    return jnp.concatenate([row, row], axis=1)


def forward_kernel(spot, q_ref, own_ref, oth_ref, place_ref, low_ref, outt_ref, out_ref, lse_ref):
    factor = SCALE * LOG2E
    for group in range(2):
        keys = []
        vals = []
        for ref in (own_ref, oth_ref):
            for half in range(2):
                lanes = pl.ds(half * QUARTER, QUARTER)
                keys.append(ref[pl.ds(group * 2 * HD, HD), lanes].T)
                vals.append(ref[pl.ds(group * 2 * HD + HD, HD), lanes])
        for block in range(2):
            q = two_heads(q_ref, group, block)
            place, low = twice(place_ref, block), twice(low_ref, block)
            scores = []
            for key in key_blocks(block):
                s = dot(keys[key], q, NN)
                scores.append(jnp.where(allowed_keys(spot, key, place, low), s, NEGATIVE))
            peak = scores[0].max(axis=0, keepdims=True)
            for s in scores[1:]:
                peak = jnp.maximum(peak, s.max(axis=0, keepdims=True))
            shift = peak * factor
            total = jnp.zeros_like(peak)
            acc = jnp.zeros((HD, 2 * QUARTER), F32)
            for key, s in zip(key_blocks(block), scores):
                p = jnp.exp2(s * factor - shift)
                total = total + p.sum(axis=0, keepdims=True)
                acc = acc + dot(vals[key], p.astype(BF16), NN)
            acc = (acc / total).astype(BF16)
            lse = shift + jnp.log2(total)
            for h in range(2):
                lanes = pl.ds(block * QUARTER, QUARTER)
                cut = slice(h * QUARTER, (h + 1) * QUARTER)
                outt_ref[pl.ds((2 * group + h) * HD, HD), lanes] = acc[:, cut]
                lse_ref[pl.ds(2 * group + h, 1), lanes] = lse[:, cut]
    out_ref[...] = outt_ref[...].T


def attend(spot, queries, own, other, place, low):
    outs = (
        shape((SHARD, TOKENS), BF16),
        shape((TOKENS, SHARD), BF16),
        shape((4, TOKENS), F32),
    )
    inputs = (queries, own, other, place, low)
    flops = 4 * 4 * HD * QUARTER * QUARTER * 6
    return stage(forward_kernel, "attend_forward", spot, inputs, outs, flops)


def mix_kernel(spot, x, h0, h1, h2, h3, own, oth, gain, mixed, h, inv, heads):
    for k, piece in enumerate((h0, h1, h2, h3)):
        _, _, y = peer(spot, k)
        heads[:, pl.ds(pl.multiple_of(y * SHARD, 128), SHARD)] = piece[...]
    for i in range(2):
        rows = pl.ds(i * QUARTER, QUARTER)
        square = jnp.zeros((QUARTER, 1), F32)
        for j, w in enumerate((own, oth)):
            lanes = pl.ds(j * WIDE, WIDE)
            value = x[rows, lanes].astype(F32)
            value = value + dot(heads[rows], w[...], NN)
            mixed[rows, lanes] = value
            square = square + (value * value).sum(axis=-1, keepdims=True)
        inverse = lax.rsqrt(square / D + EPS)
        inv[rows] = inverse
        h[rows] = (mixed[rows] * inverse * gain[...]).astype(BF16)


def mix(spot, x, pieces, own, oth, gain):
    outs = (shape((TOKENS, D), F32), shape((TOKENS, D), BF16), shape((TOKENS, 1), F32))
    inputs = (x, *pieces, own, oth, gain)
    scratch = [pltpu.VMEM((TOKENS, D), BF16)]
    return stage(mix_kernel, "mix", spot, inputs, outs, 2 * TOKENS * D * D, scratch)


def units_of(ref, k):
    return ref[:, k].reshape(-1, WIDE)


def feed_kernel(
    spot, h, pieces, own, oth, top, act, mine, others, dh, acc, stash
):
    step = pl.program_id(0)

    @pl.when(step == 0)
    def _():
        for y in range(4):
            rows = pl.ds((y // 2) * QUARTER, QUARTER)
            for j in range(2):
                lanes = pl.ds((y % 2) * SHARD + j * WIDE, SHARD)
                top[rows, lanes] = pieces[y, pl.ds(j * QUARTER, QUARTER)]
        acc[...] = jnp.zeros_like(acc)

    def hidden(k, columns):
        return dot(units_of(own, k), columns[:, :WIDE], NT) + dot(
            units_of(oth, k), columns[:, WIDE:], NT
        )

    gate, up, grad = hidden(0, h), hidden(1, h), hidden(2, top)
    sigma = jax.nn.sigmoid(gate)
    silu = gate * sigma
    grad_gate = (grad * up * sigma * (1.0 + gate * (1.0 - sigma))).astype(BF16)
    grad_up = (grad * silu).astype(BF16)
    value = (silu * up).astype(BF16)
    act[...] = value
    half = stash.shape[1] // 2
    for k, v in enumerate((grad_gate, grad_up, value)):
        stash[...] = v.reshape(stash.shape)
        for out, core in ((mine, spot[3]), (others, 1 - spot[3])):
            rows = pl.ds(pl.multiple_of(core * half, half), half)
            out[k] = stash[:, rows].reshape(out.shape[1:])
    grad_gate, grad_up = grad_gate.T, grad_up.T
    for j, w in enumerate((own, oth)):
        lanes = pl.ds(j * WIDE, WIDE)
        acc[:, lanes] += dot(grad_gate, units_of(w, 0), NN) + dot(grad_up, units_of(w, 1), NN)

    @pl.when(step == pl.num_programs(0) - 1)
    def _():
        for y in range(4):
            dh[y] = acc[pl.ds(y * CHUNK, CHUNK)].astype(BF16)


def feed(spot, h, pieces, own, oth):
    steps = 4
    ndp, _, units, _ = own.shape
    total = ndp * units
    weights = pl.BlockSpec((ndp // steps, *own.shape[1:]), lambda i, s: (i, 0, 0, 0))
    block = pl.BlockSpec((total // steps, TOKENS), lambda i, s: (i, 0))
    half = pl.BlockSpec((3, total // (2 * steps), TOKENS), lambda i, s: (0, i, 0))
    return pl.pallas_call(
        feed_kernel,
        out_shape=(
            shape((TOKENS, D), BF16),
            shape((total, TOKENS), BF16),
            *(shape((3, total // 2, TOKENS), BF16),) * 2,
            shape((4, CHUNK, D), BF16),
        ),
        grid_spec=pltpu.PrefetchScalarGridSpec(
            num_scalar_prefetch=1,
            grid=(steps,),
            in_specs=[whole((TOKENS, D)), whole(pieces.shape), weights, weights],
            out_specs=(whole((TOKENS, D)), block, half, half, whole((4, CHUNK, D))),
            scratch_shapes=[
                pltpu.VMEM((TOKENS, D), F32),
                pltpu.VMEM((ndp // steps, units, TOKENS), BF16),
            ],
        ),
        compiler_params=params(20),
        cost_estimate=cost(10 * TOKENS * D * total, 20 << 20),
        name="feed",
    )(spot, h, pieces, own, oth)


def down_kernel(spot, act, own, oth, o0, o1, o2, o3, acc):
    step = pl.program_id(0)

    @pl.when(step == 0)
    def _():
        acc[...] = jnp.zeros_like(acc)

    hidden = act[...].T
    for j, w in enumerate((own, oth)):
        acc[:, pl.ds(j * WIDE, WIDE)] += dot(hidden, w[...].reshape(-1, WIDE), NN)

    @pl.when(step == pl.num_programs(0) - 1)
    def _():
        cut_pieces(spot, acc, (o0, o1, o2, o3))


def down(spot, act, own, oth):
    steps = 4
    group = own.shape[0] // steps
    rows = act.shape[0] // steps
    weights = pl.BlockSpec((group, 1, *own.shape[2:]), lambda i, _: (i, 2, 0, 0))
    return pl.pallas_call(
        down_kernel,
        out_shape=(shape((2, QUARTER, SHARD), BF16),) * 4,
        grid_spec=pltpu.PrefetchScalarGridSpec(
            num_scalar_prefetch=1,
            grid=(steps,),
            in_specs=[pl.BlockSpec((rows, TOKENS), lambda i, _: (i, 0)), weights, weights],
            out_specs=(whole((2, QUARTER, SHARD)),) * 4,
            scratch_shapes=[pltpu.VMEM((TOKENS, D), F32)],
        ),
        compiler_params=params(),
        cost_estimate=cost(2 * TOKENS * D * act.shape[0], 8 << 20),
        name="down",
    )(spot, act, own, oth)


def residual_kernel(spot, pieces, mixed, inv, top, gain, out, part):
    grad = pieces[0].astype(F32)
    for y in range(1, 4):
        grad = grad + pieces[y].astype(F32)
    inverse = inv[...]
    normed = mixed[...] * inverse
    part[...] = (grad * normed).sum(axis=0, keepdims=True)
    scaled = grad * gain[...]
    inner = (scaled * normed).sum(axis=-1, keepdims=True) / D
    out[...] = (top[...].astype(F32) + inverse * (scaled - normed * inner)).astype(BF16)


def residual(spot, pieces, mixed, inv, top, gain):
    mine = lambda width: pl.BlockSpec((CHUNK, width), lambda i, s: (2 * s[0] + s[1], 0))
    return pl.pallas_call(
        residual_kernel,
        out_shape=(shape((CHUNK, D), BF16), shape((1, D), F32)),
        grid_spec=pltpu.PrefetchScalarGridSpec(
            num_scalar_prefetch=1,
            grid=(1,),
            in_specs=[whole((4, CHUNK, D)), mine(D), mine(1), mine(D), whole((1, D))],
            out_specs=(whole((CHUNK, D)), whole((1, D))),
        ),
        compiler_params=params(),
        cost_estimate=cost(CHUNK * D * 20, 4 << 20),
        name="residual",
    )(spot, pieces, mixed, inv, top, gain)


def backward_kernel(
    spot, r0, r1, r2, r3, wown, woth, q_ref, own_ref, oth_ref, o_ref, lse_ref, place_ref, low_ref,
    cosine, sine, rows_ref, dq_ref, down_ref, doth_ref, do_ref,
):
    for k, piece in enumerate((r0, r1, r2, r3)):
        _, _, y = peer(spot, k)
        rows_ref[pl.ds(pl.multiple_of(y * CHUNK, CHUNK), CHUNK)] = piece[...]
    do_ref[...] = (
        dot(wown[...], rows_ref[:, :WIDE], NT) + dot(woth[...], rows_ref[:, WIDE:], NT)
    ).astype(BF16)
    factor = SCALE * LOG2E
    for group in range(2):
        keys, vals, keyst = [], [], []
        for ref in (own_ref, oth_ref):
            for half in range(2):
                lanes = pl.ds(half * QUARTER, QUARTER)
                kt = ref[pl.ds(group * 2 * HD, HD), lanes]
                keyst.append(kt)
                keys.append(kt.T)
                vals.append(ref[pl.ds(group * 2 * HD + HD, HD), lanes].T)
        dks = [jnp.zeros((HD, QUARTER), F32) for _ in range(4)]
        dvs = [jnp.zeros((HD, QUARTER), F32) for _ in range(4)]
        for block in range(2):
            lanes = pl.ds(block * QUARTER, QUARTER)
            q = two_heads(q_ref, group, block)
            do = two_heads(do_ref, group, block)
            o = two_heads(o_ref, group, block)
            place, low = twice(place_ref, block), twice(low_ref, block)
            lse = jnp.concatenate(
                [lse_ref[pl.ds(2 * group + h, 1), lanes] for h in range(2)], axis=1
            )
            delta = (do.astype(F32) * o.astype(F32)).sum(axis=0, keepdims=True)
            dq = jnp.zeros((HD, 2 * QUARTER), F32)
            for key in key_blocks(block):
                s = dot(keys[key], q, NN)
                p = jnp.exp2(s * factor - lse)
                p = jnp.where(allowed_keys(spot, key, place, low), p, 0.0)
                dp = dot(vals[key], do, NN)
                ds = (p * (dp - delta)).astype(BF16)
                dvs[key] = dvs[key] + dot(do, p.astype(BF16), NT)
                dks[key] = dks[key] + dot(q, ds, NT)
                dq = dq + dot(keyst[key], ds, NN)
            dq = dq * SCALE
            cos, sin = twice(cosine, block), twice(sine, block)
            front, behind = turn(dq[:HALF], dq[HALF:], cos, -sin)
            for h in range(2):
                cut = slice(h * QUARTER, (h + 1) * QUARTER)
                base = (2 * group + h) * HD
                dq_ref[pl.ds(base, HALF), lanes] = front[:, cut].astype(BF16)
                dq_ref[pl.ds(base + HALF, HALF), lanes] = behind[:, cut].astype(BF16)
        for i, ref in enumerate((down_ref, doth_ref)):
            for half in range(2):
                lanes = pl.ds(half * QUARTER, QUARTER)
                rows = group * 2 * HD
                ref[pl.ds(rows, HD), lanes] = (dks[2 * i + half] * SCALE).astype(ref.dtype)
                ref[pl.ds(rows + HD, HD), lanes] = dvs[2 * i + half].astype(ref.dtype)


def attend_back(spot, pieces, wown, woth, queries, own, other, outs, lse, place, low, cosine, sine):
    weights = pl.BlockSpec((SHARD, WIDE), lambda i, s: (s[2], 0))
    flat = whole((SHARD, TOKENS))
    row = whole((1, TOKENS))
    return pl.pallas_call(
        backward_kernel,
        out_shape=(
            shape((TOKENS, D), BF16),
            shape((SHARD, TOKENS), BF16),
            shape((SHARD, TOKENS), F32),
            shape((SHARD, TOKENS), BF16),
        ),
        grid_spec=pltpu.PrefetchScalarGridSpec(
            num_scalar_prefetch=1,
            grid=(1,),
            in_specs=[whole((CHUNK, D))] * 4
            + [weights, weights, flat, flat, flat, flat, whole((4, TOKENS)), row, row]
            + [whole((HALF, TOKENS))] * 2,
            out_specs=(whole((TOKENS, D)), flat, flat, flat),
            scratch_shapes=[pltpu.VMEM((SHARD, TOKENS), BF16)],
        ),
        compiler_params=params(60),
        cost_estimate=cost(10 * 4 * HD * QUARTER * QUARTER * 6 + 2 * TOKENS * D * SHARD, 8 << 20),
        name="attend_backward",
    )(spot, *pieces, wown, woth, queries, own, other, outs, lse, place, low, cosine, sine)


def input_kernel(
    spot, dq, mine, got, cosine, sine, own, oth, x, inv, raw, o0, o1, o2, o3, part, acc
):
    raw[:SHARD] = dq[...]
    total = mine[...] + got[...].astype(F32)
    cos, sin = cosine[...], -sine[...]
    for group in range(2):
        base = group * 2 * HD
        front, behind = turn(total[base : base + HALF], total[base + HALF : base + HD], cos, sin)
        raw[pl.ds(SHARD + base, HALF)] = front.astype(BF16)
        raw[pl.ds(SHARD + base + HALF, HALF)] = behind.astype(BF16)
        raw[pl.ds(SHARD + base + HD, HD)] = total[base + HD : base + 2 * HD].astype(BF16)
    grads = raw[...].T
    for j, w in enumerate((own, oth)):
        lanes = pl.ds(j * WIDE, WIDE)
        value = dot(grads, w[...], NN)
        acc[:, lanes] = value.astype(BF16)
        part[:, lanes] = (value * (x[:, lanes].astype(F32) * inv[...])).sum(axis=0, keepdims=True)
    cut_pieces(spot, acc, (o0, o1, o2, o3))


def input_grad(spot, dq, mine, got, cosine, sine, own, oth, x, inv):
    outs = (
        shape((WIDE, TOKENS), BF16),
        *(shape((2, QUARTER, SHARD), BF16),) * 4,
        shape((1, D), F32),
    )
    inputs = (dq, mine, got, cosine, sine, own, oth, x, inv)
    scratch = [pltpu.VMEM((TOKENS, D), BF16)]
    return stage(input_kernel, "input_grad", spot, inputs, outs, 2 * TOKENS * D * WIDE, scratch)


def units_grad_kernel(mine, got, h, h_oth, top, top_oth, out):
    for k in range(3):
        columns, columns_oth = (top, top_oth) if k == 2 else (h, h_oth)
        half = out.shape[1] // 3
        for j in range(2):
            here, there = pl.ds(j * WIDE, WIDE), pl.ds((1 - j) * WIDE, WIDE)
            value = dot(mine[k], columns[:, here], NN) + dot(got[k], columns_oth[:, there], NN)
            out[:, pl.ds(k * half, half), here] = value.astype(BF16).reshape(-1, half, WIDE)


def units_grad(mine, got, h, h_oth, top, top_oth, ndp):
    steps = 2
    total = mine.shape[1]
    block = pl.BlockSpec((3, total // steps, TOKENS), lambda i: (0, i, 0))
    dims = (ndp, 3 * total // ndp, D)
    return pl.pallas_call(
        units_grad_kernel,
        grid=(steps,),
        out_shape=shape(dims, BF16),
        in_specs=[block, block] + [whole((TOKENS, D))] * 4,
        out_specs=pl.BlockSpec((ndp // steps, *dims[1:]), lambda i: (i, 0, 0)),
        compiler_params=params(24),
        cost_estimate=cost(12 * TOKENS * D * total, 12 << 20),
        name="units_grad",
    )(mine, got, h, h_oth, top, top_oth)


def heads_grad_kernel(raw, heads, h, rows, gain1, gain2, *rest):
    out = rest[-1]
    pairs = ((raw[:SHARD], h), (raw[SHARD:], h), (heads[...], rows))
    if len(rest) == 2:
        out[3 * SHARD :] = jnp.zeros((out.shape[0] - 3 * SHARD, WIDE), BF16)
    for i, (left, right) in enumerate(pairs):
        span = pl.ds(i * SHARD, SHARD)
        value = dot(left, right[...], NN)
        if len(rest) == 2:
            value = value + rest[0][span].astype(F32)
        out[span] = value.astype(BF16)
    span = pl.ds(3 * SHARD, 16)
    which = lax.broadcasted_iota(jnp.int32, (16, WIDE), 0)
    value = jnp.where(which == 0, gain1[...], jnp.where(which == 1, gain2[...], 0.0))
    if len(rest) == 2:
        value = value + rest[0][span].astype(F32)
    out[span] = value.astype(BF16)


def heads_grad(raw, heads, h, rows, gain1, gain2, half, *extra):
    columns = pl.BlockSpec((TOKENS, WIDE), lambda i: (0, half))
    gains = pl.BlockSpec((1, WIDE), lambda i: (0, half))
    dims = (3 * SHARD + (128 if extra else 16), WIDE)
    return pl.pallas_call(
        heads_grad_kernel,
        grid=(1,),
        out_shape=shape(dims, BF16),
        in_specs=[whole((WIDE, TOKENS)), whole((SHARD, TOKENS)), columns, columns, gains, gains]
        + [whole(v.shape) for v in extra],
        out_specs=whole(dims),
        compiler_params=params(),
        cost_estimate=cost(6 * TOKENS * WIDE * SHARD, 6 << 20),
        name="heads_grad",
    )(raw, heads, h, rows, gain1, gain2, *extra)


def fold_units_kernel(spot, value, keep, send):
    total = value[0].astype(F32)
    for i in range(1, value.shape[0]):
        total = total + value[i].astype(F32)
    total = total.astype(BF16)
    for j in range(2):
        left, right = total[:, j * WIDE : j * WIDE + SHARD], total[:, j * WIDE + SHARD : (j + 1) * WIDE]

        @pl.when(spot[1] == 0)
        def _():
            keep[j], send[j] = left, right

        @pl.when(spot[1] == 1)
        def _():
            keep[j], send[j] = right, left


def fold_units(spot, value):
    outs = (shape((2, value.shape[1], SHARD), BF16),) * 2
    return stage(fold_units_kernel, "fold_units", spot, (value,), outs, 0)


def fold_kernel(spot, value, keep, send):
    total = value[0].astype(F32)
    for i in range(1, value.shape[0]):
        total = total + value[i].astype(F32)
    left, right = total[:, :SHARD].astype(BF16), total[:, SHARD:].astype(BF16)

    @pl.when(spot[1] == 0)
    def _():
        keep[...] = left
        send[...] = right

    @pl.when(spot[1] == 1)
    def _():
        keep[...] = right
        send[...] = left


def fold(spot, value):
    outs = (shape((value.shape[1], SHARD), BF16),) * 2
    return stage(fold_kernel, "fold", spot, (value,), outs, 0)


def finish_units_kernel(spot, value, gate, up, lower, both):
    half = both.shape[0] // 4
    for j in range(value.shape[0]):
        span = pl.ds(j * 4 * half, 4 * half)
        for i, out in enumerate((gate, up, lower)):
            for place in range(4):
                low = jnp.bitwise_xor(spot[1], place % 2)
                core = jnp.bitwise_xor(spot[3], place // 2)
                rows = pl.ds(pl.multiple_of((2 * low + core) * half, half), half)
                both[rows] = value[j, place, pl.ds(i * half, half)]
            if i < 2:
                out[:, span] = both[...].astype(F32).T
            else:
                out[span] = both[...].astype(F32)


def finish_units(spot, value, steps):
    ndp = value.shape[0]
    half = value.shape[2] // 3
    cols = 4 * half * ndp // steps
    across = pl.BlockSpec((SHARD, cols), lambda i, s: (0, i))
    return pl.pallas_call(
        finish_units_kernel,
        out_shape=(shape((SHARD, cols * steps), F32),) * 2 + (shape((cols * steps, SHARD), F32),),
        grid_spec=pltpu.PrefetchScalarGridSpec(
            num_scalar_prefetch=1,
            grid=(steps,),
            in_specs=[pl.BlockSpec((ndp // steps, *value.shape[1:]), lambda i, s: (i, 0, 0, 0))],
            out_specs=(across, across, pl.BlockSpec((cols, SHARD), lambda i, s: (i, 0))),
            scratch_shapes=[pltpu.VMEM((4 * half, SHARD), BF16)],
        ),
        compiler_params=params(32),
        cost_estimate=cost(0, 14 << 20),
        name="finish_units",
    )(spot, value)


def finish_heads_kernel(spot, value, query, keyval, out, gains, rows):
    count = value.shape[2]
    for i in range(value.shape[0]):
        span = pl.ds(i * count, count)
        rows[spot[1], span] = value[i, 0].astype(F32)
        rows[1 - spot[1], span] = value[i, 1].astype(F32)
    for low in range(2):
        lanes = pl.ds(low * SHARD, SHARD)
        query[:, lanes] = rows[low, :SHARD].T
        keyval[:, lanes] = rows[low, SHARD : 2 * SHARD].T
        out[lanes] = rows[low, 2 * SHARD : 3 * SHARD]
    gains[...] = rows[0, pl.ds(3 * SHARD, 8)] + rows[1, pl.ds(3 * SHARD, 8)]


def finish_heads(spot, value):
    dims = ((SHARD, WIDE), (SHARD, WIDE), (WIDE, SHARD), (8, SHARD))
    scratch = [pltpu.VMEM((2, value.shape[0] * value.shape[2], SHARD), F32)]
    outs = tuple(shape(d, F32) for d in dims)
    return stage(finish_heads_kernel, "finish_heads", spot, (value,), outs, 0, scratch)


def body(tokens, gain1, w_query, w_keyval, w_out, gain2, w_gate, w_up, w_down, grad_out, segments):
    core, yh, yl = lax.axis_index("core"), lax.axis_index("yhi"), lax.axis_index("ylo")
    nx, nz = lax.axis_size("x"), lax.axis_size("z")
    dp = lax.axis_index(DP)
    quarter = core ^ yh
    spot = jnp.stack(
        [yh, yl, 2 * yh + yl, core]
        + [place * QUARTER for place in (core, 3 - core, 1 - core, 2 + core)]
        + [lax.axis_index("x"), lax.axis_index("z"), dp]
    ).astype(jnp.int32)

    def pick(first_is_mine, own, other):
        return jnp.where(first_is_mine, own, other), jnp.where(first_is_mine, other, own)

    def halves_of(value):
        own = lax.dynamic_slice_in_dim(value, quarter * QUARTER, QUARTER, 0)
        return own, lax.dynamic_slice_in_dim(value, (1 - quarter) * QUARTER, QUARTER, 0)

    gains = jnp.stack([gain1, gain2])
    gains = jnp.stack([gains, swap(gains, "core")], axis=1)
    gains = jnp.stack(pick(yl == 0, gains, swap(gains, "ylo")), axis=2).reshape(2, 1, D)

    head_mine, head_send, unit_send, out_send = prepare(
        spot, w_query, w_keyval, w_gate, w_up, w_down, w_out, nx * nz
    )
    others = gather_dp(
        jnp.concatenate([swap_y(unit_send, 1), swap_y(out_send, 2), swap_y(out_send, 3)])
    )

    (x_own, x_other), (top_own, top_other) = halves_of(tokens[0]), halves_of(grad_out[0])
    got = swap(jnp.concatenate([x_other, top_other]), "core")
    pieces = peers_y(jnp.concatenate([x_own, got[:QUARTER]]))
    top_pair = jnp.concatenate([top_own, got[QUARTER:]])
    head_got = swap(head_send, "ylo")
    *pieces, head_got, head_mine, gains, top_pair = together(
        *pieces, head_got, head_mine, gains, top_pair
    )
    head_pieces = (head_mine, head_got, swap(head_mine, "core"), swap(head_got, "core"))

    ids = segments[0]
    low_all = jnp.sum((ids[None, :] < ids[:, None]).astype(jnp.int32), axis=1)
    low = jnp.concatenate(
        [
            lax.dynamic_slice_in_dim(low_all, core * QUARTER, QUARTER),
            lax.dynamic_slice_in_dim(low_all, (3 - core) * QUARTER, QUARTER),
        ]
    )
    step = jnp.arange(QUARTER, dtype=jnp.int32)
    place = jnp.concatenate([core * QUARTER + step, (3 - core) * QUARTER + step])
    rates = THETA ** (-jnp.arange(HALF, dtype=F32) * 2.0 / HD)
    angles = rates[:, None] * (place - low).astype(F32)[None, :]
    cosine, sine = jnp.cos(angles), jnp.sin(angles)
    place, low = place[None, :], low[None, :]

    x, h_one, inv_one, queries, keyval, head_rows, head_rows_oth = project(
        spot, pieces, gains[0], head_pieces, cosine, sine
    )
    keyval_oth = swap(keyval, "core")
    top_pieces = gather_y(after(top_pair, head_pieces[3]))
    others = after(others, queries)
    w_o = out_rows(spot, w_out, others)
    w_f = unit_rows(spot, w_gate, w_up, w_down, after(others, w_o))
    top_pieces, w_f, w_o, low, keyval_oth = together(top_pieces, w_f, w_o, low, keyval_oth)
    w_o_oth, w_f_oth = swap(w_o, "core"), swap(w_f, "core")
    heads_t, heads, lse = attend(spot, queries, keyval, keyval_oth, place, low)
    heads_pieces = peers_y(heads)
    mixed, h_two, inv_two = mix(spot, x, heads_pieces, w_o, w_o_oth, gains[1])
    top, act, mine, send, parts = feed(spot, h_two, top_pieces, w_f, w_f_oth)
    parts = over_y(parts)

    got, h_two_oth, top_oth = swap(send, "core"), swap(h_two, "core"), swap(top, "core")
    unit_parts = units_grad(mine, got, h_two, h_two_oth, top, top_oth, nx * nz)
    rows, gain2_part = residual(spot, parts, mixed, inv_two, top, gains[1])
    unit_parts = scatter_dp(unit_parts)

    row_all, dq, dkv, dkv_oth = attend_back(
        spot, peers_y(rows), w_o, w_o_oth, queries, keyval, keyval_oth, heads_t, lse, place, low,
        cosine, sine,
    )
    raw, *parts, gain1_part = input_grad(
        spot, dq, dkv, swap(dkv_oth, "core"), cosine, sine, head_rows, head_rows_oth, x, inv_one
    )
    parts = to_peers_y(parts)
    grads = (raw, heads_t, h_one, row_all, gain1_part, gain2_part)
    send = heads_grad(*grads, 1)
    head_parts = heads_grad(*grads, 0, swap(send, "core"))
    unit_parts = after(unit_parts, head_parts)
    head_parts = scatter_dp(head_parts.reshape(nx * nz, -1, WIDE))

    keep, send = fold_units(spot, unit_parts)
    got = swap(send, "ylo")
    got_oth = swap(jnp.stack([keep[1], got[1]]), "core")
    unit_parts = gather_dp(jnp.stack([keep[0], got[0], got_oth[0], got_oth[1]]))
    keep, send = fold(spot, head_parts)
    head_parts = gather_dp_now(jnp.stack([keep, swap(send, "ylo")]))

    got = sum([g.astype(F32) for g in parts])

    def my_block(value):
        return jnp.stack(
            [
                lax.dynamic_slice(value, (yh * QUARTER, j * WIDE + yl * SHARD), (QUARTER, SHARD))
                for j in range(2)
            ]
        )

    def to_home(block):
        return jnp.concatenate(pick(quarter == 0, block[0], swap(block[1], "core")))

    gain = jnp.stack(
        [lax.dynamic_slice(gains[0], (0, j * WIDE + yl * SHARD), (1, SHARD)) for j in range(2)]
    )
    inverse = lax.dynamic_slice_in_dim(inv_one, yh * QUARTER, QUARTER, 0)
    normed = my_block(x).astype(F32) * inverse
    scaled = got * gain
    inner = (scaled * normed).sum(axis=(0, 2))
    inner = (inner + swap(inner, "ylo"))[:, None] / D
    grad_in = to_home(my_block(row_all).astype(F32) + inverse * (scaled - normed * inner))

    parts = to_peers_y(down(spot, after(act, raw), w_f, w_f_oth))
    output = my_block(mixed) + sum([g.astype(F32) for g in parts])
    output = to_home(output.astype(BF16))

    grad_w_gate, grad_w_up, grad_w_down = finish_units(spot, unit_parts, nx)
    head_parts, grad_w_down = together(head_parts, grad_w_down)
    grad_w_query, grad_w_keyval, grad_w_out, sums = finish_heads(spot, head_parts)
    sums = sums + swap(sums, "yhi")
    return (
        output[None],
        grad_in[None],
        sums[0],
        grad_w_query,
        grad_w_keyval,
        grad_w_out,
        sums[1],
        grad_w_gate,
        grad_w_up,
        grad_w_down,
    )


def solution(mesh):
    dp = mesh.shape["dp"]
    side = int(round(dp**0.5))
    fine = Mesh(
        mesh.devices.reshape(side, dp // side, 2, 2, 2), ("x", "z", "ylo", "core", "yhi")
    )
    seq, row, col = DP, ("ylo", "core"), "yhi"
    return jax.shard_map(
        body,
        mesh=fine,
        in_specs=(
            P(seq, col, row),
            P(row),
            P(row, col),
            P(row, col),
            P(col, row),
            P(row),
            P(row, col),
            P(row, col),
            P(col, row),
            P(seq, col, row),
            P(seq, None),
        ),
        out_specs=(
            P(seq, col, row),
            P(seq, col, row),
            P(row),
            P(row, col),
            P(row, col),
            P(col, row),
            P(row),
            P(row, col),
            P(row, col),
            P(col, row),
        ),
        check_vma=False,
    )
```

```python
import functools

import jax
import jax.numpy as jnp
from jax import lax
from jax.experimental import pallas as pl
from jax.experimental.pallas import tpu as pltpu
from jax.sharding import Mesh
from jax.sharding import PartitionSpec as P

D = 1536
HD = 96
HALF = HD // 2
EPS = 1e-05
THETA = 100000.0
NEGATIVE = -1e30
SCALE = HD**-0.5
LOG2E = 1.4426950408889634
F32 = jnp.float32
BF16 = jnp.bfloat16
QUARTER = 256
TOKENS = 2 * QUARTER
CHUNK = 128
WIDE = D // 2
SHARD = D // 4
DP = ("x", "z")

NN = ((1,), (0,))
NT = ((1,), (1,))
TN = ((0,), (0,))


def dot(a, b, dims):
    return lax.dot_general(a, b, (dims, ((), ())), preferred_element_type=F32)


def swap(value, axis, step=1):
    count = lax.axis_size(axis)
    return lax.ppermute(value, axis, [(i, i ^ step) for i in range(count)])


def swap_y(value, k):
    return swap(value, ("ylo", "yhi"), 2 * (k & 1) + (k >> 1))


def peers_y(value):
    return [value] + [swap_y(value, k) for k in (1, 2, 3)]


def to_peers_y(values):
    return [values[0]] + [swap_y(values[k], k) for k in (1, 2, 3)]


def from_peers(value, axis):
    return [value] + [swap(value, axis, k) for k in range(1, lax.axis_size(axis))]


def over_y(value):
    return lax.all_to_all(value, ("yhi", "ylo"), 0, 0, tiled=True)


def gather_y(value):
    return over_y(jnp.broadcast_to(value[None], (4, *value.shape)))


def to_peers(values, axis):
    return [values[0]] + [swap(values[k], axis, k) for k in range(1, lax.axis_size(axis))]


def scatter_dp(value):
    return lax.all_to_all(value, DP, 0, 0, tiled=True)


def gather_dp(value):
    return lax.all_gather(value, DP, axis=0)


def gather_dp_now(value):
    count = lax.axis_size(DP)
    return scatter_dp(jnp.broadcast_to(value[None], (count, *value.shape)))


def together(*values):
    return lax.optimization_barrier(values)


def after(value, *others):
    return lax.optimization_barrier((value, *others))[0]


def shape(dims, dtype):
    return jax.ShapeDtypeStruct(dims, dtype)


def cost(flops, nbytes):
    return pl.CostEstimate(flops=1, bytes_accessed=1, transcendentals=0)


def params(mib=60):
    return pltpu.CompilerParams(vmem_limit_bytes=mib << 20)


def whole(dims):
    return pl.BlockSpec(dims, lambda *_: (0,) * len(dims))


def stage(kernel, name, spot, inputs, outs, flops, scratch=(), mib=60):
    nbytes = sum(v.size * v.dtype.itemsize for v in (*inputs, *outs))
    return pl.pallas_call(
        kernel,
        out_shape=tuple(outs),
        grid_spec=pltpu.PrefetchScalarGridSpec(
            num_scalar_prefetch=1,
            grid=(1,),
            in_specs=[whole(v.shape) for v in inputs],
            out_specs=tuple(whole(v.shape) for v in outs),
            scratch_shapes=scratch,
        ),
        compiler_params=params(mib),
        cost_estimate=cost(flops, nbytes),
        name=name,
    )(spot, *inputs)


def peer(spot, k):
    high = jnp.bitwise_xor(spot[0], k >> 1)
    low = jnp.bitwise_xor(spot[1], k & 1)
    return high, low, 2 * high + low


def place_pieces(spot, pieces, out):
    for k, piece in enumerate(pieces):
        high, low, _ = peer(spot, k)
        rows = pl.ds(pl.multiple_of(high * QUARTER, QUARTER), QUARTER)
        for j in range(2):
            lanes = pl.ds(pl.multiple_of(low * SHARD + j * WIDE, 128), SHARD)
            out[rows, lanes] = piece[pl.ds(j * QUARTER, QUARTER)]


def cut_pieces(spot, value, outs):
    for k, out in enumerate(outs):
        high, low, _ = peer(spot, k)
        rows = pl.ds(pl.multiple_of(high * QUARTER, QUARTER), QUARTER)
        for j in range(2):
            lanes = pl.ds(pl.multiple_of(low * SHARD + j * WIDE, 128), SHARD)
            out[j] = value[rows, lanes].astype(out.dtype)


def turn(front, behind, cosine, sine):
    return front * cosine - behind * sine, behind * cosine + front * sine


def prepare_kernel(
    spot, query, keyval, gate, up, lower, outer, mine, send, units_send, out_send, turned, part
):
    low = spot[1]
    for i, w in enumerate((query, keyval)):
        value = w[...].T
        turned[0, pl.ds(i * SHARD, SHARD)] = value[:SHARD]
        turned[1, pl.ds(i * SHARD, SHARD)] = value[SHARD:]
    mine[...] = turned[low]
    send[...] = turned[1 - low]
    units = part.shape[0] // 2
    for k, value in enumerate((gate[...].T, up[...].T, lower[...])):
        part[...] = value
        units_send[pl.ds(k * units, units)] = part[
            pl.ds(pl.multiple_of((1 - low) * units, 64), units)
        ]
    units_send[3 * units :] = outer[...]
    out_send[...] = outer[...]


def prepare(spot, query, keyval, gate, up, lower, outer, ndp):
    cols = gate.shape[1] // ndp
    across = pl.BlockSpec((SHARD, cols), lambda i, s: (0, s[10]))
    count = WIDE // ndp
    dims = ((WIDE, SHARD), (WIDE, SHARD), (3 * cols // 2 + count, SHARD), (count, SHARD))
    return pl.pallas_call(
        prepare_kernel,
        out_shape=tuple(shape(d, BF16) for d in dims),
        grid_spec=pltpu.PrefetchScalarGridSpec(
            num_scalar_prefetch=1,
            grid=(1,),
            in_specs=[whole(query.shape), whole(keyval.shape), across, across]
            + [pl.BlockSpec((cols, SHARD), lambda i, s: (s[10], 0))]
            + [pl.BlockSpec((count, SHARD), lambda i, s: (s[10], 0))],
            out_specs=tuple(whole(d) for d in dims),
            scratch_shapes=[pltpu.VMEM((2, WIDE, SHARD), BF16), pltpu.VMEM((cols, SHARD), BF16)],
        ),
        compiler_params=params(60),
        cost_estimate=cost(0, 4 << 20),
        name="prepare",
    )(spot, query, keyval, gate, up, lower, outer)


def join_rows(spot, mine, got, out):
    out[:, pl.ds(pl.multiple_of(spot[1] * SHARD, 128), SHARD)] = mine[...]
    out[:, pl.ds(pl.multiple_of((1 - spot[1]) * SHARD, 128), SHARD)] = got[...]


def out_rows_kernel(spot, mine, value, out):
    rows = pl.ds(pl.multiple_of(spot[0] * WIDE, 64), WIDE)
    out[rows, pl.ds(pl.multiple_of(spot[1] * SHARD, 128), SHARD)] = mine[...]
    ndp = value.shape[0]
    count = WIDE // ndp
    base = value.shape[1] - 3 * count
    for i in range(ndp):
        for k in (1, 2, 3):
            high, low, _ = peer(spot, k)
            rows = pl.ds(pl.multiple_of(high * WIDE + i * count, 16), count)
            lanes = pl.ds(pl.multiple_of(low * SHARD, 128), SHARD)
            out[rows, lanes] = value[i, pl.ds(base + (k - 1) * count, count)]


def out_rows(spot, mine, value):
    outs = (shape((D, WIDE), BF16),)
    return stage(out_rows_kernel, "out_rows", spot, (mine, value), outs, 0, mib=60)[0]


def unit_rows_kernel(spot, gate, up, lower, other, out, turned):
    low = spot[1]
    units = out.shape[2]
    for k, value in enumerate((gate[...].T, up[...].T, lower[...])):
        turned[k] = value
    for j in range(out.shape[0]):
        for k in range(3):
            rows = pl.ds(pl.multiple_of((2 * j + low) * units, 64), units)
            out[j, k, :, pl.ds(pl.multiple_of(low * SHARD, 128), SHARD)] = turned[k, rows]
            out[j, k, :, pl.ds(pl.multiple_of((1 - low) * SHARD, 128), SHARD)] = other[
                j, pl.ds(k * units, units)
            ]


def unit_rows(spot, gate, up, lower, other, steps=4):
    ndp, rows, _ = other.shape
    cols = gate.shape[1] // steps
    units = gate.shape[1] // (2 * ndp)
    across = pl.BlockSpec((SHARD, cols), lambda i, s: (0, i))
    dims = (ndp, 3, units, WIDE)
    return pl.pallas_call(
        unit_rows_kernel,
        out_shape=shape(dims, BF16),
        grid_spec=pltpu.PrefetchScalarGridSpec(
            num_scalar_prefetch=1,
            grid=(steps,),
            in_specs=[across, across, pl.BlockSpec((cols, SHARD), lambda i, s: (i, 0))]
            + [pl.BlockSpec((ndp // steps, rows, SHARD), lambda i, s: (i, 0, 0))],
            out_specs=pl.BlockSpec((ndp // steps, *dims[1:]), lambda i, s: (i, 0, 0, 0)),
            scratch_shapes=[pltpu.VMEM((3, cols, SHARD), BF16)],
        ),
        compiler_params=params(60),
        cost_estimate=cost(0, 12 << 20),
        name="unit_rows",
    )(spot, gate, up, lower, other)


def qkv_kernel(
    spot, p0, p1, p2, p3, gain, mine, got, mine_oth, got_oth, cosine, sine,
    x, h, inv, q, kv, own, oth,
):
    place_pieces(spot, (p0, p1, p2, p3), x)
    join_rows(spot, mine, got, own)
    join_rows(spot, mine_oth, got_oth, oth)
    for i in range(4):
        rows = pl.ds(i * CHUNK, CHUNK)
        value = x[rows].astype(F32)
        inverse = lax.rsqrt((value * value).sum(axis=-1, keepdims=True) / D + EPS)
        inv[rows] = inverse
        h[rows] = (value * inverse * gain[...]).astype(BF16)
    cos, sin = cosine[...], sine[...]
    for i in range(4):
        rows = pl.ds(i * 2 * HD, 2 * HD)
        raw = dot(own[rows], h[:, :WIDE], NT) + dot(oth[rows], h[:, WIDE:], NT)
        out, base = (q, i * 2 * HD) if i < 2 else (kv, (i - 2) * 2 * HD)
        for head in range(2):
            front, behind = raw[head * HD : head * HD + HALF], raw[head * HD + HALF : (head + 1) * HD]
            if i < 2 or head == 0:
                front, behind = turn(front, behind, cos, sin)
            out[pl.ds(base + head * HD, HALF)] = front.astype(BF16)
            out[pl.ds(base + head * HD + HALF, HALF)] = behind.astype(BF16)


def project(spot, pieces, gain, rows, cosine, sine):
    outs = (
        shape((TOKENS, D), BF16),
        shape((TOKENS, D), BF16),
        shape((TOKENS, 1), F32),
        shape((SHARD, TOKENS), BF16),
        shape((SHARD, TOKENS), BF16),
        shape((WIDE, WIDE), BF16),
        shape((WIDE, WIDE), BF16),
    )
    inputs = (*pieces, gain, *rows, cosine, sine)
    return stage(qkv_kernel, "project", spot, inputs, outs, 2 * TOKENS * D * WIDE, mib=60)


def key_blocks(block):
    return (0, 2) if block == 0 else (0, 1, 2, 3)


def allowed_keys(spot, key, place, low):
    at = spot[4 + key] + lax.broadcasted_iota(jnp.int32, (QUARTER, place.shape[1]), 0)
    return (at >= low) & (at <= place)


def two_heads(ref, group, block):
    lanes = pl.ds(block * QUARTER, QUARTER)
    return jnp.concatenate(
        [ref[pl.ds((2 * group + h) * HD, HD), lanes] for h in range(2)], axis=1
    )


def twice(ref, block):
    row = ref[:, pl.ds(block * QUARTER, QUARTER)]
    return jnp.concatenate([row, row], axis=1)


def half_of(core, first=0):
    return pl.ds(pl.multiple_of(first + core * (SHARD // 2), 64), SHARD // 2)


def forward_kernel(
    spot, q_ref, own_ref, oth_ref, place_ref, low_ref, outt_ref, out_ref, lse_ref, mine_ref, send_ref
):
    factor = SCALE * LOG2E
    for group in range(2):
        keys = []
        vals = []
        for ref in (own_ref, oth_ref):
            for half in range(2):
                lanes = pl.ds(half * QUARTER, QUARTER)
                keys.append(ref[pl.ds(group * 2 * HD, HD), lanes].T)
                vals.append(ref[pl.ds(group * 2 * HD + HD, HD), lanes])
        for block in range(2):
            q = two_heads(q_ref, group, block)
            place, low = twice(place_ref, block), twice(low_ref, block)
            scores = []
            for key in key_blocks(block):
                s = dot(keys[key], q, NN)
                scores.append(jnp.where(allowed_keys(spot, key, place, low), s, NEGATIVE))
            peak = scores[0].max(axis=0, keepdims=True)
            for s in scores[1:]:
                peak = jnp.maximum(peak, s.max(axis=0, keepdims=True))
            shift = peak * factor
            total = jnp.zeros_like(peak)
            acc = jnp.zeros((HD, 2 * QUARTER), F32)
            for key, s in zip(key_blocks(block), scores):
                p = jnp.exp2(s * factor - shift)
                total = total + p.sum(axis=0, keepdims=True)
                acc = acc + dot(vals[key], p.astype(BF16), NN)
            acc = (acc / total).astype(BF16)
            lse = shift + jnp.log2(total)
            for h in range(2):
                lanes = pl.ds(block * QUARTER, QUARTER)
                cut = slice(h * QUARTER, (h + 1) * QUARTER)
                outt_ref[pl.ds((2 * group + h) * HD, HD), lanes] = acc[:, cut]
                lse_ref[pl.ds(2 * group + h, 1), lanes] = lse[:, cut]
    out_ref[...] = outt_ref[...].T
    for ref, core in ((mine_ref, spot[3]), (send_ref, 1 - spot[3])):
        ref[...] = outt_ref[half_of(core)]


def attend(spot, queries, own, other, place, low):
    outs = (
        shape((SHARD, TOKENS), BF16),
        shape((TOKENS, SHARD), BF16),
        shape((4, TOKENS), F32),
        *(shape((SHARD // 2, TOKENS), BF16),) * 2,
    )
    inputs = (queries, own, other, place, low)
    flops = 4 * 4 * HD * QUARTER * QUARTER * 6
    return stage(forward_kernel, "attend_forward", spot, inputs, outs, flops)


def mix_kernel(spot, x, h0, h1, h2, h3, own, oth, gain, mixed, h, inv, heads):
    for k, piece in enumerate((h0, h1, h2, h3)):
        _, _, y = peer(spot, k)
        heads[:, pl.ds(pl.multiple_of(y * SHARD, 128), SHARD)] = piece[...]
    for i in range(2):
        rows = pl.ds(i * QUARTER, QUARTER)
        square = jnp.zeros((QUARTER, 1), F32)
        for j, w in enumerate((own, oth)):
            lanes = pl.ds(j * WIDE, WIDE)
            value = x[rows, lanes].astype(F32)
            value = value + dot(heads[rows], w[...], NN)
            mixed[rows, lanes] = value
            square = square + (value * value).sum(axis=-1, keepdims=True)
        inverse = lax.rsqrt(square / D + EPS)
        inv[rows] = inverse
        h[rows] = (mixed[rows] * inverse * gain[...]).astype(BF16)


def mix(spot, x, pieces, own, oth, gain):
    outs = (shape((TOKENS, D), F32), shape((TOKENS, D), BF16), shape((TOKENS, 1), F32))
    inputs = (x, *pieces, own, oth, gain)
    scratch = [pltpu.VMEM((TOKENS, D), BF16)]
    return stage(mix_kernel, "mix", spot, inputs, outs, 2 * TOKENS * D * D, scratch)


def units_of(ref, k):
    return ref[:, k].reshape(-1, WIDE)


def feed_kernel(
    spot, h, pieces, own, oth, top, act, mine, others, dh, acc, stash
):
    step = pl.program_id(0)

    @pl.when(step == 0)
    def _():
        for y in range(4):
            rows = pl.ds((y // 2) * QUARTER, QUARTER)
            for j in range(2):
                lanes = pl.ds((y % 2) * SHARD + j * WIDE, SHARD)
                top[rows, lanes] = pieces[y, pl.ds(j * QUARTER, QUARTER)]
        acc[...] = jnp.zeros_like(acc)

    def hidden(k, columns):
        return dot(units_of(own, k), columns[:, :WIDE], NT) + dot(
            units_of(oth, k), columns[:, WIDE:], NT
        )

    gate, up, grad = hidden(0, h), hidden(1, h), hidden(2, top)
    sigma = jax.nn.sigmoid(gate)
    silu = gate * sigma
    grad_gate = (grad * up * sigma * (1.0 + gate * (1.0 - sigma))).astype(BF16)
    grad_up = (grad * silu).astype(BF16)
    value = (silu * up).astype(BF16)
    act[...] = value
    half = stash.shape[1] // 2
    for k, v in enumerate((grad_gate, grad_up, value)):
        stash[...] = v.reshape(stash.shape)
        for out, core in ((mine, spot[3]), (others, 1 - spot[3])):
            rows = pl.ds(pl.multiple_of(core * half, half), half)
            out[k] = stash[:, rows].reshape(out.shape[1:])
    grad_gate, grad_up = grad_gate.T, grad_up.T
    for j, w in enumerate((own, oth)):
        lanes = pl.ds(j * WIDE, WIDE)
        acc[:, lanes] += dot(grad_gate, units_of(w, 0), NN) + dot(grad_up, units_of(w, 1), NN)

    @pl.when(step == pl.num_programs(0) - 1)
    def _():
        for y in range(4):
            dh[y] = acc[pl.ds(y * CHUNK, CHUNK)].astype(BF16)


def feed(spot, h, pieces, own, oth):
    steps = 4
    ndp, _, units, _ = own.shape
    total = ndp * units
    weights = pl.BlockSpec((ndp // steps, *own.shape[1:]), lambda i, s: (i, 0, 0, 0))
    block = pl.BlockSpec((total // steps, TOKENS), lambda i, s: (i, 0))
    half = pl.BlockSpec((3, total // (2 * steps), TOKENS), lambda i, s: (0, i, 0))
    return pl.pallas_call(
        feed_kernel,
        out_shape=(
            shape((TOKENS, D), BF16),
            shape((total, TOKENS), BF16),
            *(shape((3, total // 2, TOKENS), BF16),) * 2,
            shape((4, CHUNK, D), BF16),
        ),
        grid_spec=pltpu.PrefetchScalarGridSpec(
            num_scalar_prefetch=1,
            grid=(steps,),
            in_specs=[whole((TOKENS, D)), whole(pieces.shape), weights, weights],
            out_specs=(whole((TOKENS, D)), block, half, half, whole((4, CHUNK, D))),
            scratch_shapes=[
                pltpu.VMEM((TOKENS, D), F32),
                pltpu.VMEM((ndp // steps, units, TOKENS), BF16),
            ],
        ),
        compiler_params=params(60),
        cost_estimate=cost(10 * TOKENS * D * total, 20 << 20),
        name="feed",
    )(spot, h, pieces, own, oth)


def down_kernel(spot, act, own, oth, o0, o1, o2, o3, acc):
    step = pl.program_id(0)

    @pl.when(step == 0)
    def _():
        acc[...] = jnp.zeros_like(acc)

    hidden = act[...].T
    for j, w in enumerate((own, oth)):
        acc[:, pl.ds(j * WIDE, WIDE)] += dot(hidden, w[...].reshape(-1, WIDE), NN)

    @pl.when(step == pl.num_programs(0) - 1)
    def _():
        cut_pieces(spot, acc, (o0, o1, o2, o3))


def down(spot, act, own, oth):
    steps = 4
    group = own.shape[0] // steps
    rows = act.shape[0] // steps
    weights = pl.BlockSpec((group, 1, *own.shape[2:]), lambda i, _: (i, 2, 0, 0))
    return pl.pallas_call(
        down_kernel,
        out_shape=(shape((2, QUARTER, SHARD), BF16),) * 4,
        grid_spec=pltpu.PrefetchScalarGridSpec(
            num_scalar_prefetch=1,
            grid=(steps,),
            in_specs=[pl.BlockSpec((rows, TOKENS), lambda i, _: (i, 0)), weights, weights],
            out_specs=(whole((2, QUARTER, SHARD)),) * 4,
            scratch_shapes=[pltpu.VMEM((TOKENS, D), F32)],
        ),
        compiler_params=params(60),
        cost_estimate=cost(2 * TOKENS * D * act.shape[0], 8 << 20),
        name="down",
    )(spot, act, own, oth)


def residual_kernel(spot, pieces, mixed, inv, top, gain, out, part):
    grad = pieces[0].astype(F32)
    for y in range(1, 4):
        grad = grad + pieces[y].astype(F32)
    inverse = inv[...]
    normed = mixed[...] * inverse
    part[...] = (grad * normed).sum(axis=0, keepdims=True)
    scaled = grad * gain[...]
    inner = (scaled * normed).sum(axis=-1, keepdims=True) / D
    out[...] = (top[...].astype(F32) + inverse * (scaled - normed * inner)).astype(BF16)


def residual(spot, pieces, mixed, inv, top, gain):
    mine = lambda width: pl.BlockSpec((CHUNK, width), lambda i, s: (2 * s[0] + s[1], 0))
    return pl.pallas_call(
        residual_kernel,
        out_shape=(shape((CHUNK, D), BF16), shape((1, D), F32)),
        grid_spec=pltpu.PrefetchScalarGridSpec(
            num_scalar_prefetch=1,
            grid=(1,),
            in_specs=[whole((4, CHUNK, D)), mine(D), mine(1), mine(D), whole((1, D))],
            out_specs=(whole((CHUNK, D)), whole((1, D))),
        ),
        compiler_params=params(60),
        cost_estimate=cost(CHUNK * D * 20, 4 << 20),
        name="residual",
    )(spot, pieces, mixed, inv, top, gain)


def backward_kernel(
    spot, r0, r1, r2, r3, wown, woth, q_ref, own_ref, oth_ref, o_ref, lse_ref, place_ref, low_ref,
    cosine, sine, rows_ref, dq_ref, down_ref, doth_ref, do_ref,
):
    for k, piece in enumerate((r0, r1, r2, r3)):
        _, _, y = peer(spot, k)
        rows_ref[pl.ds(pl.multiple_of(y * CHUNK, CHUNK), CHUNK)] = piece[...]
    do_ref[...] = (
        dot(wown[...], rows_ref[:, :WIDE], NT) + dot(woth[...], rows_ref[:, WIDE:], NT)
    ).astype(BF16)
    factor = SCALE * LOG2E
    for group in range(2):
        keys, vals, keyst = [], [], []
        for ref in (own_ref, oth_ref):
            for half in range(2):
                lanes = pl.ds(half * QUARTER, QUARTER)
                kt = ref[pl.ds(group * 2 * HD, HD), lanes]
                keyst.append(kt)
                keys.append(kt.T)
                vals.append(ref[pl.ds(group * 2 * HD + HD, HD), lanes].T)
        dks = [jnp.zeros((HD, QUARTER), F32) for _ in range(4)]
        dvs = [jnp.zeros((HD, QUARTER), F32) for _ in range(4)]
        for block in range(2):
            lanes = pl.ds(block * QUARTER, QUARTER)
            q = two_heads(q_ref, group, block)
            do = two_heads(do_ref, group, block)
            o = two_heads(o_ref, group, block)
            place, low = twice(place_ref, block), twice(low_ref, block)
            lse = jnp.concatenate(
                [lse_ref[pl.ds(2 * group + h, 1), lanes] for h in range(2)], axis=1
            )
            delta = (do.astype(F32) * o.astype(F32)).sum(axis=0, keepdims=True)
            dq = jnp.zeros((HD, 2 * QUARTER), F32)
            for key in key_blocks(block):
                s = dot(keys[key], q, NN)
                p = jnp.exp2(s * factor - lse)
                p = jnp.where(allowed_keys(spot, key, place, low), p, 0.0)
                dp = dot(vals[key], do, NN)
                ds = (p * (dp - delta)).astype(BF16)
                dvs[key] = dvs[key] + dot(do, p.astype(BF16), NT)
                dks[key] = dks[key] + dot(q, ds, NT)
                dq = dq + dot(keyst[key], ds, NN)
            dq = dq * SCALE
            cos, sin = twice(cosine, block), twice(sine, block)
            front, behind = turn(dq[:HALF], dq[HALF:], cos, -sin)
            for h in range(2):
                cut = slice(h * QUARTER, (h + 1) * QUARTER)
                base = (2 * group + h) * HD
                dq_ref[pl.ds(base, HALF), lanes] = front[:, cut].astype(BF16)
                dq_ref[pl.ds(base + HALF, HALF), lanes] = behind[:, cut].astype(BF16)
        for i, ref in enumerate((down_ref, doth_ref)):
            for half in range(2):
                lanes = pl.ds(half * QUARTER, QUARTER)
                rows = group * 2 * HD
                ref[pl.ds(rows, HD), lanes] = (dks[2 * i + half] * SCALE).astype(ref.dtype)
                ref[pl.ds(rows + HD, HD), lanes] = dvs[2 * i + half].astype(ref.dtype)


def attend_back(spot, pieces, wown, woth, queries, own, other, outs, lse, place, low, cosine, sine):
    weights = pl.BlockSpec((SHARD, WIDE), lambda i, s: (s[2], 0))
    flat = whole((SHARD, TOKENS))
    row = whole((1, TOKENS))
    return pl.pallas_call(
        backward_kernel,
        out_shape=(
            shape((TOKENS, D), BF16),
            shape((SHARD, TOKENS), BF16),
            shape((SHARD, TOKENS), F32),
            shape((SHARD, TOKENS), BF16),
        ),
        grid_spec=pltpu.PrefetchScalarGridSpec(
            num_scalar_prefetch=1,
            grid=(1,),
            in_specs=[whole((CHUNK, D))] * 4
            + [weights, weights, flat, flat, flat, flat, whole((4, TOKENS)), row, row]
            + [whole((HALF, TOKENS))] * 2,
            out_specs=(whole((TOKENS, D)), flat, flat, flat),
            scratch_shapes=[pltpu.VMEM((SHARD, TOKENS), BF16)],
        ),
        compiler_params=params(60),
        cost_estimate=cost(10 * 4 * HD * QUARTER * QUARTER * 6 + 2 * TOKENS * D * SHARD, 8 << 20),
        name="attend_backward",
    )(spot, *pieces, wown, woth, queries, own, other, outs, lse, place, low, cosine, sine)


def input_kernel(
    spot, dq, mine, got, cosine, sine, own, oth, x, inv, here, send, o0, o1, o2, o3, part, acc, raw
):
    raw[:SHARD] = dq[...]
    total = mine[...] + got[...].astype(F32)
    cos, sin = cosine[...], -sine[...]
    for group in range(2):
        base = group * 2 * HD
        front, behind = turn(total[base : base + HALF], total[base + HALF : base + HD], cos, sin)
        raw[pl.ds(SHARD + base, HALF)] = front.astype(BF16)
        raw[pl.ds(SHARD + base + HALF, HALF)] = behind.astype(BF16)
        raw[pl.ds(SHARD + base + HD, HD)] = total[base + HD : base + 2 * HD].astype(BF16)
    for j in range(2):
        span = pl.ds(j * (SHARD // 2), SHARD // 2)
        here[span] = raw[half_of(spot[3], j * SHARD)]
        send[span] = raw[half_of(1 - spot[3], j * SHARD)]
    grads = raw[...].T
    for j, w in enumerate((own, oth)):
        lanes = pl.ds(j * WIDE, WIDE)
        value = dot(grads, w[...], NN)
        acc[:, lanes] = value.astype(BF16)
        part[:, lanes] = (value * (x[:, lanes].astype(F32) * inv[...])).sum(axis=0, keepdims=True)
    cut_pieces(spot, acc, (o0, o1, o2, o3))


def input_grad(spot, dq, mine, got, cosine, sine, own, oth, x, inv):
    outs = (
        *(shape((SHARD, TOKENS), BF16),) * 2,
        *(shape((2, QUARTER, SHARD), BF16),) * 4,
        shape((1, D), F32),
    )
    inputs = (dq, mine, got, cosine, sine, own, oth, x, inv)
    scratch = [pltpu.VMEM((TOKENS, D), BF16), pltpu.VMEM((WIDE, TOKENS), BF16)]
    return stage(input_kernel, "input_grad", spot, inputs, outs, 2 * TOKENS * D * WIDE, scratch)


def units_grad_kernel(spot, mine, got, h, h_oth, top, top_oth, left, *rest):
    rights, stash = rest[:-1], rest[-1]
    half = left.shape[1] // 3
    for k in range(3):
        columns, columns_oth = (top, top_oth) if k == 2 else (h, h_oth)
        for j, out in enumerate((left, stash)):
            here, there = pl.ds(j * WIDE, WIDE), pl.ds((1 - j) * WIDE, WIDE)
            value = dot(mine[k], columns[:, here], NN) + dot(got[k], columns_oth[:, there], NN)
            out[:, pl.ds(k * half, half)] = value.astype(BF16).reshape(-1, half, WIDE)
    nz = len(rights)
    count = left.shape[0] // nz
    for j, right in enumerate(rights):
        for i in range(count):
            right[pl.program_id(0) * count + i] = stash[i * nz + jnp.bitwise_xor(spot[9], j)]


def units_grad(spot, mine, got, h, h_oth, top, top_oth, nx, nz):
    steps = 2
    ndp = nx * nz
    total = mine.shape[1]
    rows = 3 * total // ndp
    block = pl.BlockSpec((3, total // steps, TOKENS), lambda i, s: (0, i, 0))
    return pl.pallas_call(
        units_grad_kernel,
        out_shape=(shape((ndp, rows, WIDE), BF16),) + (shape((nx, rows, WIDE), BF16),) * nz,
        grid_spec=pltpu.PrefetchScalarGridSpec(
            num_scalar_prefetch=1,
            grid=(steps,),
            in_specs=[block, block] + [whole((TOKENS, D))] * 4,
            out_specs=(pl.BlockSpec((ndp // steps, rows, WIDE), lambda i, s: (i, 0, 0)),)
            + (whole((nx, rows, WIDE)),) * nz,
            scratch_shapes=[pltpu.VMEM((ndp // steps, rows, WIDE), BF16)],
        ),
        compiler_params=params(60),
        cost_estimate=cost(12 * TOKENS * D * total, 12 << 20),
        name="units_grad",
    )(spot, mine, got, h, h_oth, top, top_oth)


def heads_grad_kernel(mine, got, heads, heads_got, h, h_oth, rows, rows_oth, gain1, gain2, out):
    count = 3 * SHARD // 2
    sets = ((mine, got, h, h_oth), (heads, heads_got, rows, rows_oth))
    for j in range(2):
        here, there = pl.ds(j * WIDE, WIDE), pl.ds((1 - j) * WIDE, WIDE)
        first = 0
        for left, left_got, right, right_oth in sets:
            value = dot(left[...], right[:, here], NN) + dot(left_got[...], right_oth[:, there], NN)
            out[pl.ds(first, left.shape[0]), here] = value.astype(BF16)
            first += left.shape[0]
    out[count:] = jnp.zeros((out.shape[0] - count, D), BF16)
    which = lax.broadcasted_iota(jnp.int32, (16, D), 0)
    value = jnp.where(which == 0, gain1[...], jnp.where(which == 1, gain2[...], 0.0))
    out[pl.ds(count, 16)] = value.astype(BF16)


def heads_grad(spot, *inputs):
    outs = (shape((640, D), BF16),)
    kernel = lambda spot, *refs: heads_grad_kernel(*refs)
    return stage(kernel, "heads_grad", spot, inputs, outs, 6 * TOKENS * D * SHARD)[0]


def fold_first_kernel(spot, left, *refs, nx, nz):
    rights, out, outs = refs[:nz], refs[nz], refs[nz + 1 :]
    total = left[:nz].astype(F32)
    for i in range(1, nx):
        total = total + left[i * nz : (i + 1) * nz].astype(F32)
    out[...] = total.astype(BF16)
    for k in range(nx):
        place = jnp.bitwise_xor(spot[8], k)
        total = rights[0][place].astype(F32)
        for right in rights[1:]:
            total = total + right[place].astype(F32)
        outs[k][...] = total.astype(BF16)


def fold_first(spot, left, rights, nx):
    nz = len(rights)
    dims = left.shape[1:]
    outs = (shape((nz, *dims), BF16),) + (shape(dims, BF16),) * nx
    kernel = functools.partial(fold_first_kernel, nx=nx, nz=nz)
    return stage(kernel, "fold_first", spot, (left, *rights), outs, 0)


def fold_last_kernel(spot, left, *refs):
    rights, keep, send = refs[:-2], refs[-2], refs[-1]
    total = left[0].astype(F32)
    for i in range(1, left.shape[0]):
        total = total + left[i].astype(F32)
    other = rights[0][...].astype(F32)
    for right in rights[1:]:
        other = other + right[...].astype(F32)
    for j, value in enumerate((total.astype(BF16), other.astype(BF16))):
        low, high = value[:, :SHARD], value[:, SHARD:]

        @pl.when(spot[1] == 0)
        def _():
            keep[j], send[j] = low, high

        @pl.when(spot[1] == 1)
        def _():
            keep[j], send[j] = high, low


def fold_last(spot, left, rights):
    outs = (shape((2, left.shape[1], SHARD), BF16),) * 2
    return stage(fold_last_kernel, "fold_last", spot, (left, *rights), outs, 0)


def fold_kernel(spot, value, keep, send):
    total = value[0].astype(F32)
    for i in range(1, value.shape[0]):
        total = total + value[i].astype(F32)
    total = total.astype(BF16)
    for j in range(2):
        low = total[:, j * WIDE : j * WIDE + SHARD]
        high = total[:, j * WIDE + SHARD : (j + 1) * WIDE]

        @pl.when(spot[1] == 0)
        def _():
            keep[j], send[j] = low, high

        @pl.when(spot[1] == 1)
        def _():
            keep[j], send[j] = high, low


def fold(spot, value):
    outs = (shape((2, value.shape[1], SHARD), BF16),) * 2
    return stage(fold_kernel, "fold", spot, (value,), outs, 0)


def finish_units_kernel(spot, value, gate, up, lower, both):
    half = both.shape[0] // 4
    for j in range(value.shape[0]):
        span = pl.ds(j * 4 * half, 4 * half)
        for i, out in enumerate((gate, up, lower)):
            for place in range(4):
                low = jnp.bitwise_xor(spot[1], place % 2)
                core = jnp.bitwise_xor(spot[3], place // 2)
                rows = pl.ds(pl.multiple_of((2 * low + core) * half, half), half)
                both[rows] = value[j, place, pl.ds(i * half, half)]
            if i < 2:
                out[:, span] = both[...].astype(F32).T
            else:
                out[span] = both[...].astype(F32)


def finish_units(spot, value, steps):
    ndp = value.shape[0]
    half = value.shape[2] // 3
    cols = 4 * half * ndp // steps
    across = pl.BlockSpec((SHARD, cols), lambda i, s: (0, i))
    return pl.pallas_call(
        finish_units_kernel,
        out_shape=(shape((SHARD, cols * steps), F32),) * 2 + (shape((cols * steps, SHARD), F32),),
        grid_spec=pltpu.PrefetchScalarGridSpec(
            num_scalar_prefetch=1,
            grid=(steps,),
            in_specs=[pl.BlockSpec((ndp // steps, *value.shape[1:]), lambda i, s: (i, 0, 0, 0))],
            out_specs=(across, across, pl.BlockSpec((cols, SHARD), lambda i, s: (i, 0))),
            scratch_shapes=[pltpu.VMEM((4 * half, SHARD), BF16)],
        ),
        compiler_params=params(60),
        cost_estimate=cost(0, 14 << 20),
        name="finish_units",
    )(spot, value)


def finish_heads_kernel(spot, value, query, keyval, out, gains, part, full):
    count = value.shape[2]
    half = SHARD // 2
    total = jnp.zeros((8, SHARD), F32)
    for place in range(4):
        for i in range(value.shape[0]):
            part[pl.ds(i * count, count)] = value[i, place].astype(F32)
        low = jnp.bitwise_xor(spot[1], place % 2)
        core = jnp.bitwise_xor(spot[3], place // 2)
        rows = pl.ds(pl.multiple_of((2 * low + core) * half, half), half)
        for k in range(2):
            full[k, rows] = part[pl.ds(k * half, half)]
        out[rows] = part[pl.ds(2 * half, half)]
        total = total + part[pl.ds(3 * half, 8)]
    query[...] = full[0].T
    keyval[...] = full[1].T
    gains[...] = total


def finish_heads(spot, value):
    dims = ((SHARD, WIDE), (SHARD, WIDE), (WIDE, SHARD), (8, SHARD))
    scratch = [
        pltpu.VMEM((value.shape[0] * value.shape[2], SHARD), F32),
        pltpu.VMEM((2, WIDE, SHARD), F32),
    ]
    outs = tuple(shape(d, F32) for d in dims)
    return stage(finish_heads_kernel, "finish_heads", spot, (value,), outs, 0, scratch)


def body(tokens, gain1, w_query, w_keyval, w_out, gain2, w_gate, w_up, w_down, grad_out, segments):
    core, yh, yl = lax.axis_index("core"), lax.axis_index("yhi"), lax.axis_index("ylo")
    nx, nz = lax.axis_size("x"), lax.axis_size("z")
    dp = lax.axis_index(DP)
    quarter = core ^ yh
    spot = jnp.stack(
        [yh, yl, 2 * yh + yl, core]
        + [place * QUARTER for place in (core, 3 - core, 1 - core, 2 + core)]
        + [lax.axis_index("x"), lax.axis_index("z"), dp]
    ).astype(jnp.int32)

    def pick(first_is_mine, own, other):
        return jnp.where(first_is_mine, own, other), jnp.where(first_is_mine, other, own)

    def halves_of(value):
        own = lax.dynamic_slice_in_dim(value, quarter * QUARTER, QUARTER, 0)
        return own, lax.dynamic_slice_in_dim(value, (1 - quarter) * QUARTER, QUARTER, 0)

    gains = jnp.stack([gain1, gain2])
    gains = jnp.stack([gains, swap(gains, "core")], axis=1)
    gains = jnp.stack(pick(yl == 0, gains, swap(gains, "ylo")), axis=2).reshape(2, 1, D)

    ids = segments[0]
    low_all = jnp.sum((ids[None, :] < ids[:, None]).astype(jnp.int32), axis=1)
    low = jnp.concatenate(
        [
            lax.dynamic_slice_in_dim(low_all, core * QUARTER, QUARTER),
            lax.dynamic_slice_in_dim(low_all, (3 - core) * QUARTER, QUARTER),
        ]
    )
    step = jnp.arange(QUARTER, dtype=jnp.int32)
    place = jnp.concatenate([core * QUARTER + step, (3 - core) * QUARTER + step])
    rates = THETA ** (-jnp.arange(HALF, dtype=F32) * 2.0 / HD)
    angles = rates[:, None] * (place - low).astype(F32)[None, :]
    cosine, sine = jnp.cos(angles), jnp.sin(angles)
    place, low = place[None, :], low[None, :]

    head_mine, head_send, unit_send, out_send = prepare(
        spot, w_query, w_keyval, w_gate, w_up, w_down, w_out, nx * nz
    )
    others = gather_dp(
        jnp.concatenate([swap_y(unit_send, 1), swap_y(out_send, 2), swap_y(out_send, 3)])
    )

    (x_own, x_other), (top_own, top_other) = halves_of(tokens[0]), halves_of(grad_out[0])
    got = swap(jnp.concatenate([x_other, top_other]), "core")
    pieces = peers_y(jnp.concatenate([x_own, got[:QUARTER]]))
    top_pair = jnp.concatenate([top_own, got[QUARTER:]])
    head_got = swap(head_send, "ylo")
    top_pair = jnp.broadcast_to(top_pair[None], (4, *top_pair.shape))
    *pieces, head_got, head_mine, gains, top_pair, cosine, sine, low = together(
        *pieces, head_got, head_mine, gains, top_pair, cosine, sine, low
    )
    head_pieces = (head_mine, head_got, swap(head_mine, "core"), swap(head_got, "core"))

    x, h_one, inv_one, queries, keyval, head_rows, head_rows_oth = project(
        spot, pieces, gains[0], head_pieces, cosine, sine
    )
    keyval_oth = swap(keyval, "core")
    top_pieces = over_y(after(top_pair, head_pieces[3]))
    others = after(others, queries)
    w_o = out_rows(spot, w_out, others)
    w_f = unit_rows(spot, w_gate, w_up, w_down, after(others, w_o))
    top_pieces, w_f, w_o, low, keyval_oth = together(top_pieces, w_f, w_o, low, keyval_oth)
    w_o_oth, w_f_oth = swap(w_o, "core"), swap(w_f, "core")
    heads_t, heads, lse, heads_mine, heads_send = attend(
        spot, queries, keyval, keyval_oth, place, low
    )
    heads_pieces = peers_y(heads)
    mixed, h_two, inv_two = mix(spot, x, heads_pieces, w_o, w_o_oth, gains[1])
    top, act, mine, send, parts = feed(spot, h_two, top_pieces, w_f, w_f_oth)
    parts, h_one_oth = together(over_y(parts), swap(h_one, "core"))

    got, h_two_oth, top_oth = swap(send, "core"), swap(h_two, "core"), swap(top, "core")
    left, *rights = units_grad(spot, mine, got, h_two, h_two_oth, top, top_oth, nx, nz)
    rows, gain2_part = residual(spot, parts, mixed, inv_two, top, gains[1])
    left = lax.all_to_all(left, "x", 0, 0, tiled=True)
    rights = to_peers(rights, "z")

    row_all, dq, dkv, dkv_oth = attend_back(
        spot, peers_y(rows), w_o, w_o_oth, queries, keyval, keyval_oth, heads_t, lse, place, low,
        cosine, sine,
    )
    dq, left, *rights = together(dq, left, *rights)
    left, *rights = fold_first(spot, left, rights, nx)
    left = lax.all_to_all(left, "z", 0, 0, tiled=True)
    rights = to_peers(rights, "x")
    raw, send, *parts, gain1_part = input_grad(
        spot, dq, dkv, swap(dkv_oth, "core"), cosine, sine, head_rows, head_rows_oth, x, inv_one
    )
    got = swap(send, "core")
    parts = to_peers_y(parts)

    sums = jnp.concatenate([gain1_part, gain2_part])
    sums = sums + swap(sums, "yhi")
    raw, got, row_all_oth, heads_got = together(
        raw, got, swap(row_all, "core"), swap(heads_send, "core")
    )
    head_parts = heads_grad(
        spot, raw, got, heads_mine, heads_got, h_one, h_one_oth, row_all, row_all_oth,
        sums[:1], sums[1:],
    )
    head_parts, left, *rights = together(head_parts, left, *rights)
    head_parts = scatter_dp(head_parts.reshape(nx * nz, -1, D))
    keep, send = fold_last(spot, left, rights)
    low_got = swap(send, "ylo")

    def over_cores(keep, got):
        other = swap(jnp.stack([keep[1], got[1]]), "core")
        return jnp.stack([keep[0], got[0], other[0], other[1]])

    unit_parts = gather_dp(over_cores(keep, low_got))
    outs = to_peers_y(down(spot, after(act, keep), w_f, w_f_oth))
    head_parts, *both = together(head_parts, *parts, *outs)
    parts, outs = both[:4], both[4:]
    keep, send = fold(spot, head_parts)
    head_parts = gather_dp_now(over_cores(keep, swap(send, "ylo")))

    got = sum([g.astype(F32) for g in parts])

    def my_block(value):
        return jnp.stack(
            [
                lax.dynamic_slice(value, (yh * QUARTER, j * WIDE + yl * SHARD), (QUARTER, SHARD))
                for j in range(2)
            ]
        )

    def to_home(block):
        return jnp.concatenate(pick(quarter == 0, block[0], swap(block[1], "core")))

    gain = jnp.stack(
        [lax.dynamic_slice(gains[0], (0, j * WIDE + yl * SHARD), (1, SHARD)) for j in range(2)]
    )
    inverse = lax.dynamic_slice_in_dim(inv_one, yh * QUARTER, QUARTER, 0)
    normed = my_block(x).astype(F32) * inverse
    scaled = got * gain
    inner = (scaled * normed).sum(axis=(0, 2))
    inner = (inner + swap(inner, "ylo"))[:, None] / D
    grad_in = to_home(my_block(row_all).astype(F32) + inverse * (scaled - normed * inner))

    output = my_block(mixed) + sum([g.astype(F32) for g in outs])
    output = to_home(output.astype(BF16))

    grad_w_gate, grad_w_up, grad_w_down = finish_units(spot, unit_parts, nx)
    head_parts, grad_w_down = together(head_parts, grad_w_down)
    grad_w_query, grad_w_keyval, grad_w_out, sums = finish_heads(spot, head_parts)
    return (
        output[None],
        grad_in[None],
        sums[0],
        grad_w_query,
        grad_w_keyval,
        grad_w_out,
        sums[1],
        grad_w_gate,
        grad_w_up,
        grad_w_down,
    )


def solution(mesh):
    dp = mesh.shape["dp"]
    side = int(round(dp**0.5))
    fine = Mesh(
        mesh.devices.reshape(side, dp // side, 2, 2, 2), ("x", "z", "ylo", "core", "yhi")
    )
    seq, row, col = DP, ("ylo", "core"), "yhi"
    return jax.shard_map(
        body,
        mesh=fine,
        in_specs=(
            P(seq, col, row),
            P(row),
            P(row, col),
            P(row, col),
            P(col, row),
            P(row),
            P(row, col),
            P(row, col),
            P(col, row),
            P(seq, col, row),
            P(seq, None),
        ),
        out_specs=(
            P(seq, col, row),
            P(seq, col, row),
            P(row),
            P(row, col),
            P(row, col),
            P(col, row),
            P(row),
            P(row, col),
            P(row, col),
            P(col, row),
        ),
        check_vma=False,
    )
```

```python
import functools

import jax
import jax.numpy as jnp
from jax import lax
from jax.experimental import pallas as pl
from jax.experimental.pallas import tpu as pltpu
from jax.sharding import Mesh
from jax.sharding import PartitionSpec as P

D = 1536
HD = 96
HALF = HD // 2
EPS = 1e-05
THETA = 100000.0
NEGATIVE = -1e30
SCALE = HD**-0.5
LOG2E = 1.4426950408889634
F32 = jnp.float32
BF16 = jnp.bfloat16
QUARTER = 256
TOKENS = 2 * QUARTER
CHUNK = 128
WIDE = D // 2
SHARD = D // 4
DP = ("x", "z")

NN = ((1,), (0,))
NT = ((1,), (1,))
TN = ((0,), (0,))


def dot(a, b, dims):
    return lax.dot_general(a, b, (dims, ((), ())), preferred_element_type=F32)


def swap(value, axis, step=1):
    count = lax.axis_size(axis)
    return lax.ppermute(value, axis, [(i, i ^ step) for i in range(count)])


def swap_y(value, k):
    return swap(value, ("ylo", "yhi"), 2 * (k & 1) + (k >> 1))


def peers_y(value):
    return [value] + [swap_y(value, k) for k in (1, 2, 3)]


def to_peers_y(values):
    return [values[0]] + [swap_y(values[k], k) for k in (1, 2, 3)]


def from_peers(value, axis):
    return [value] + [swap(value, axis, k) for k in range(1, lax.axis_size(axis))]


def over_y(value):
    return lax.all_to_all(value, ("yhi", "ylo"), 0, 0, tiled=True)


def gather_y(value):
    return over_y(jnp.broadcast_to(value[None], (4, *value.shape)))


def to_peers(values, axis):
    return [values[0]] + [swap(values[k], axis, k) for k in range(1, lax.axis_size(axis))]


def scatter_dp(value):
    return lax.all_to_all(value, DP, 0, 0, tiled=True)


def gather_dp(value):
    return lax.all_gather(value, DP, axis=0)


def gather_dp_now(value):
    count = lax.axis_size(DP)
    return scatter_dp(jnp.broadcast_to(value[None], (count, *value.shape)))


def together(*values):
    return lax.optimization_barrier(values)


def after(value, *others):
    return lax.optimization_barrier((value, *others))[0]


def shape(dims, dtype):
    return jax.ShapeDtypeStruct(dims, dtype)


def cost(flops, nbytes):
    return pl.CostEstimate(flops=1, bytes_accessed=1, transcendentals=0)


def params(mib=60):
    return pltpu.CompilerParams(vmem_limit_bytes=mib << 20)


def whole(dims):
    return pl.BlockSpec(dims, lambda *_: (0,) * len(dims))


def stage(kernel, name, spot, inputs, outs, flops, scratch=(), mib=60):
    nbytes = sum(v.size * v.dtype.itemsize for v in (*inputs, *outs))
    return pl.pallas_call(
        kernel,
        out_shape=tuple(outs),
        grid_spec=pltpu.PrefetchScalarGridSpec(
            num_scalar_prefetch=1,
            grid=(1,),
            in_specs=[whole(v.shape) for v in inputs],
            out_specs=tuple(whole(v.shape) for v in outs),
            scratch_shapes=scratch,
        ),
        compiler_params=params(mib),
        cost_estimate=cost(flops, nbytes),
        name=name,
    )(spot, *inputs)


def peer(spot, k):
    high = jnp.bitwise_xor(spot[0], k >> 1)
    low = jnp.bitwise_xor(spot[1], k & 1)
    return high, low, 2 * high + low


def place_pieces(spot, pieces, out):
    for k, piece in enumerate(pieces):
        high, low, _ = peer(spot, k)
        rows = pl.ds(pl.multiple_of(high * QUARTER, QUARTER), QUARTER)
        for j in range(2):
            lanes = pl.ds(pl.multiple_of(low * SHARD + j * WIDE, 128), SHARD)
            out[rows, lanes] = piece[pl.ds(j * QUARTER, QUARTER)]


def cut_pieces(spot, value, outs):
    for k, out in enumerate(outs):
        high, low, _ = peer(spot, k)
        rows = pl.ds(pl.multiple_of(high * QUARTER, QUARTER), QUARTER)
        for j in range(2):
            lanes = pl.ds(pl.multiple_of(low * SHARD + j * WIDE, 128), SHARD)
            out[j] = value[rows, lanes].astype(out.dtype)


def turn(front, behind, cosine, sine):
    return front * cosine - behind * sine, behind * cosine + front * sine


def prepare_kernel(
    spot, query, keyval, gate, up, lower, outer, mine, send, units_send, out_send, turned, part
):
    low = spot[1]
    for i, w in enumerate((query, keyval)):
        value = w[...].T
        turned[0, pl.ds(i * SHARD, SHARD)] = value[:SHARD]
        turned[1, pl.ds(i * SHARD, SHARD)] = value[SHARD:]
    mine[...] = turned[low]
    send[...] = turned[1 - low]
    units = part.shape[0] // 2
    for k, value in enumerate((gate[...].T, up[...].T, lower[...])):
        part[...] = value
        units_send[pl.ds(k * units, units)] = part[
            pl.ds(pl.multiple_of((1 - low) * units, 64), units)
        ]
    units_send[3 * units :] = outer[...]
    out_send[...] = outer[...]


def prepare(spot, query, keyval, gate, up, lower, outer, ndp):
    cols = gate.shape[1] // ndp
    across = pl.BlockSpec((SHARD, cols), lambda i, s: (0, s[10]))
    count = WIDE // ndp
    dims = ((WIDE, SHARD), (WIDE, SHARD), (3 * cols // 2 + count, SHARD), (count, SHARD))
    return pl.pallas_call(
        prepare_kernel,
        out_shape=tuple(shape(d, BF16) for d in dims),
        grid_spec=pltpu.PrefetchScalarGridSpec(
            num_scalar_prefetch=1,
            grid=(1,),
            in_specs=[whole(query.shape), whole(keyval.shape), across, across]
            + [pl.BlockSpec((cols, SHARD), lambda i, s: (s[10], 0))]
            + [pl.BlockSpec((count, SHARD), lambda i, s: (s[10], 0))],
            out_specs=tuple(whole(d) for d in dims),
            scratch_shapes=[pltpu.VMEM((2, WIDE, SHARD), BF16), pltpu.VMEM((cols, SHARD), BF16)],
        ),
        compiler_params=params(60),
        cost_estimate=cost(0, 4 << 20),
        name="prepare",
    )(spot, query, keyval, gate, up, lower, outer)


def join_rows(spot, mine, got, out):
    out[:, pl.ds(pl.multiple_of(spot[1] * SHARD, 128), SHARD)] = mine[...]
    out[:, pl.ds(pl.multiple_of((1 - spot[1]) * SHARD, 128), SHARD)] = got[...]


def out_rows_kernel(spot, mine, value, out):
    rows = pl.ds(pl.multiple_of(spot[0] * WIDE, 64), WIDE)
    out[rows, pl.ds(pl.multiple_of(spot[1] * SHARD, 128), SHARD)] = mine[...]
    ndp = value.shape[0]
    count = WIDE // ndp
    base = value.shape[1] - 3 * count
    for i in range(ndp):
        for k in (1, 2, 3):
            high, low, _ = peer(spot, k)
            rows = pl.ds(pl.multiple_of(high * WIDE + i * count, 16), count)
            lanes = pl.ds(pl.multiple_of(low * SHARD, 128), SHARD)
            out[rows, lanes] = value[i, pl.ds(base + (k - 1) * count, count)]


def out_rows(spot, mine, value):
    outs = (shape((D, WIDE), BF16),)
    return stage(out_rows_kernel, "out_rows", spot, (mine, value), outs, 0, mib=60)[0]


def unit_rows_kernel(spot, gate, up, lower, other, out, turned):
    low = spot[1]
    units = out.shape[2]
    for k, value in enumerate((gate[...].T, up[...].T, lower[...])):
        turned[k] = value
    for j in range(out.shape[0]):
        for k in range(3):
            rows = pl.ds(pl.multiple_of((2 * j + low) * units, 64), units)
            out[j, k, :, pl.ds(pl.multiple_of(low * SHARD, 128), SHARD)] = turned[k, rows]
            out[j, k, :, pl.ds(pl.multiple_of((1 - low) * SHARD, 128), SHARD)] = other[
                j, pl.ds(k * units, units)
            ]


def unit_rows(spot, gate, up, lower, other, steps=4):
    ndp, rows, _ = other.shape
    cols = gate.shape[1] // steps
    units = gate.shape[1] // (2 * ndp)
    across = pl.BlockSpec((SHARD, cols), lambda i, s: (0, i))
    dims = (ndp, 3, units, WIDE)
    return pl.pallas_call(
        unit_rows_kernel,
        out_shape=shape(dims, BF16),
        grid_spec=pltpu.PrefetchScalarGridSpec(
            num_scalar_prefetch=1,
            grid=(steps,),
            in_specs=[across, across, pl.BlockSpec((cols, SHARD), lambda i, s: (i, 0))]
            + [pl.BlockSpec((ndp // steps, rows, SHARD), lambda i, s: (i, 0, 0))],
            out_specs=pl.BlockSpec((ndp // steps, *dims[1:]), lambda i, s: (i, 0, 0, 0)),
            scratch_shapes=[pltpu.VMEM((3, cols, SHARD), BF16)],
        ),
        compiler_params=params(60),
        cost_estimate=cost(0, 12 << 20),
        name="unit_rows",
    )(spot, gate, up, lower, other)


def qkv_kernel(
    spot, p0, p1, p2, p3, gain, mine, got, mine_oth, got_oth, cosine, sine,
    x, h, inv, q, kv, own, oth, block,
):
    place_pieces(spot, (p0, p1, p2, p3), x)
    cut_pieces(spot, x, (block,))
    join_rows(spot, mine, got, own)
    join_rows(spot, mine_oth, got_oth, oth)
    for i in range(4):
        rows = pl.ds(i * CHUNK, CHUNK)
        value = x[rows].astype(F32)
        inverse = lax.rsqrt((value * value).sum(axis=-1, keepdims=True) / D + EPS)
        inv[rows] = inverse
        h[rows] = (value * inverse * gain[...]).astype(BF16)
    cos, sin = cosine[...], sine[...]
    for i in range(4):
        rows = pl.ds(i * 2 * HD, 2 * HD)
        raw = dot(own[rows], h[:, :WIDE], NT) + dot(oth[rows], h[:, WIDE:], NT)
        out, base = (q, i * 2 * HD) if i < 2 else (kv, (i - 2) * 2 * HD)
        for head in range(2):
            front, behind = raw[head * HD : head * HD + HALF], raw[head * HD + HALF : (head + 1) * HD]
            if i < 2 or head == 0:
                front, behind = turn(front, behind, cos, sin)
            out[pl.ds(base + head * HD, HALF)] = front.astype(BF16)
            out[pl.ds(base + head * HD + HALF, HALF)] = behind.astype(BF16)


def project(spot, pieces, gain, rows, cosine, sine):
    outs = (
        shape((TOKENS, D), BF16),
        shape((TOKENS, D), BF16),
        shape((TOKENS, 1), F32),
        shape((SHARD, TOKENS), BF16),
        shape((SHARD, TOKENS), BF16),
        shape((WIDE, WIDE), BF16),
        shape((WIDE, WIDE), BF16),
        shape((2, QUARTER, SHARD), BF16),
    )
    inputs = (*pieces, gain, *rows, cosine, sine)
    return stage(qkv_kernel, "project", spot, inputs, outs, 2 * TOKENS * D * WIDE, mib=60)


def key_blocks(block):
    return (0, 2) if block == 0 else (0, 1, 2, 3)


def allowed_keys(spot, key, place, low):
    at = spot[4 + key] + lax.broadcasted_iota(jnp.int32, (QUARTER, place.shape[1]), 0)
    return (at >= low) & (at <= place)


def two_heads(ref, group, block):
    lanes = pl.ds(block * QUARTER, QUARTER)
    return jnp.concatenate(
        [ref[pl.ds((2 * group + h) * HD, HD), lanes] for h in range(2)], axis=1
    )


def twice(ref, block):
    row = ref[:, pl.ds(block * QUARTER, QUARTER)]
    return jnp.concatenate([row, row], axis=1)


def half_of(core, first=0):
    return pl.ds(pl.multiple_of(first + core * (SHARD // 2), 64), SHARD // 2)


def forward_kernel(
    spot, q_ref, own_ref, oth_ref, place_ref, low_ref, outt_ref, out_ref, lse_ref, mine_ref, send_ref
):
    factor = SCALE * LOG2E
    for group in range(2):
        keys = []
        vals = []
        for ref in (own_ref, oth_ref):
            for half in range(2):
                lanes = pl.ds(half * QUARTER, QUARTER)
                keys.append(ref[pl.ds(group * 2 * HD, HD), lanes].T)
                vals.append(ref[pl.ds(group * 2 * HD + HD, HD), lanes])
        for block in range(2):
            q = two_heads(q_ref, group, block)
            place, low = twice(place_ref, block), twice(low_ref, block)
            scores = []
            for key in key_blocks(block):
                s = dot(keys[key], q, NN)
                scores.append(jnp.where(allowed_keys(spot, key, place, low), s, NEGATIVE))
            peak = scores[0].max(axis=0, keepdims=True)
            for s in scores[1:]:
                peak = jnp.maximum(peak, s.max(axis=0, keepdims=True))
            shift = peak * factor
            total = jnp.zeros_like(peak)
            acc = jnp.zeros((HD, 2 * QUARTER), F32)
            for key, s in zip(key_blocks(block), scores):
                p = jnp.exp2(s * factor - shift)
                total = total + p.sum(axis=0, keepdims=True)
                acc = acc + dot(vals[key], p.astype(BF16), NN)
            acc = (acc / total).astype(BF16)
            lse = shift + jnp.log2(total)
            for h in range(2):
                lanes = pl.ds(block * QUARTER, QUARTER)
                cut = slice(h * QUARTER, (h + 1) * QUARTER)
                outt_ref[pl.ds((2 * group + h) * HD, HD), lanes] = acc[:, cut]
                lse_ref[pl.ds(2 * group + h, 1), lanes] = lse[:, cut]
    out_ref[...] = outt_ref[...].T
    for ref, core in ((mine_ref, spot[3]), (send_ref, 1 - spot[3])):
        ref[...] = outt_ref[half_of(core)]


def attend(spot, queries, own, other, place, low):
    outs = (
        shape((SHARD, TOKENS), BF16),
        shape((TOKENS, SHARD), BF16),
        shape((4, TOKENS), F32),
        *(shape((SHARD // 2, TOKENS), BF16),) * 2,
    )
    inputs = (queries, own, other, place, low)
    flops = 4 * 4 * HD * QUARTER * QUARTER * 6
    return stage(forward_kernel, "attend_forward", spot, inputs, outs, flops)


def mix_kernel(spot, x, h0, h1, h2, h3, own, oth, gain, mine, h, inv, block, heads, mixed):
    for k, piece in enumerate((h0, h1, h2, h3)):
        _, _, y = peer(spot, k)
        heads[:, pl.ds(pl.multiple_of(y * SHARD, 128), SHARD)] = piece[...]
    for i in range(2):
        rows = pl.ds(i * QUARTER, QUARTER)
        square = jnp.zeros((QUARTER, 1), F32)
        for j, w in enumerate((own, oth)):
            lanes = pl.ds(j * WIDE, WIDE)
            value = x[rows, lanes].astype(F32)
            value = value + dot(heads[rows], w[...], NN)
            mixed[rows, lanes] = value
            square = square + (value * value).sum(axis=-1, keepdims=True)
        inverse = lax.rsqrt(square / D + EPS)
        inv[rows] = inverse
        h[rows] = (mixed[rows] * inverse * gain[...]).astype(BF16)
    cut_pieces(spot, mixed, (block,))
    mine[...] = mixed[pl.ds(pl.multiple_of(spot[2] * CHUNK, CHUNK), CHUNK)]


def mix(spot, x, pieces, own, oth, gain):
    outs = (
        shape((CHUNK, D), F32),
        shape((TOKENS, D), BF16),
        shape((TOKENS, 1), F32),
        shape((2, QUARTER, SHARD), F32),
    )
    inputs = (x, *pieces, own, oth, gain)
    scratch = [pltpu.VMEM((TOKENS, D), BF16), pltpu.VMEM((TOKENS, D), F32)]
    return stage(mix_kernel, "mix", spot, inputs, outs, 2 * TOKENS * D * D, scratch)


def units_of(ref, k):
    return ref[:, k].reshape(-1, WIDE)


def feed_kernel(
    spot, h, pieces, own, oth, top, act, mine, others, dh, acc, stash
):
    step = pl.program_id(0)

    @pl.when(step == 0)
    def _():
        for y in range(4):
            rows = pl.ds((y // 2) * QUARTER, QUARTER)
            for j in range(2):
                lanes = pl.ds((y % 2) * SHARD + j * WIDE, SHARD)
                top[rows, lanes] = pieces[y, pl.ds(j * QUARTER, QUARTER)]
        acc[...] = jnp.zeros_like(acc)

    def hidden(k, columns):
        return dot(units_of(own, k), columns[:, :WIDE], NT) + dot(
            units_of(oth, k), columns[:, WIDE:], NT
        )

    gate, up, grad = hidden(0, h), hidden(1, h), hidden(2, top)
    sigma = jax.nn.sigmoid(gate)
    silu = gate * sigma
    grad_gate = (grad * up * sigma * (1.0 + gate * (1.0 - sigma))).astype(BF16)
    grad_up = (grad * silu).astype(BF16)
    value = (silu * up).astype(BF16)
    act[...] = value
    half = stash.shape[1] // 2
    for k, v in enumerate((grad_gate, grad_up, value)):
        stash[...] = v.reshape(stash.shape)
        for out, core in ((mine, spot[3]), (others, 1 - spot[3])):
            rows = pl.ds(pl.multiple_of(core * half, half), half)
            out[k] = stash[:, rows].reshape(out.shape[1:])
    grad_gate, grad_up = grad_gate.T, grad_up.T
    for j, w in enumerate((own, oth)):
        lanes = pl.ds(j * WIDE, WIDE)
        acc[:, lanes] += dot(grad_gate, units_of(w, 0), NN) + dot(grad_up, units_of(w, 1), NN)

    @pl.when(step == pl.num_programs(0) - 1)
    def _():
        for y in range(4):
            dh[y] = acc[pl.ds(y * CHUNK, CHUNK)].astype(BF16)


def feed(spot, h, pieces, own, oth):
    steps = 4
    ndp, _, units, _ = own.shape
    total = ndp * units
    weights = pl.BlockSpec((ndp // steps, *own.shape[1:]), lambda i, s: (i, 0, 0, 0))
    block = pl.BlockSpec((total // steps, TOKENS), lambda i, s: (i, 0))
    half = pl.BlockSpec((3, total // (2 * steps), TOKENS), lambda i, s: (0, i, 0))
    return pl.pallas_call(
        feed_kernel,
        out_shape=(
            shape((TOKENS, D), BF16),
            shape((total, TOKENS), BF16),
            *(shape((3, total // 2, TOKENS), BF16),) * 2,
            shape((4, CHUNK, D), BF16),
        ),
        grid_spec=pltpu.PrefetchScalarGridSpec(
            num_scalar_prefetch=1,
            grid=(steps,),
            in_specs=[whole((TOKENS, D)), whole(pieces.shape), weights, weights],
            out_specs=(whole((TOKENS, D)), block, half, half, whole((4, CHUNK, D))),
            scratch_shapes=[
                pltpu.VMEM((TOKENS, D), F32),
                pltpu.VMEM((ndp // steps, units, TOKENS), BF16),
            ],
        ),
        compiler_params=params(60),
        cost_estimate=cost(10 * TOKENS * D * total, 20 << 20),
        name="feed",
    )(spot, h, pieces, own, oth)


def down_kernel(spot, act, own, oth, o0, o1, o2, o3, acc):
    step = pl.program_id(0)

    @pl.when(step == 0)
    def _():
        acc[...] = jnp.zeros_like(acc)

    hidden = act[...].T
    for j, w in enumerate((own, oth)):
        acc[:, pl.ds(j * WIDE, WIDE)] += dot(hidden, w[...].reshape(-1, WIDE), NN)

    @pl.when(step == pl.num_programs(0) - 1)
    def _():
        cut_pieces(spot, acc, (o0, o1, o2, o3))


def down(spot, act, own, oth):
    steps = 4
    group = own.shape[0] // steps
    rows = act.shape[0] // steps
    weights = pl.BlockSpec((group, 1, *own.shape[2:]), lambda i, _: (i, 2, 0, 0))
    return pl.pallas_call(
        down_kernel,
        out_shape=(shape((2, QUARTER, SHARD), BF16),) * 4,
        grid_spec=pltpu.PrefetchScalarGridSpec(
            num_scalar_prefetch=1,
            grid=(steps,),
            in_specs=[pl.BlockSpec((rows, TOKENS), lambda i, _: (i, 0)), weights, weights],
            out_specs=(whole((2, QUARTER, SHARD)),) * 4,
            scratch_shapes=[pltpu.VMEM((TOKENS, D), F32)],
        ),
        compiler_params=params(60),
        cost_estimate=cost(2 * TOKENS * D * act.shape[0], 8 << 20),
        name="down",
    )(spot, act, own, oth)


def residual_kernel(spot, pieces, mixed, inv, top, gain, out, part):
    grad = pieces[0].astype(F32)
    for y in range(1, 4):
        grad = grad + pieces[y].astype(F32)
    inverse = inv[...]
    normed = mixed[...] * inverse
    part[...] = (grad * normed).sum(axis=0, keepdims=True)
    scaled = grad * gain[...]
    inner = (scaled * normed).sum(axis=-1, keepdims=True) / D
    out[...] = (top[...].astype(F32) + inverse * (scaled - normed * inner)).astype(BF16)


def residual(spot, pieces, mixed, inv, top, gain):
    mine = lambda width: pl.BlockSpec((CHUNK, width), lambda i, s: (2 * s[0] + s[1], 0))
    return pl.pallas_call(
        residual_kernel,
        out_shape=(shape((CHUNK, D), BF16), shape((1, D), F32)),
        grid_spec=pltpu.PrefetchScalarGridSpec(
            num_scalar_prefetch=1,
            grid=(1,),
            in_specs=[whole((4, CHUNK, D)), whole((CHUNK, D)), mine(1), mine(D), whole((1, D))],
            out_specs=(whole((CHUNK, D)), whole((1, D))),
        ),
        compiler_params=params(60),
        cost_estimate=cost(CHUNK * D * 20, 4 << 20),
        name="residual",
    )(spot, pieces, mixed, inv, top, gain)


def backward_kernel(
    spot, r0, r1, r2, r3, wown, woth, q_ref, own_ref, oth_ref, o_ref, lse_ref, place_ref, low_ref,
    cosine, sine, rows_ref, dq_ref, down_ref, doth_ref, block_ref, do_ref,
):
    for k, piece in enumerate((r0, r1, r2, r3)):
        _, _, y = peer(spot, k)
        rows_ref[pl.ds(pl.multiple_of(y * CHUNK, CHUNK), CHUNK)] = piece[...]
    cut_pieces(spot, rows_ref, (block_ref,))
    do_ref[...] = (
        dot(wown[...], rows_ref[:, :WIDE], NT) + dot(woth[...], rows_ref[:, WIDE:], NT)
    ).astype(BF16)
    factor = SCALE * LOG2E
    for group in range(2):
        keys, vals, keyst = [], [], []
        for ref in (own_ref, oth_ref):
            for half in range(2):
                lanes = pl.ds(half * QUARTER, QUARTER)
                kt = ref[pl.ds(group * 2 * HD, HD), lanes]
                keyst.append(kt)
                keys.append(kt.T)
                vals.append(ref[pl.ds(group * 2 * HD + HD, HD), lanes].T)
        dks = [jnp.zeros((HD, QUARTER), F32) for _ in range(4)]
        dvs = [jnp.zeros((HD, QUARTER), F32) for _ in range(4)]
        for block in range(2):
            lanes = pl.ds(block * QUARTER, QUARTER)
            q = two_heads(q_ref, group, block)
            do = two_heads(do_ref, group, block)
            o = two_heads(o_ref, group, block)
            place, low = twice(place_ref, block), twice(low_ref, block)
            lse = jnp.concatenate(
                [lse_ref[pl.ds(2 * group + h, 1), lanes] for h in range(2)], axis=1
            )
            delta = (do.astype(F32) * o.astype(F32)).sum(axis=0, keepdims=True)
            dq = jnp.zeros((HD, 2 * QUARTER), F32)
            for key in key_blocks(block):
                s = dot(keys[key], q, NN)
                p = jnp.exp2(s * factor - lse)
                p = jnp.where(allowed_keys(spot, key, place, low), p, 0.0)
                dp = dot(vals[key], do, NN)
                ds = (p * (dp - delta)).astype(BF16)
                dvs[key] = dvs[key] + dot(do, p.astype(BF16), NT)
                dks[key] = dks[key] + dot(q, ds, NT)
                dq = dq + dot(keyst[key], ds, NN)
            dq = dq * SCALE
            cos, sin = twice(cosine, block), twice(sine, block)
            front, behind = turn(dq[:HALF], dq[HALF:], cos, -sin)
            for h in range(2):
                cut = slice(h * QUARTER, (h + 1) * QUARTER)
                base = (2 * group + h) * HD
                dq_ref[pl.ds(base, HALF), lanes] = front[:, cut].astype(BF16)
                dq_ref[pl.ds(base + HALF, HALF), lanes] = behind[:, cut].astype(BF16)
        for i, ref in enumerate((down_ref, doth_ref)):
            for half in range(2):
                lanes = pl.ds(half * QUARTER, QUARTER)
                rows = group * 2 * HD
                ref[pl.ds(rows, HD), lanes] = (dks[2 * i + half] * SCALE).astype(ref.dtype)
                ref[pl.ds(rows + HD, HD), lanes] = dvs[2 * i + half].astype(ref.dtype)


def attend_back(spot, pieces, wown, woth, queries, own, other, outs, lse, place, low, cosine, sine):
    weights = pl.BlockSpec((SHARD, WIDE), lambda i, s: (s[2], 0))
    flat = whole((SHARD, TOKENS))
    row = whole((1, TOKENS))
    return pl.pallas_call(
        backward_kernel,
        out_shape=(
            shape((TOKENS, D), BF16),
            shape((SHARD, TOKENS), BF16),
            shape((SHARD, TOKENS), F32),
            shape((SHARD, TOKENS), BF16),
            shape((2, QUARTER, SHARD), BF16),
        ),
        grid_spec=pltpu.PrefetchScalarGridSpec(
            num_scalar_prefetch=1,
            grid=(1,),
            in_specs=[whole((CHUNK, D))] * 4
            + [weights, weights, flat, flat, flat, flat, whole((4, TOKENS)), row, row]
            + [whole((HALF, TOKENS))] * 2,
            out_specs=(whole((TOKENS, D)), flat, flat, flat, whole((2, QUARTER, SHARD))),
            scratch_shapes=[pltpu.VMEM((SHARD, TOKENS), BF16)],
        ),
        compiler_params=params(60),
        cost_estimate=cost(10 * 4 * HD * QUARTER * QUARTER * 6 + 2 * TOKENS * D * SHARD, 8 << 20),
        name="attend_backward",
    )(spot, *pieces, wown, woth, queries, own, other, outs, lse, place, low, cosine, sine)


def input_kernel(
    spot, dq, mine, got, cosine, sine, own, oth, x, inv, here, send, o0, o1, o2, o3, part, acc, raw
):
    raw[:SHARD] = dq[...]
    total = mine[...] + got[...].astype(F32)
    cos, sin = cosine[...], -sine[...]
    for group in range(2):
        base = group * 2 * HD
        front, behind = turn(total[base : base + HALF], total[base + HALF : base + HD], cos, sin)
        raw[pl.ds(SHARD + base, HALF)] = front.astype(BF16)
        raw[pl.ds(SHARD + base + HALF, HALF)] = behind.astype(BF16)
        raw[pl.ds(SHARD + base + HD, HD)] = total[base + HD : base + 2 * HD].astype(BF16)
    for j in range(2):
        span = pl.ds(j * (SHARD // 2), SHARD // 2)
        here[span] = raw[half_of(spot[3], j * SHARD)]
        send[span] = raw[half_of(1 - spot[3], j * SHARD)]
    grads = raw[...].T
    for j, w in enumerate((own, oth)):
        lanes = pl.ds(j * WIDE, WIDE)
        value = dot(grads, w[...], NN)
        acc[:, lanes] = value.astype(BF16)
        part[:, lanes] = (value * (x[:, lanes].astype(F32) * inv[...])).sum(axis=0, keepdims=True)
    cut_pieces(spot, acc, (o0, o1, o2, o3))


def input_grad(spot, dq, mine, got, cosine, sine, own, oth, x, inv):
    outs = (
        *(shape((SHARD, TOKENS), BF16),) * 2,
        *(shape((2, QUARTER, SHARD), BF16),) * 4,
        shape((1, D), F32),
    )
    inputs = (dq, mine, got, cosine, sine, own, oth, x, inv)
    scratch = [pltpu.VMEM((TOKENS, D), BF16), pltpu.VMEM((WIDE, TOKENS), BF16)]
    return stage(input_kernel, "input_grad", spot, inputs, outs, 2 * TOKENS * D * WIDE, scratch)


def units_grad_kernel(spot, mine, got, h, h_oth, top, top_oth, left, *rest):
    rights, stash = rest[:-1], rest[-1]
    half = left.shape[1] // 3
    for k in range(3):
        columns, columns_oth = (top, top_oth) if k == 2 else (h, h_oth)
        for j, out in enumerate((left, stash)):
            here, there = pl.ds(j * WIDE, WIDE), pl.ds((1 - j) * WIDE, WIDE)
            value = dot(mine[k], columns[:, here], NN) + dot(got[k], columns_oth[:, there], NN)
            out[:, pl.ds(k * half, half)] = value.astype(BF16).reshape(-1, half, WIDE)
    nz = len(rights)
    count = left.shape[0] // nz
    for j, right in enumerate(rights):
        for i in range(count):
            right[pl.program_id(0) * count + i] = stash[i * nz + jnp.bitwise_xor(spot[9], j)]


def units_grad(spot, mine, got, h, h_oth, top, top_oth, nx, nz):
    steps = 2
    ndp = nx * nz
    total = mine.shape[1]
    rows = 3 * total // ndp
    block = pl.BlockSpec((3, total // steps, TOKENS), lambda i, s: (0, i, 0))
    return pl.pallas_call(
        units_grad_kernel,
        out_shape=(shape((ndp, rows, WIDE), BF16),) + (shape((nx, rows, WIDE), BF16),) * nz,
        grid_spec=pltpu.PrefetchScalarGridSpec(
            num_scalar_prefetch=1,
            grid=(steps,),
            in_specs=[block, block] + [whole((TOKENS, D))] * 4,
            out_specs=(pl.BlockSpec((ndp // steps, rows, WIDE), lambda i, s: (i, 0, 0)),)
            + (whole((nx, rows, WIDE)),) * nz,
            scratch_shapes=[pltpu.VMEM((ndp // steps, rows, WIDE), BF16)],
        ),
        compiler_params=params(60),
        cost_estimate=cost(12 * TOKENS * D * total, 12 << 20),
        name="units_grad",
    )(spot, mine, got, h, h_oth, top, top_oth)


def heads_grad_kernel(mine, got, heads, heads_got, h, h_oth, rows, rows_oth, gain1, gain2, out):
    count = 3 * SHARD // 2
    first = 0
    for left, left_got, right, right_oth in (
        (mine, got, h, h_oth),
        (heads, heads_got, rows, rows_oth),
    ):
        value = dot(left[...], right[...], NN) + dot(left_got[...], right_oth[...], NN)
        out[pl.ds(first, left.shape[0])] = value.astype(BF16)
        first += left.shape[0]
    out[count:] = jnp.zeros((out.shape[0] - count, WIDE), BF16)
    which = lax.broadcasted_iota(jnp.int32, (16, WIDE), 0)
    value = jnp.where(which == 0, gain1[...], jnp.where(which == 1, gain2[...], 0.0))
    out[pl.ds(count, 16)] = value.astype(BF16)


def heads_grad(*inputs):
    left = [whole(v.shape) for v in inputs[:4]]
    here = pl.BlockSpec((TOKENS, WIDE), lambda i: (0, i))
    there = pl.BlockSpec((TOKENS, WIDE), lambda i: (0, 1 - i))
    gain = pl.BlockSpec((1, WIDE), lambda i: (0, i))
    return pl.pallas_call(
        heads_grad_kernel,
        grid=(2,),
        out_shape=shape((640, D), BF16),
        in_specs=[*left, here, there, here, there, gain, gain],
        out_specs=pl.BlockSpec((640, WIDE), lambda i: (0, i)),
        compiler_params=params(60),
        cost_estimate=cost(6 * TOKENS * D * SHARD, 10 << 20),
        name="heads_grad",
    )(*inputs)


def fold_first_kernel(spot, left, *refs, nx, nz):
    rights, out, outs = refs[:nz], refs[nz], refs[nz + 1 :]
    total = left[:nz].astype(F32)
    for i in range(1, nx):
        total = total + left[i * nz : (i + 1) * nz].astype(F32)
    out[...] = total.astype(BF16)
    for k in range(nx):
        place = jnp.bitwise_xor(spot[8], k)
        total = rights[0][place].astype(F32)
        for right in rights[1:]:
            total = total + right[place].astype(F32)
        outs[k][...] = total.astype(BF16)


def fold_first(spot, left, rights, nx):
    nz = len(rights)
    dims = left.shape[1:]
    outs = (shape((nz, *dims), BF16),) + (shape(dims, BF16),) * nx
    kernel = functools.partial(fold_first_kernel, nx=nx, nz=nz)
    return stage(kernel, "fold_first", spot, (left, *rights), outs, 0)


def fold_last_kernel(spot, left, *refs):
    rights, keep, send = refs[:-2], refs[-2], refs[-1]
    total = left[0].astype(F32)
    for i in range(1, left.shape[0]):
        total = total + left[i].astype(F32)
    other = rights[0][...].astype(F32)
    for right in rights[1:]:
        other = other + right[...].astype(F32)
    for j, value in enumerate((total.astype(BF16), other.astype(BF16))):
        low, high = value[:, :SHARD], value[:, SHARD:]

        @pl.when(spot[1] == 0)
        def _():
            keep[j], send[j] = low, high

        @pl.when(spot[1] == 1)
        def _():
            keep[j], send[j] = high, low


def fold_last(spot, left, rights):
    outs = (shape((2, left.shape[1], SHARD), BF16),) * 2
    return stage(fold_last_kernel, "fold_last", spot, (left, *rights), outs, 0)


def fold_kernel(spot, value, keep, send):
    total = value[0].astype(F32)
    for i in range(1, value.shape[0]):
        total = total + value[i].astype(F32)
    total = total.astype(BF16)
    for j in range(2):
        low = total[:, j * WIDE : j * WIDE + SHARD]
        high = total[:, j * WIDE + SHARD : (j + 1) * WIDE]

        @pl.when(spot[1] == 0)
        def _():
            keep[j], send[j] = low, high

        @pl.when(spot[1] == 1)
        def _():
            keep[j], send[j] = high, low


def fold(spot, value):
    outs = (shape((2, value.shape[1], SHARD), BF16),) * 2
    return stage(fold_kernel, "fold", spot, (value,), outs, 0)


def finish_units_kernel(spot, value, gate, up, lower, both):
    half = both.shape[0] // 4
    for j in range(value.shape[0]):
        span = pl.ds(j * 4 * half, 4 * half)
        for i, out in enumerate((gate, up, lower)):
            for place in range(4):
                low = jnp.bitwise_xor(spot[1], place % 2)
                core = jnp.bitwise_xor(spot[3], place // 2)
                rows = pl.ds(pl.multiple_of((2 * low + core) * half, half), half)
                both[rows] = value[j, place, pl.ds(i * half, half)]
            if i < 2:
                out[:, span] = both[...].astype(F32).T
            else:
                out[span] = both[...].astype(F32)


def finish_units(spot, value, steps):
    ndp = value.shape[0]
    half = value.shape[2] // 3
    cols = 4 * half * ndp // steps
    across = pl.BlockSpec((SHARD, cols), lambda i, s: (0, i))
    return pl.pallas_call(
        finish_units_kernel,
        out_shape=(shape((SHARD, cols * steps), F32),) * 2 + (shape((cols * steps, SHARD), F32),),
        grid_spec=pltpu.PrefetchScalarGridSpec(
            num_scalar_prefetch=1,
            grid=(steps,),
            in_specs=[pl.BlockSpec((ndp // steps, *value.shape[1:]), lambda i, s: (i, 0, 0, 0))],
            out_specs=(across, across, pl.BlockSpec((cols, SHARD), lambda i, s: (i, 0))),
            scratch_shapes=[pltpu.VMEM((4 * half, SHARD), BF16)],
        ),
        compiler_params=params(60),
        cost_estimate=cost(0, 14 << 20),
        name="finish_units",
    )(spot, value)


def finish_heads_kernel(spot, value, query, keyval, out, gains, part, full):
    count = value.shape[2]
    half = SHARD // 2
    total = jnp.zeros((8, SHARD), F32)
    for place in range(4):
        for i in range(value.shape[0]):
            part[pl.ds(i * count, count)] = value[i, place].astype(F32)
        low = jnp.bitwise_xor(spot[1], place % 2)
        core = jnp.bitwise_xor(spot[3], place // 2)
        rows = pl.ds(pl.multiple_of((2 * low + core) * half, half), half)
        for k in range(2):
            full[k, rows] = part[pl.ds(k * half, half)]
        out[rows] = part[pl.ds(2 * half, half)]
        total = total + part[pl.ds(3 * half, 8)]
    query[...] = full[0].T
    keyval[...] = full[1].T
    gains[...] = total


def finish_heads(spot, value):
    dims = ((SHARD, WIDE), (SHARD, WIDE), (WIDE, SHARD), (8, SHARD))
    scratch = [
        pltpu.VMEM((value.shape[0] * value.shape[2], SHARD), F32),
        pltpu.VMEM((2, WIDE, SHARD), F32),
    ]
    outs = tuple(shape(d, F32) for d in dims)
    return stage(finish_heads_kernel, "finish_heads", spot, (value,), outs, 0, scratch, 24)


def body(tokens, gain1, w_query, w_keyval, w_out, gain2, w_gate, w_up, w_down, grad_out, segments):
    core, yh, yl = lax.axis_index("core"), lax.axis_index("yhi"), lax.axis_index("ylo")
    nx, nz = lax.axis_size("x"), lax.axis_size("z")
    dp = lax.axis_index(DP)
    quarter = core ^ yh
    spot = jnp.stack(
        [yh, yl, 2 * yh + yl, core]
        + [place * QUARTER for place in (core, 3 - core, 1 - core, 2 + core)]
        + [lax.axis_index("x"), lax.axis_index("z"), dp]
    ).astype(jnp.int32)

    def pick(first_is_mine, own, other):
        return jnp.where(first_is_mine, own, other), jnp.where(first_is_mine, other, own)

    def halves_of(value):
        own = lax.dynamic_slice_in_dim(value, quarter * QUARTER, QUARTER, 0)
        return own, lax.dynamic_slice_in_dim(value, (1 - quarter) * QUARTER, QUARTER, 0)

    gains = jnp.stack([gain1, gain2])
    gains = jnp.stack([gains, swap(gains, "core")], axis=1)
    gains = jnp.stack(pick(yl == 0, gains, swap(gains, "ylo")), axis=2).reshape(2, 1, D)

    ids = segments[0]
    low_all = jnp.sum((ids[None, :] < ids[:, None]).astype(jnp.int32), axis=1)
    low = jnp.concatenate(
        [
            lax.dynamic_slice_in_dim(low_all, core * QUARTER, QUARTER),
            lax.dynamic_slice_in_dim(low_all, (3 - core) * QUARTER, QUARTER),
        ]
    )
    step = jnp.arange(QUARTER, dtype=jnp.int32)
    place = jnp.concatenate([core * QUARTER + step, (3 - core) * QUARTER + step])
    rates = THETA ** (-jnp.arange(HALF, dtype=F32) * 2.0 / HD)
    angles = rates[:, None] * (place - low).astype(F32)[None, :]
    cosine, sine = jnp.cos(angles), jnp.sin(angles)
    place, low = place[None, :], low[None, :]

    head_mine, head_send, unit_send, out_send = prepare(
        spot, w_query, w_keyval, w_gate, w_up, w_down, w_out, nx * nz
    )
    others = gather_dp(
        jnp.concatenate([swap_y(unit_send, 1), swap_y(out_send, 2), swap_y(out_send, 3)])
    )

    (x_own, x_other), (top_own, top_other) = halves_of(tokens[0]), halves_of(grad_out[0])
    got = swap(jnp.concatenate([x_other, top_other]), "core")
    pieces = peers_y(jnp.concatenate([x_own, got[:QUARTER]]))
    top_pair = jnp.concatenate([top_own, got[QUARTER:]])
    head_got = swap(head_send, "ylo")
    top_pair = jnp.broadcast_to(top_pair[None], (4, *top_pair.shape))
    *pieces, head_got, head_mine, gains, top_pair, cosine, sine, low = together(
        *pieces, head_got, head_mine, gains, top_pair, cosine, sine, low
    )
    head_pieces = (head_mine, head_got, swap(head_mine, "core"), swap(head_got, "core"))

    x, h_one, inv_one, queries, keyval, head_rows, head_rows_oth, x_block = project(
        spot, pieces, gains[0], head_pieces, cosine, sine
    )
    keyval_oth = swap(keyval, "core")
    top_pieces = over_y(after(top_pair, head_pieces[3]))
    others = after(others, queries)
    w_o = out_rows(spot, w_out, others)
    w_f = unit_rows(spot, w_gate, w_up, w_down, after(others, w_o))
    top_pieces, w_f, w_o, low, keyval_oth = together(top_pieces, w_f, w_o, low, keyval_oth)
    w_o_oth, w_f_oth = swap(w_o, "core"), swap(w_f, "core")
    heads_t, heads, lse, heads_mine, heads_send = attend(
        spot, queries, keyval, keyval_oth, place, low
    )
    heads_pieces = peers_y(heads)
    mixed, h_two, inv_two, mixed_block = mix(spot, x, heads_pieces, w_o, w_o_oth, gains[1])
    top, act, mine, send, parts = feed(spot, h_two, top_pieces, w_f, w_f_oth)
    parts = over_y(parts)

    got, h_two_oth, top_oth = swap(send, "core"), swap(h_two, "core"), swap(top, "core")
    left, *rights = units_grad(spot, mine, got, h_two, h_two_oth, top, top_oth, nx, nz)
    outs = down(spot, act, w_f, w_f_oth)
    parts, h_one_oth, left, *both = together(parts, swap(h_one, "core"), left, *rights, *outs)
    rights, outs = both[:nz], both[nz:]
    rows, gain2_part = residual(spot, parts, mixed, inv_two, top, gains[1])
    left = lax.all_to_all(left, "x", 0, 0, tiled=True)
    rights = to_peers(rights, "z")

    row_all, dq, dkv, dkv_oth, row_block = attend_back(
        spot, peers_y(rows), w_o, w_o_oth, queries, keyval, keyval_oth, heads_t, lse, place, low,
        cosine, sine,
    )
    dq, left, *rights = together(dq, left, *rights)
    left, *rights = fold_first(spot, left, rights, nx)
    left = lax.all_to_all(left, "z", 0, 0, tiled=True)
    rights = to_peers(rights, "x")
    raw, send, *parts, gain1_part = input_grad(
        spot, dq, dkv, swap(dkv_oth, "core"), cosine, sine, head_rows, head_rows_oth, x, inv_one
    )
    got = swap(send, "core")
    parts = to_peers_y(parts)

    sums = jnp.concatenate([gain1_part, gain2_part])
    sums = sums + swap(sums, "yhi")
    raw, got, row_all_oth, heads_got = together(
        raw, got, swap(row_all, "core"), swap(heads_send, "core")
    )
    head_parts = heads_grad(
        raw, got, heads_mine, heads_got, h_one, h_one_oth, row_all, row_all_oth,
        sums[:1], sums[1:],
    )
    head_parts, left, *rights = together(head_parts, left, *rights)
    head_parts = scatter_dp(head_parts.reshape(nx * nz, -1, D))
    keep, send = fold_last(spot, left, rights)
    low_got = swap(send, "ylo")

    def over_cores(keep, got):
        other = swap(jnp.stack([keep[1], got[1]]), "core")
        return jnp.stack([keep[0], got[0], other[0], other[1]])

    unit_parts = gather_dp(over_cores(keep, low_got))
    head_parts, *parts = together(head_parts, *parts)
    keep, send = fold(spot, head_parts)
    head_parts = gather_dp_now(over_cores(keep, swap(send, "ylo")))
    *outs, _ = together(*outs, keep)
    outs = to_peers_y(outs)

    got = sum([g.astype(F32) for g in parts])

    def to_home(block):
        return jnp.concatenate(pick(quarter == 0, block[0], swap(block[1], "core")))

    gain = jnp.stack(
        [lax.dynamic_slice(gains[0], (0, j * WIDE + yl * SHARD), (1, SHARD)) for j in range(2)]
    )
    inverse = lax.dynamic_slice_in_dim(inv_one, yh * QUARTER, QUARTER, 0)
    normed = x_block.astype(F32) * inverse
    scaled = got * gain
    inner = (scaled * normed).sum(axis=(0, 2))
    inner = (inner + swap(inner, "ylo"))[:, None] / D
    grad_in = to_home(row_block.astype(F32) + inverse * (scaled - normed * inner))

    output = mixed_block + sum([g.astype(F32) for g in outs])
    output = to_home(output.astype(BF16))

    grad_w_gate, grad_w_up, grad_w_down = finish_units(spot, unit_parts, nx)
    head_parts, grad_w_down = together(head_parts, grad_w_down)
    grad_w_query, grad_w_keyval, grad_w_out, sums = finish_heads(spot, head_parts)
    return (
        output[None],
        grad_in[None],
        sums[0],
        grad_w_query,
        grad_w_keyval,
        grad_w_out,
        sums[1],
        grad_w_gate,
        grad_w_up,
        grad_w_down,
    )


def solution(mesh):
    dp = mesh.shape["dp"]
    side = int(round(dp**0.5))
    fine = Mesh(
        mesh.devices.reshape(side, dp // side, 2, 2, 2), ("x", "z", "ylo", "core", "yhi")
    )
    seq, row, col = DP, ("ylo", "core"), "yhi"
    return jax.shard_map(
        body,
        mesh=fine,
        in_specs=(
            P(seq, col, row),
            P(row),
            P(row, col),
            P(row, col),
            P(col, row),
            P(row),
            P(row, col),
            P(row, col),
            P(col, row),
            P(seq, col, row),
            P(seq, None),
        ),
        out_specs=(
            P(seq, col, row),
            P(seq, col, row),
            P(row),
            P(row, col),
            P(row, col),
            P(col, row),
            P(row),
            P(row, col),
            P(row, col),
            P(col, row),
        ),
        check_vma=False,
    )
```

```python
import functools

import jax
import jax.numpy as jnp
from jax import lax
from jax.experimental import pallas as pl
from jax.experimental.pallas import tpu as pltpu
from jax.sharding import Mesh
from jax.sharding import PartitionSpec as P

D = 1536
HD = 96
HALF = HD // 2
EPS = 1e-05
THETA = 100000.0
NEGATIVE = -1e30
SCALE = HD**-0.5
LOG2E = 1.4426950408889634
F32 = jnp.float32
BF16 = jnp.bfloat16
QUARTER = 256
TOKENS = 2 * QUARTER
CHUNK = 128
WIDE = D // 2
SHARD = D // 4
DP = ("x", "z")

NN = ((1,), (0,))
NT = ((1,), (1,))
TN = ((0,), (0,))


def dot(a, b, dims):
    return lax.dot_general(a, b, (dims, ((), ())), preferred_element_type=F32)


def swap(value, axis, step=1):
    count = lax.axis_size(axis)
    return lax.ppermute(value, axis, [(i, i ^ step) for i in range(count)])


def swap_y(value, k):
    return swap(value, ("ylo", "yhi"), 2 * (k & 1) + (k >> 1))


def peers_y(value):
    return [value] + [swap_y(value, k) for k in (1, 2, 3)]


def to_peers_y(values):
    return [values[0]] + [swap_y(values[k], k) for k in (1, 2, 3)]


def from_peers(value, axis):
    return [value] + [swap(value, axis, k) for k in range(1, lax.axis_size(axis))]


def over_y(value):
    return lax.all_to_all(value, ("yhi", "ylo"), 0, 0, tiled=True)


def gather_y(value):
    return over_y(jnp.broadcast_to(value[None], (4, *value.shape)))


def to_peers(values, axis):
    return [values[0]] + [swap(values[k], axis, k) for k in range(1, lax.axis_size(axis))]


def scatter_dp(value):
    return lax.all_to_all(value, DP, 0, 0, tiled=True)


def gather_dp(value):
    return lax.all_gather(value, DP, axis=0)


def gather_dp_now(value):
    count = lax.axis_size(DP)
    return scatter_dp(jnp.broadcast_to(value[None], (count, *value.shape)))


def together(*values):
    return lax.optimization_barrier(values)


def after(value, *others):
    return lax.optimization_barrier((value, *others))[0]


def shape(dims, dtype):
    return jax.ShapeDtypeStruct(dims, dtype)


def cost(flops, nbytes):
    return pl.CostEstimate(flops=1, bytes_accessed=1, transcendentals=0)


def params(mib=60):
    return pltpu.CompilerParams(vmem_limit_bytes=mib << 20)


def whole(dims):
    return pl.BlockSpec(dims, lambda *_: (0,) * len(dims))


def stage(kernel, name, spot, inputs, outs, flops, scratch=(), mib=60):
    nbytes = sum(v.size * v.dtype.itemsize for v in (*inputs, *outs))
    return pl.pallas_call(
        kernel,
        out_shape=tuple(outs),
        grid_spec=pltpu.PrefetchScalarGridSpec(
            num_scalar_prefetch=1,
            grid=(1,),
            in_specs=[whole(v.shape) for v in inputs],
            out_specs=tuple(whole(v.shape) for v in outs),
            scratch_shapes=scratch,
        ),
        compiler_params=params(mib),
        cost_estimate=cost(flops, nbytes),
        name=name,
    )(spot, *inputs)


def peer(spot, k):
    high = jnp.bitwise_xor(spot[0], k >> 1)
    low = jnp.bitwise_xor(spot[1], k & 1)
    return high, low, 2 * high + low


def place_pieces(spot, pieces, out):
    for k, piece in enumerate(pieces):
        high, low, _ = peer(spot, k)
        rows = pl.ds(pl.multiple_of(high * QUARTER, QUARTER), QUARTER)
        for j in range(2):
            lanes = pl.ds(pl.multiple_of(low * SHARD + j * WIDE, 128), SHARD)
            out[rows, lanes] = piece[pl.ds(j * QUARTER, QUARTER)]


def cut_pieces(spot, value, outs):
    for k, out in enumerate(outs):
        high, low, _ = peer(spot, k)
        rows = pl.ds(pl.multiple_of(high * QUARTER, QUARTER), QUARTER)
        for j in range(2):
            lanes = pl.ds(pl.multiple_of(low * SHARD + j * WIDE, 128), SHARD)
            out[j] = value[rows, lanes].astype(out.dtype)


def turn(front, behind, cosine, sine):
    return front * cosine - behind * sine, behind * cosine + front * sine


def prepare_kernel(
    spot, query, keyval, gate, up, lower, outer, mine, send, units_send, out_send, turned, part
):
    low = spot[1]
    for i, w in enumerate((query, keyval)):
        value = w[...].T
        turned[0, pl.ds(i * SHARD, SHARD)] = value[:SHARD]
        turned[1, pl.ds(i * SHARD, SHARD)] = value[SHARD:]
    mine[...] = turned[low]
    send[...] = turned[1 - low]
    units = part.shape[0] // 2
    for k, value in enumerate((gate[...].T, up[...].T, lower[...])):
        part[...] = value
        units_send[pl.ds(k * units, units)] = part[
            pl.ds(pl.multiple_of((1 - low) * units, 64), units)
        ]
    units_send[3 * units :] = outer[...]
    out_send[...] = outer[...]


def prepare(spot, query, keyval, gate, up, lower, outer, ndp):
    cols = gate.shape[1] // ndp
    across = pl.BlockSpec((SHARD, cols), lambda i, s: (0, s[10]))
    count = WIDE // ndp
    dims = ((WIDE, SHARD), (WIDE, SHARD), (3 * cols // 2 + count, SHARD), (count, SHARD))
    return pl.pallas_call(
        prepare_kernel,
        out_shape=tuple(shape(d, BF16) for d in dims),
        grid_spec=pltpu.PrefetchScalarGridSpec(
            num_scalar_prefetch=1,
            grid=(1,),
            in_specs=[whole(query.shape), whole(keyval.shape), across, across]
            + [pl.BlockSpec((cols, SHARD), lambda i, s: (s[10], 0))]
            + [pl.BlockSpec((count, SHARD), lambda i, s: (s[10], 0))],
            out_specs=tuple(whole(d) for d in dims),
            scratch_shapes=[pltpu.VMEM((2, WIDE, SHARD), BF16), pltpu.VMEM((cols, SHARD), BF16)],
        ),
        compiler_params=params(60),
        cost_estimate=cost(0, 4 << 20),
        name="prepare",
    )(spot, query, keyval, gate, up, lower, outer)


def join_rows(spot, mine, got, out):
    out[:, pl.ds(pl.multiple_of(spot[1] * SHARD, 128), SHARD)] = mine[...]
    out[:, pl.ds(pl.multiple_of((1 - spot[1]) * SHARD, 128), SHARD)] = got[...]


def out_rows_kernel(spot, mine, value, out):
    rows = pl.ds(pl.multiple_of(spot[0] * WIDE, 64), WIDE)
    out[rows, pl.ds(pl.multiple_of(spot[1] * SHARD, 128), SHARD)] = mine[...]
    ndp = value.shape[0]
    count = WIDE // ndp
    base = value.shape[1] - 3 * count
    for i in range(ndp):
        for k in (1, 2, 3):
            high, low, _ = peer(spot, k)
            rows = pl.ds(pl.multiple_of(high * WIDE + i * count, 16), count)
            lanes = pl.ds(pl.multiple_of(low * SHARD, 128), SHARD)
            out[rows, lanes] = value[i, pl.ds(base + (k - 1) * count, count)]


def out_rows(spot, mine, value):
    outs = (shape((D, WIDE), BF16),)
    return stage(out_rows_kernel, "out_rows", spot, (mine, value), outs, 0, mib=60)[0]


def unit_rows_kernel(spot, gate, up, lower, other, out, turned):
    low = spot[1]
    units = out.shape[2]
    for k, value in enumerate((gate[...].T, up[...].T, lower[...])):
        turned[k] = value
    for j in range(out.shape[0]):
        for k in range(3):
            rows = pl.ds(pl.multiple_of((2 * j + low) * units, 64), units)
            out[j, k, :, pl.ds(pl.multiple_of(low * SHARD, 128), SHARD)] = turned[k, rows]
            out[j, k, :, pl.ds(pl.multiple_of((1 - low) * SHARD, 128), SHARD)] = other[
                j, pl.ds(k * units, units)
            ]


def unit_rows(spot, gate, up, lower, other, steps=4):
    ndp, rows, _ = other.shape
    cols = gate.shape[1] // steps
    units = gate.shape[1] // (2 * ndp)
    across = pl.BlockSpec((SHARD, cols), lambda i, s: (0, i))
    dims = (ndp, 3, units, WIDE)
    return pl.pallas_call(
        unit_rows_kernel,
        out_shape=shape(dims, BF16),
        grid_spec=pltpu.PrefetchScalarGridSpec(
            num_scalar_prefetch=1,
            grid=(steps,),
            in_specs=[across, across, pl.BlockSpec((cols, SHARD), lambda i, s: (i, 0))]
            + [pl.BlockSpec((ndp // steps, rows, SHARD), lambda i, s: (i, 0, 0))],
            out_specs=pl.BlockSpec((ndp // steps, *dims[1:]), lambda i, s: (i, 0, 0, 0)),
            scratch_shapes=[pltpu.VMEM((3, cols, SHARD), BF16)],
        ),
        compiler_params=params(60),
        cost_estimate=cost(0, 12 << 20),
        name="unit_rows",
    )(spot, gate, up, lower, other)


def qkv_kernel(
    spot, p0, p1, p2, p3, gain, mine, got, mine_oth, got_oth, cosine, sine,
    x, h, inv, q, kv, own, oth, block,
):
    place_pieces(spot, (p0, p1, p2, p3), x)
    cut_pieces(spot, x, (block,))
    join_rows(spot, mine, got, own)
    join_rows(spot, mine_oth, got_oth, oth)
    for i in range(4):
        rows = pl.ds(i * CHUNK, CHUNK)
        value = x[rows].astype(F32)
        inverse = lax.rsqrt((value * value).sum(axis=-1, keepdims=True) / D + EPS)
        inv[rows] = inverse
        h[rows] = (value * inverse * gain[...]).astype(BF16)
    cos, sin = cosine[...], sine[...]
    for i in range(4):
        rows = pl.ds(i * 2 * HD, 2 * HD)
        raw = dot(own[rows], h[:, :WIDE], NT) + dot(oth[rows], h[:, WIDE:], NT)
        out, base = (q, i * 2 * HD) if i < 2 else (kv, (i - 2) * 2 * HD)
        for head in range(2):
            front, behind = raw[head * HD : head * HD + HALF], raw[head * HD + HALF : (head + 1) * HD]
            if i < 2 or head == 0:
                front, behind = turn(front, behind, cos, sin)
            out[pl.ds(base + head * HD, HALF)] = front.astype(BF16)
            out[pl.ds(base + head * HD + HALF, HALF)] = behind.astype(BF16)


def project(spot, pieces, gain, rows, cosine, sine):
    outs = (
        shape((TOKENS, D), BF16),
        shape((TOKENS, D), BF16),
        shape((TOKENS, 1), F32),
        shape((SHARD, TOKENS), BF16),
        shape((SHARD, TOKENS), BF16),
        shape((WIDE, WIDE), BF16),
        shape((WIDE, WIDE), BF16),
        shape((2, QUARTER, SHARD), BF16),
    )
    inputs = (*pieces, gain, *rows, cosine, sine)
    return stage(qkv_kernel, "project", spot, inputs, outs, 2 * TOKENS * D * WIDE, mib=60)


def key_blocks(block):
    return (0, 2) if block == 0 else (0, 1, 2, 3)


def allowed_keys(spot, key, place, low):
    at = spot[4 + key] + lax.broadcasted_iota(jnp.int32, (QUARTER, place.shape[1]), 0)
    return (at >= low) & (at <= place)


def two_heads(ref, group, block):
    lanes = pl.ds(block * QUARTER, QUARTER)
    return jnp.concatenate(
        [ref[pl.ds((2 * group + h) * HD, HD), lanes] for h in range(2)], axis=1
    )


def twice(ref, block):
    row = ref[:, pl.ds(block * QUARTER, QUARTER)]
    return jnp.concatenate([row, row], axis=1)


def half_of(core, first=0):
    return pl.ds(pl.multiple_of(first + core * (SHARD // 2), 64), SHARD // 2)


def forward_kernel(
    spot, q_ref, own_ref, oth_ref, place_ref, low_ref, outt_ref, out_ref, lse_ref, mine_ref, send_ref
):
    factor = SCALE * LOG2E
    for group in range(2):
        keys = []
        vals = []
        for ref in (own_ref, oth_ref):
            for half in range(2):
                lanes = pl.ds(half * QUARTER, QUARTER)
                keys.append(ref[pl.ds(group * 2 * HD, HD), lanes].T)
                vals.append(ref[pl.ds(group * 2 * HD + HD, HD), lanes])
        for block in range(2):
            q = two_heads(q_ref, group, block)
            place, low = twice(place_ref, block), twice(low_ref, block)
            scores = []
            for key in key_blocks(block):
                s = dot(keys[key], q, NN)
                scores.append(jnp.where(allowed_keys(spot, key, place, low), s, NEGATIVE))
            peak = scores[0].max(axis=0, keepdims=True)
            for s in scores[1:]:
                peak = jnp.maximum(peak, s.max(axis=0, keepdims=True))
            shift = peak * factor
            total = jnp.zeros_like(peak)
            acc = jnp.zeros((HD, 2 * QUARTER), F32)
            for key, s in zip(key_blocks(block), scores):
                p = jnp.exp2(s * factor - shift)
                total = total + p.sum(axis=0, keepdims=True)
                acc = acc + dot(vals[key], p.astype(BF16), NN)
            acc = (acc / total).astype(BF16)
            lse = shift + jnp.log2(total)
            for h in range(2):
                lanes = pl.ds(block * QUARTER, QUARTER)
                cut = slice(h * QUARTER, (h + 1) * QUARTER)
                outt_ref[pl.ds((2 * group + h) * HD, HD), lanes] = acc[:, cut]
                lse_ref[pl.ds(2 * group + h, 1), lanes] = lse[:, cut]
    out_ref[...] = outt_ref[...].T
    for ref, core in ((mine_ref, spot[3]), (send_ref, 1 - spot[3])):
        ref[...] = outt_ref[half_of(core)]


def attend(spot, queries, own, other, place, low):
    outs = (
        shape((SHARD, TOKENS), BF16),
        shape((TOKENS, SHARD), BF16),
        shape((4, TOKENS), F32),
        *(shape((SHARD // 2, TOKENS), BF16),) * 2,
    )
    inputs = (queries, own, other, place, low)
    flops = 4 * 4 * HD * QUARTER * QUARTER * 6
    return stage(forward_kernel, "attend_forward", spot, inputs, outs, flops)


def mix_kernel(spot, x, h0, h1, h2, h3, own, oth, gain, mine, h, inv, block, heads, mixed):
    for k, piece in enumerate((h0, h1, h2, h3)):
        _, _, y = peer(spot, k)
        heads[:, pl.ds(pl.multiple_of(y * SHARD, 128), SHARD)] = piece[...]
    for i in range(2):
        rows = pl.ds(i * QUARTER, QUARTER)
        square = jnp.zeros((QUARTER, 1), F32)
        for j, w in enumerate((own, oth)):
            lanes = pl.ds(j * WIDE, WIDE)
            value = x[rows, lanes].astype(F32)
            value = value + dot(heads[rows], w[...], NN)
            mixed[rows, lanes] = value
            square = square + (value * value).sum(axis=-1, keepdims=True)
        inverse = lax.rsqrt(square / D + EPS)
        inv[rows] = inverse
        h[rows] = (mixed[rows] * inverse * gain[...]).astype(BF16)
    cut_pieces(spot, mixed, (block,))
    mine[...] = mixed[pl.ds(pl.multiple_of(spot[2] * CHUNK, CHUNK), CHUNK)]


def mix(spot, x, pieces, own, oth, gain):
    outs = (
        shape((CHUNK, D), F32),
        shape((TOKENS, D), BF16),
        shape((TOKENS, 1), F32),
        shape((2, QUARTER, SHARD), F32),
    )
    inputs = (x, *pieces, own, oth, gain)
    scratch = [pltpu.VMEM((TOKENS, D), BF16), pltpu.VMEM((TOKENS, D), F32)]
    return stage(mix_kernel, "mix", spot, inputs, outs, 2 * TOKENS * D * D, scratch)


def units_of(ref, k):
    return ref[:, k].reshape(-1, WIDE)


def feed_kernel(
    spot, h, pieces, own, oth, top, act, mine, others, dh, acc, stash
):
    step = pl.program_id(0)

    @pl.when(step == 0)
    def _():
        for y in range(4):
            rows = pl.ds((y // 2) * QUARTER, QUARTER)
            for j in range(2):
                lanes = pl.ds((y % 2) * SHARD + j * WIDE, SHARD)
                top[rows, lanes] = pieces[y, pl.ds(j * QUARTER, QUARTER)]
        acc[...] = jnp.zeros_like(acc)

    def hidden(k, columns):
        return dot(units_of(own, k), columns[:, :WIDE], NT) + dot(
            units_of(oth, k), columns[:, WIDE:], NT
        )

    gate, up, grad = hidden(0, h), hidden(1, h), hidden(2, top)
    sigma = jax.nn.sigmoid(gate)
    silu = gate * sigma
    grad_gate = (grad * up * sigma * (1.0 + gate * (1.0 - sigma))).astype(BF16)
    grad_up = (grad * silu).astype(BF16)
    value = (silu * up).astype(BF16)
    act[...] = value
    half = stash.shape[1] // 2
    for k, v in enumerate((grad_gate, grad_up, value)):
        stash[...] = v.reshape(stash.shape)
        for out, core in ((mine, spot[3]), (others, 1 - spot[3])):
            rows = pl.ds(pl.multiple_of(core * half, half), half)
            out[k] = stash[:, rows].reshape(out.shape[1:])
    grad_gate, grad_up = grad_gate.T, grad_up.T
    for j, w in enumerate((own, oth)):
        lanes = pl.ds(j * WIDE, WIDE)
        acc[:, lanes] += dot(grad_gate, units_of(w, 0), NN) + dot(grad_up, units_of(w, 1), NN)

    @pl.when(step == pl.num_programs(0) - 1)
    def _():
        for y in range(4):
            dh[y] = acc[pl.ds(y * CHUNK, CHUNK)].astype(BF16)


def feed(spot, h, pieces, own, oth):
    steps = 4
    ndp, _, units, _ = own.shape
    total = ndp * units
    weights = pl.BlockSpec((ndp // steps, *own.shape[1:]), lambda i, s: (i, 0, 0, 0))
    block = pl.BlockSpec((total // steps, TOKENS), lambda i, s: (i, 0))
    half = pl.BlockSpec((3, total // (2 * steps), TOKENS), lambda i, s: (0, i, 0))
    return pl.pallas_call(
        feed_kernel,
        out_shape=(
            shape((TOKENS, D), BF16),
            shape((total, TOKENS), BF16),
            *(shape((3, total // 2, TOKENS), BF16),) * 2,
            shape((4, CHUNK, D), BF16),
        ),
        grid_spec=pltpu.PrefetchScalarGridSpec(
            num_scalar_prefetch=1,
            grid=(steps,),
            in_specs=[whole((TOKENS, D)), whole(pieces.shape), weights, weights],
            out_specs=(whole((TOKENS, D)), block, half, half, whole((4, CHUNK, D))),
            scratch_shapes=[
                pltpu.VMEM((TOKENS, D), F32),
                pltpu.VMEM((ndp // steps, units, TOKENS), BF16),
            ],
        ),
        compiler_params=params(60),
        cost_estimate=cost(10 * TOKENS * D * total, 20 << 20),
        name="feed",
    )(spot, h, pieces, own, oth)


def down_kernel(spot, act, own, oth, o0, o1, o2, o3, acc):
    step = pl.program_id(0)

    @pl.when(step == 0)
    def _():
        acc[...] = jnp.zeros_like(acc)

    hidden = act[...].T
    for j, w in enumerate((own, oth)):
        acc[:, pl.ds(j * WIDE, WIDE)] += dot(hidden, w[...].reshape(-1, WIDE), NN)

    @pl.when(step == pl.num_programs(0) - 1)
    def _():
        cut_pieces(spot, acc, (o0, o1, o2, o3))


def down(spot, act, own, oth):
    steps = 4
    group = own.shape[0] // steps
    rows = act.shape[0] // steps
    weights = pl.BlockSpec((group, 1, *own.shape[2:]), lambda i, _: (i, 2, 0, 0))
    return pl.pallas_call(
        down_kernel,
        out_shape=(shape((2, QUARTER, SHARD), BF16),) * 4,
        grid_spec=pltpu.PrefetchScalarGridSpec(
            num_scalar_prefetch=1,
            grid=(steps,),
            in_specs=[pl.BlockSpec((rows, TOKENS), lambda i, _: (i, 0)), weights, weights],
            out_specs=(whole((2, QUARTER, SHARD)),) * 4,
            scratch_shapes=[pltpu.VMEM((TOKENS, D), F32)],
        ),
        compiler_params=params(60),
        cost_estimate=cost(2 * TOKENS * D * act.shape[0], 8 << 20),
        name="down",
    )(spot, act, own, oth)


def residual_kernel(spot, pieces, mixed, inv, top, gain, out, part):
    grad = pieces[0].astype(F32)
    for y in range(1, 4):
        grad = grad + pieces[y].astype(F32)
    inverse = inv[...]
    normed = mixed[...] * inverse
    part[...] = (grad * normed).sum(axis=0, keepdims=True)
    scaled = grad * gain[...]
    inner = (scaled * normed).sum(axis=-1, keepdims=True) / D
    out[...] = (top[...].astype(F32) + inverse * (scaled - normed * inner)).astype(BF16)


def residual(spot, pieces, mixed, inv, top, gain):
    mine = lambda width: pl.BlockSpec((CHUNK, width), lambda i, s: (2 * s[0] + s[1], 0))
    return pl.pallas_call(
        residual_kernel,
        out_shape=(shape((CHUNK, D), BF16), shape((1, D), F32)),
        grid_spec=pltpu.PrefetchScalarGridSpec(
            num_scalar_prefetch=1,
            grid=(1,),
            in_specs=[whole((4, CHUNK, D)), whole((CHUNK, D)), mine(1), mine(D), whole((1, D))],
            out_specs=(whole((CHUNK, D)), whole((1, D))),
        ),
        compiler_params=params(16),
        cost_estimate=cost(CHUNK * D * 20, 4 << 20),
        name="residual",
    )(spot, pieces, mixed, inv, top, gain)


def backward_kernel(
    spot, r0, r1, r2, r3, wown, woth, q_ref, own_ref, oth_ref, o_ref, lse_ref, place_ref, low_ref,
    cosine, sine, rows_ref, dq_ref, down_ref, doth_ref, block_ref, do_ref,
):
    for k, piece in enumerate((r0, r1, r2, r3)):
        _, _, y = peer(spot, k)
        rows_ref[pl.ds(pl.multiple_of(y * CHUNK, CHUNK), CHUNK)] = piece[...]
    cut_pieces(spot, rows_ref, (block_ref,))
    do_ref[...] = (
        dot(wown[...], rows_ref[:, :WIDE], NT) + dot(woth[...], rows_ref[:, WIDE:], NT)
    ).astype(BF16)
    factor = SCALE * LOG2E
    for group in range(2):
        keys, vals, keyst = [], [], []
        for ref in (own_ref, oth_ref):
            for half in range(2):
                lanes = pl.ds(half * QUARTER, QUARTER)
                kt = ref[pl.ds(group * 2 * HD, HD), lanes]
                keyst.append(kt)
                keys.append(kt.T)
                vals.append(ref[pl.ds(group * 2 * HD + HD, HD), lanes].T)
        dks = [jnp.zeros((HD, QUARTER), F32) for _ in range(4)]
        dvs = [jnp.zeros((HD, QUARTER), F32) for _ in range(4)]
        for block in range(2):
            lanes = pl.ds(block * QUARTER, QUARTER)
            q = two_heads(q_ref, group, block)
            do = two_heads(do_ref, group, block)
            o = two_heads(o_ref, group, block)
            place, low = twice(place_ref, block), twice(low_ref, block)
            lse = jnp.concatenate(
                [lse_ref[pl.ds(2 * group + h, 1), lanes] for h in range(2)], axis=1
            )
            delta = (do.astype(F32) * o.astype(F32)).sum(axis=0, keepdims=True)
            dq = jnp.zeros((HD, 2 * QUARTER), F32)
            for key in key_blocks(block):
                s = dot(keys[key], q, NN)
                p = jnp.exp2(s * factor - lse)
                p = jnp.where(allowed_keys(spot, key, place, low), p, 0.0)
                dp = dot(vals[key], do, NN)
                ds = (p * (dp - delta)).astype(BF16)
                dvs[key] = dvs[key] + dot(do, p.astype(BF16), NT)
                dks[key] = dks[key] + dot(q, ds, NT)
                dq = dq + dot(keyst[key], ds, NN)
            dq = dq * SCALE
            cos, sin = twice(cosine, block), twice(sine, block)
            front, behind = turn(dq[:HALF], dq[HALF:], cos, -sin)
            for h in range(2):
                cut = slice(h * QUARTER, (h + 1) * QUARTER)
                base = (2 * group + h) * HD
                dq_ref[pl.ds(base, HALF), lanes] = front[:, cut].astype(BF16)
                dq_ref[pl.ds(base + HALF, HALF), lanes] = behind[:, cut].astype(BF16)
        for i, ref in enumerate((down_ref, doth_ref)):
            for half in range(2):
                lanes = pl.ds(half * QUARTER, QUARTER)
                rows = group * 2 * HD
                ref[pl.ds(rows, HD), lanes] = (dks[2 * i + half] * SCALE).astype(ref.dtype)
                ref[pl.ds(rows + HD, HD), lanes] = dvs[2 * i + half].astype(ref.dtype)


def attend_back(spot, pieces, wown, woth, queries, own, other, outs, lse, place, low, cosine, sine):
    weights = pl.BlockSpec((SHARD, WIDE), lambda i, s: (s[2], 0))
    flat = whole((SHARD, TOKENS))
    row = whole((1, TOKENS))
    return pl.pallas_call(
        backward_kernel,
        out_shape=(
            shape((TOKENS, D), BF16),
            shape((SHARD, TOKENS), BF16),
            shape((SHARD, TOKENS), F32),
            shape((SHARD, TOKENS), BF16),
            shape((2, QUARTER, SHARD), BF16),
        ),
        grid_spec=pltpu.PrefetchScalarGridSpec(
            num_scalar_prefetch=1,
            grid=(1,),
            in_specs=[whole((CHUNK, D))] * 4
            + [weights, weights, flat, flat, flat, flat, whole((4, TOKENS)), row, row]
            + [whole((HALF, TOKENS))] * 2,
            out_specs=(whole((TOKENS, D)), flat, flat, flat, whole((2, QUARTER, SHARD))),
            scratch_shapes=[pltpu.VMEM((SHARD, TOKENS), BF16)],
        ),
        compiler_params=params(60),
        cost_estimate=cost(10 * 4 * HD * QUARTER * QUARTER * 6 + 2 * TOKENS * D * SHARD, 8 << 20),
        name="attend_backward",
    )(spot, *pieces, wown, woth, queries, own, other, outs, lse, place, low, cosine, sine)


def input_kernel(
    spot, dq, mine, got, cosine, sine, own, oth, x, inv, here, send, o0, o1, o2, o3, part, acc, raw
):
    raw[:SHARD] = dq[...]
    total = mine[...] + got[...].astype(F32)
    cos, sin = cosine[...], -sine[...]
    for group in range(2):
        base = group * 2 * HD
        front, behind = turn(total[base : base + HALF], total[base + HALF : base + HD], cos, sin)
        raw[pl.ds(SHARD + base, HALF)] = front.astype(BF16)
        raw[pl.ds(SHARD + base + HALF, HALF)] = behind.astype(BF16)
        raw[pl.ds(SHARD + base + HD, HD)] = total[base + HD : base + 2 * HD].astype(BF16)
    for j in range(2):
        span = pl.ds(j * (SHARD // 2), SHARD // 2)
        here[span] = raw[half_of(spot[3], j * SHARD)]
        send[span] = raw[half_of(1 - spot[3], j * SHARD)]
    grads = raw[...].T
    for j, w in enumerate((own, oth)):
        lanes = pl.ds(j * WIDE, WIDE)
        value = dot(grads, w[...], NN)
        acc[:, lanes] = value.astype(BF16)
        part[:, lanes] = (value * (x[:, lanes].astype(F32) * inv[...])).sum(axis=0, keepdims=True)
    cut_pieces(spot, acc, (o0, o1, o2, o3))


def input_grad(spot, dq, mine, got, cosine, sine, own, oth, x, inv):
    outs = (
        *(shape((SHARD, TOKENS), BF16),) * 2,
        *(shape((2, QUARTER, SHARD), BF16),) * 4,
        shape((1, D), F32),
    )
    inputs = (dq, mine, got, cosine, sine, own, oth, x, inv)
    scratch = [pltpu.VMEM((TOKENS, D), BF16), pltpu.VMEM((WIDE, TOKENS), BF16)]
    return stage(input_kernel, "input_grad", spot, inputs, outs, 2 * TOKENS * D * WIDE, scratch)


def units_grad_kernel(spot, mine, got, h, h_oth, top, top_oth, left, *rest):
    rights, stash = rest[:-1], rest[-1]
    half = left.shape[1] // 3
    for k in range(3):
        columns, columns_oth = (top, top_oth) if k == 2 else (h, h_oth)
        for j, out in enumerate((left, stash)):
            here, there = pl.ds(j * WIDE, WIDE), pl.ds((1 - j) * WIDE, WIDE)
            value = dot(mine[k], columns[:, here], NN) + dot(got[k], columns_oth[:, there], NN)
            out[:, pl.ds(k * half, half)] = value.astype(BF16).reshape(-1, half, WIDE)
    nz = len(rights)
    count = left.shape[0] // nz
    for j, right in enumerate(rights):
        for i in range(count):
            right[pl.program_id(0) * count + i] = stash[i * nz + jnp.bitwise_xor(spot[9], j)]


def units_grad(spot, mine, got, h, h_oth, top, top_oth, nx, nz):
    steps = 2
    ndp = nx * nz
    total = mine.shape[1]
    rows = 3 * total // ndp
    block = pl.BlockSpec((3, total // steps, TOKENS), lambda i, s: (0, i, 0))
    return pl.pallas_call(
        units_grad_kernel,
        out_shape=(shape((ndp, rows, WIDE), BF16),) + (shape((nx, rows, WIDE), BF16),) * nz,
        grid_spec=pltpu.PrefetchScalarGridSpec(
            num_scalar_prefetch=1,
            grid=(steps,),
            in_specs=[block, block] + [whole((TOKENS, D))] * 4,
            out_specs=(pl.BlockSpec((ndp // steps, rows, WIDE), lambda i, s: (i, 0, 0)),)
            + (whole((nx, rows, WIDE)),) * nz,
            scratch_shapes=[pltpu.VMEM((ndp // steps, rows, WIDE), BF16)],
        ),
        compiler_params=params(60),
        cost_estimate=cost(12 * TOKENS * D * total, 12 << 20),
        name="units_grad",
    )(spot, mine, got, h, h_oth, top, top_oth)


def heads_grad_kernel(mine, got, heads, heads_got, h, h_oth, rows, rows_oth, gain1, gain2, out):
    count = 3 * SHARD // 2
    first = 0
    for left, left_got, right, right_oth in (
        (mine, got, h, h_oth),
        (heads, heads_got, rows, rows_oth),
    ):
        value = dot(left[...], right[...], NN) + dot(left_got[...], right_oth[...], NN)
        out[pl.ds(first, left.shape[0])] = value.astype(BF16)
        first += left.shape[0]
    out[count:] = jnp.zeros((out.shape[0] - count, WIDE), BF16)
    which = lax.broadcasted_iota(jnp.int32, (16, WIDE), 0)
    value = jnp.where(which == 0, gain1[...], jnp.where(which == 1, gain2[...], 0.0))
    out[pl.ds(count, 16)] = value.astype(BF16)


def heads_grad(*inputs):
    left = [whole(v.shape) for v in inputs[:4]]
    here = pl.BlockSpec((TOKENS, WIDE), lambda i: (0, i))
    there = pl.BlockSpec((TOKENS, WIDE), lambda i: (0, 1 - i))
    gain = pl.BlockSpec((1, WIDE), lambda i: (0, i))
    return pl.pallas_call(
        heads_grad_kernel,
        grid=(2,),
        out_shape=shape((640, D), BF16),
        in_specs=[*left, here, there, here, there, gain, gain],
        out_specs=pl.BlockSpec((640, WIDE), lambda i: (0, i)),
        compiler_params=params(60),
        cost_estimate=cost(6 * TOKENS * D * SHARD, 10 << 20),
        name="heads_grad",
    )(*inputs)


def fold_first_kernel(spot, left, *refs, nx, nz):
    rights, out, outs = refs[:nz], refs[nz], refs[nz + 1 :]
    total = left[:nz].astype(F32)
    for i in range(1, nx):
        total = total + left[i * nz : (i + 1) * nz].astype(F32)
    out[...] = total.astype(BF16)
    for k in range(nx):
        place = jnp.bitwise_xor(spot[8], k)
        total = rights[0][place].astype(F32)
        for right in rights[1:]:
            total = total + right[place].astype(F32)
        outs[k][...] = total.astype(BF16)


def fold_first(spot, left, rights, nx):
    nz = len(rights)
    dims = left.shape[1:]
    outs = (shape((nz, *dims), BF16),) + (shape(dims, BF16),) * nx
    kernel = functools.partial(fold_first_kernel, nx=nx, nz=nz)
    return stage(kernel, "fold_first", spot, (left, *rights), outs, 0)


def fold_last_kernel(spot, left, *refs):
    rights, keep, send = refs[:-2], refs[-2], refs[-1]
    total = left[0].astype(F32)
    for i in range(1, left.shape[0]):
        total = total + left[i].astype(F32)
    other = rights[0][...].astype(F32)
    for right in rights[1:]:
        other = other + right[...].astype(F32)
    for j, value in enumerate((total.astype(BF16), other.astype(BF16))):
        low, high = value[:, :SHARD], value[:, SHARD:]

        @pl.when(spot[1] == 0)
        def _():
            keep[j], send[j] = low, high

        @pl.when(spot[1] == 1)
        def _():
            keep[j], send[j] = high, low


def fold_last(spot, left, rights):
    outs = (shape((2, left.shape[1], SHARD), BF16),) * 2
    return stage(fold_last_kernel, "fold_last", spot, (left, *rights), outs, 0, (), 16)


def fold_kernel(spot, value, keep, send):
    total = value[0].astype(F32)
    for i in range(1, value.shape[0]):
        total = total + value[i].astype(F32)
    total = total.astype(BF16)
    for j in range(2):
        low = total[:, j * WIDE : j * WIDE + SHARD]
        high = total[:, j * WIDE + SHARD : (j + 1) * WIDE]

        @pl.when(spot[1] == 0)
        def _():
            keep[j], send[j] = low, high

        @pl.when(spot[1] == 1)
        def _():
            keep[j], send[j] = high, low


def fold(spot, value):
    outs = (shape((2, value.shape[1], SHARD), BF16),) * 2
    return stage(fold_kernel, "fold", spot, (value,), outs, 0, (), 16)


def finish_units_kernel(spot, value, gate, up, lower, both):
    half = both.shape[0] // 4
    for j in range(value.shape[0]):
        span = pl.ds(j * 4 * half, 4 * half)
        for i, out in enumerate((gate, up, lower)):
            for place in range(4):
                low = jnp.bitwise_xor(spot[1], place % 2)
                core = jnp.bitwise_xor(spot[3], place // 2)
                rows = pl.ds(pl.multiple_of((2 * low + core) * half, half), half)
                both[rows] = value[j, place, pl.ds(i * half, half)]
            if i < 2:
                out[:, span] = both[...].astype(F32).T
            else:
                out[span] = both[...].astype(F32)


def finish_units(spot, value, steps):
    ndp = value.shape[0]
    half = value.shape[2] // 3
    cols = 4 * half * ndp // steps
    across = pl.BlockSpec((SHARD, cols), lambda i, s: (0, i))
    return pl.pallas_call(
        finish_units_kernel,
        out_shape=(shape((SHARD, cols * steps), F32),) * 2 + (shape((cols * steps, SHARD), F32),),
        grid_spec=pltpu.PrefetchScalarGridSpec(
            num_scalar_prefetch=1,
            grid=(steps,),
            in_specs=[pl.BlockSpec((ndp // steps, *value.shape[1:]), lambda i, s: (i, 0, 0, 0))],
            out_specs=(across, across, pl.BlockSpec((cols, SHARD), lambda i, s: (i, 0))),
            scratch_shapes=[pltpu.VMEM((4 * half, SHARD), BF16)],
        ),
        compiler_params=params(60),
        cost_estimate=cost(0, 14 << 20),
        name="finish_units",
    )(spot, value)


def finish_heads_kernel(spot, value, query, keyval, out, gains, part, full):
    count = value.shape[2]
    half = SHARD // 2
    total = jnp.zeros((8, SHARD), F32)
    for place in range(4):
        for i in range(value.shape[0]):
            part[pl.ds(i * count, count)] = value[i, place].astype(F32)
        low = jnp.bitwise_xor(spot[1], place % 2)
        core = jnp.bitwise_xor(spot[3], place // 2)
        rows = pl.ds(pl.multiple_of((2 * low + core) * half, half), half)
        for k in range(2):
            full[k, rows] = part[pl.ds(k * half, half)]
        out[rows] = part[pl.ds(2 * half, half)]
        total = total + part[pl.ds(3 * half, 8)]
    query[...] = full[0].T
    keyval[...] = full[1].T
    gains[...] = total


def finish_heads(spot, value):
    dims = ((SHARD, WIDE), (SHARD, WIDE), (WIDE, SHARD), (8, SHARD))
    scratch = [
        pltpu.VMEM((value.shape[0] * value.shape[2], SHARD), F32),
        pltpu.VMEM((2, WIDE, SHARD), F32),
    ]
    outs = tuple(shape(d, F32) for d in dims)
    return stage(finish_heads_kernel, "finish_heads", spot, (value,), outs, 0, scratch, 24)


def body(tokens, gain1, w_query, w_keyval, w_out, gain2, w_gate, w_up, w_down, grad_out, segments):
    core, yh, yl = lax.axis_index("core"), lax.axis_index("yhi"), lax.axis_index("ylo")
    nx, nz = lax.axis_size("x"), lax.axis_size("z")
    dp = lax.axis_index(DP)
    quarter = core ^ yh
    spot = jnp.stack(
        [yh, yl, 2 * yh + yl, core]
        + [place * QUARTER for place in (core, 3 - core, 1 - core, 2 + core)]
        + [lax.axis_index("x"), lax.axis_index("z"), dp]
    ).astype(jnp.int32)

    def pick(first_is_mine, own, other):
        return jnp.where(first_is_mine, own, other), jnp.where(first_is_mine, other, own)

    def halves_of(value):
        own = lax.dynamic_slice_in_dim(value, quarter * QUARTER, QUARTER, 0)
        return own, lax.dynamic_slice_in_dim(value, (1 - quarter) * QUARTER, QUARTER, 0)

    gains = jnp.stack([gain1, gain2])
    gains = jnp.stack([gains, swap(gains, "core")], axis=1)
    gains = jnp.stack(pick(yl == 0, gains, swap(gains, "ylo")), axis=2).reshape(2, 1, D)

    ids = segments[0]
    low_all = jnp.sum((ids[None, :] < ids[:, None]).astype(jnp.int32), axis=1)
    low = jnp.concatenate(
        [
            lax.dynamic_slice_in_dim(low_all, core * QUARTER, QUARTER),
            lax.dynamic_slice_in_dim(low_all, (3 - core) * QUARTER, QUARTER),
        ]
    )
    step = jnp.arange(QUARTER, dtype=jnp.int32)
    place = jnp.concatenate([core * QUARTER + step, (3 - core) * QUARTER + step])
    rates = THETA ** (-jnp.arange(HALF, dtype=F32) * 2.0 / HD)
    angles = rates[:, None] * (place - low).astype(F32)[None, :]
    cosine, sine = jnp.cos(angles), jnp.sin(angles)
    place, low = place[None, :], low[None, :]

    head_mine, head_send, unit_send, out_send = prepare(
        spot, w_query, w_keyval, w_gate, w_up, w_down, w_out, nx * nz
    )
    others = gather_dp(
        jnp.concatenate([swap_y(unit_send, 1), swap_y(out_send, 2), swap_y(out_send, 3)])
    )

    (x_own, x_other), (top_own, top_other) = halves_of(tokens[0]), halves_of(grad_out[0])
    got = swap(jnp.concatenate([x_other, top_other]), "core")
    pieces = peers_y(jnp.concatenate([x_own, got[:QUARTER]]))
    top_pair = jnp.concatenate([top_own, got[QUARTER:]])
    head_got = swap(head_send, "ylo")
    top_pair = jnp.broadcast_to(top_pair[None], (4, *top_pair.shape))
    *pieces, head_got, head_mine, gains, top_pair, cosine, sine, low = together(
        *pieces, head_got, head_mine, gains, top_pair, cosine, sine, low
    )
    head_pieces = (head_mine, head_got, swap(head_mine, "core"), swap(head_got, "core"))

    x, h_one, inv_one, queries, keyval, head_rows, head_rows_oth, x_block = project(
        spot, pieces, gains[0], head_pieces, cosine, sine
    )
    keyval_oth = swap(keyval, "core")
    top_pieces = over_y(after(top_pair, head_pieces[3]))
    others = after(others, queries)
    w_o = out_rows(spot, w_out, others)
    w_f = unit_rows(spot, w_gate, w_up, w_down, after(others, w_o))
    top_pieces, w_f, w_o, low, keyval_oth = together(top_pieces, w_f, w_o, low, keyval_oth)
    w_o_oth, w_f_oth = swap(w_o, "core"), swap(w_f, "core")
    heads_t, heads, lse, heads_mine, heads_send = attend(
        spot, queries, keyval, keyval_oth, place, low
    )
    heads_pieces = peers_y(heads)
    mixed, h_two, inv_two, mixed_block = mix(spot, x, heads_pieces, w_o, w_o_oth, gains[1])
    top, act, mine, send, parts = feed(spot, h_two, top_pieces, w_f, w_f_oth)
    parts = over_y(parts)

    got, h_two_oth, top_oth = swap(send, "core"), swap(h_two, "core"), swap(top, "core")
    left, *rights = units_grad(spot, mine, got, h_two, h_two_oth, top, top_oth, nx, nz)
    outs = down(spot, act, w_f, w_f_oth)
    parts, h_one_oth, left, *both = together(parts, swap(h_one, "core"), left, *rights, *outs)
    rights, outs = both[:nz], both[nz:]
    rows, gain2_part = residual(spot, parts, mixed, inv_two, top, gains[1])
    left = lax.all_to_all(left, "x", 0, 0, tiled=True)
    rights = to_peers(rights, "z")

    row_all, dq, dkv, dkv_oth, row_block = attend_back(
        spot, peers_y(rows), w_o, w_o_oth, queries, keyval, keyval_oth, heads_t, lse, place, low,
        cosine, sine,
    )
    dq, left, *rights = together(dq, left, *rights)
    left, *rights = fold_first(spot, left, rights, nx)
    left = lax.all_to_all(left, "z", 0, 0, tiled=True)
    rights = to_peers(rights, "x")
    raw, send, *parts, gain1_part = input_grad(
        spot, dq, dkv, swap(dkv_oth, "core"), cosine, sine, head_rows, head_rows_oth, x, inv_one
    )
    got = swap(send, "core")
    parts = to_peers_y(parts)

    sums = jnp.concatenate([gain1_part, gain2_part])
    sums = sums + swap(sums, "yhi")
    raw, got, row_all_oth, heads_got = together(
        raw, got, swap(row_all, "core"), swap(heads_send, "core")
    )
    head_parts = heads_grad(
        raw, got, heads_mine, heads_got, h_one, h_one_oth, row_all, row_all_oth,
        sums[:1], sums[1:],
    )
    head_parts, left, *rights = together(head_parts, left, *rights)
    head_parts = scatter_dp(head_parts.reshape(nx * nz, -1, D))
    keep, send = fold_last(spot, left, rights)
    low_got = swap(send, "ylo")

    def over_cores(keep, got):
        other = swap(jnp.stack([keep[1], got[1]]), "core")
        return jnp.stack([keep[0], got[0], other[0], other[1]])

    unit_parts = gather_dp(over_cores(keep, low_got))
    head_parts, *parts = together(head_parts, *parts)
    keep, send = fold(spot, head_parts)
    head_parts = gather_dp_now(over_cores(keep, swap(send, "ylo")))
    *outs, _ = together(*outs, keep)
    outs = to_peers_y(outs)

    got = sum([g.astype(F32) for g in parts])

    def to_home(block):
        return jnp.concatenate(pick(quarter == 0, block[0], swap(block[1], "core")))

    gain = jnp.stack(
        [lax.dynamic_slice(gains[0], (0, j * WIDE + yl * SHARD), (1, SHARD)) for j in range(2)]
    )
    inverse = lax.dynamic_slice_in_dim(inv_one, yh * QUARTER, QUARTER, 0)
    normed = x_block.astype(F32) * inverse
    scaled = got * gain
    inner = (scaled * normed).sum(axis=(0, 2))
    inner = (inner + swap(inner, "ylo"))[:, None] / D
    grad_in = to_home(row_block.astype(F32) + inverse * (scaled - normed * inner))

    output = mixed_block + sum([g.astype(F32) for g in outs])
    output = to_home(output.astype(BF16))

    grad_w_gate, grad_w_up, grad_w_down = finish_units(spot, unit_parts, nx)
    head_parts, grad_w_down = together(head_parts, grad_w_down)
    grad_w_query, grad_w_keyval, grad_w_out, sums = finish_heads(spot, head_parts)
    return (
        output[None],
        grad_in[None],
        sums[0],
        grad_w_query,
        grad_w_keyval,
        grad_w_out,
        sums[1],
        grad_w_gate,
        grad_w_up,
        grad_w_down,
    )


def solution(mesh):
    dp = mesh.shape["dp"]
    side = int(round(dp**0.5))
    fine = Mesh(
        mesh.devices.reshape(side, dp // side, 2, 2, 2), ("x", "z", "ylo", "core", "yhi")
    )
    seq, row, col = DP, ("ylo", "core"), "yhi"
    return jax.shard_map(
        body,
        mesh=fine,
        in_specs=(
            P(seq, col, row),
            P(row),
            P(row, col),
            P(row, col),
            P(col, row),
            P(row),
            P(row, col),
            P(row, col),
            P(col, row),
            P(seq, col, row),
            P(seq, None),
        ),
        out_specs=(
            P(seq, col, row),
            P(seq, col, row),
            P(row),
            P(row, col),
            P(row, col),
            P(col, row),
            P(row),
            P(row, col),
            P(row, col),
            P(col, row),
        ),
        check_vma=False,
    )
```

```python
import functools

import jax
import jax.numpy as jnp
from jax import lax
from jax.experimental import pallas as pl
from jax.experimental.pallas import tpu as pltpu
from jax.sharding import Mesh
from jax.sharding import PartitionSpec as P

D = 1536
HD = 96
HALF = HD // 2
EPS = 1e-05
THETA = 100000.0
NEGATIVE = -1e30
SCALE = HD**-0.5
LOG2E = 1.4426950408889634
F32 = jnp.float32
BF16 = jnp.bfloat16
QUARTER = 256
TOKENS = 2 * QUARTER
CHUNK = 128
WIDE = D // 2
SHARD = D // 4
DP = ("x", "z")

NN = ((1,), (0,))
NT = ((1,), (1,))
TN = ((0,), (0,))


def dot(a, b, dims):
    return lax.dot_general(a, b, (dims, ((), ())), preferred_element_type=F32)


def swap(value, axis, step=1):
    count = lax.axis_size(axis)
    return lax.ppermute(value, axis, [(i, i ^ step) for i in range(count)])


def swap_y(value, k):
    return swap(value, ("ylo", "yhi"), 2 * (k & 1) + (k >> 1))


def peers_y(value):
    return [value] + [swap_y(value, k) for k in (1, 2, 3)]


def to_peers_y(values):
    return [values[0]] + [swap_y(values[k], k) for k in (1, 2, 3)]


def from_peers(value, axis):
    return [value] + [swap(value, axis, k) for k in range(1, lax.axis_size(axis))]


def over_y(value):
    return lax.all_to_all(value, ("yhi", "ylo"), 0, 0, tiled=True)


def gather_y(value):
    return over_y(jnp.broadcast_to(value[None], (4, *value.shape)))


def to_peers(values, axis):
    return [values[0]] + [swap(values[k], axis, k) for k in range(1, lax.axis_size(axis))]


def scatter_dp(value):
    return lax.all_to_all(value, DP, 0, 0, tiled=True)


def gather_dp(value):
    return lax.all_gather(value, DP, axis=0)


def gather_dp_now(value):
    count = lax.axis_size(DP)
    return scatter_dp(jnp.broadcast_to(value[None], (count, *value.shape)))


def together(*values):
    return lax.optimization_barrier(values)


def after(value, *others):
    return lax.optimization_barrier((value, *others))[0]


def shape(dims, dtype):
    return jax.ShapeDtypeStruct(dims, dtype)


def cost(flops, nbytes):
    return pl.CostEstimate(flops=1, bytes_accessed=1, transcendentals=0)


def params(mib=60):
    return pltpu.CompilerParams(vmem_limit_bytes=mib << 20)


def whole(dims):
    return pl.BlockSpec(dims, lambda *_: (0,) * len(dims))


def stage(kernel, name, spot, inputs, outs, flops, scratch=(), mib=60):
    nbytes = sum(v.size * v.dtype.itemsize for v in (*inputs, *outs))
    return pl.pallas_call(
        kernel,
        out_shape=tuple(outs),
        grid_spec=pltpu.PrefetchScalarGridSpec(
            num_scalar_prefetch=1,
            grid=(1,),
            in_specs=[whole(v.shape) for v in inputs],
            out_specs=tuple(whole(v.shape) for v in outs),
            scratch_shapes=scratch,
        ),
        compiler_params=params(mib),
        cost_estimate=cost(flops, nbytes),
        name=name,
    )(spot, *inputs)


def peer(spot, k):
    high = jnp.bitwise_xor(spot[0], k >> 1)
    low = jnp.bitwise_xor(spot[1], k & 1)
    return high, low, 2 * high + low


def place_pieces(spot, pieces, out):
    for k, piece in enumerate(pieces):
        high, low, _ = peer(spot, k)
        rows = pl.ds(pl.multiple_of(high * QUARTER, QUARTER), QUARTER)
        for j in range(2):
            lanes = pl.ds(pl.multiple_of(low * SHARD + j * WIDE, 128), SHARD)
            out[rows, lanes] = piece[pl.ds(j * QUARTER, QUARTER)]


def cut_pieces(spot, value, outs):
    for k, out in enumerate(outs):
        high, low, _ = peer(spot, k)
        rows = pl.ds(pl.multiple_of(high * QUARTER, QUARTER), QUARTER)
        for j in range(2):
            lanes = pl.ds(pl.multiple_of(low * SHARD + j * WIDE, 128), SHARD)
            out[j] = value[rows, lanes].astype(out.dtype)


def turn(front, behind, cosine, sine):
    return front * cosine - behind * sine, behind * cosine + front * sine


def prepare_kernel(
    spot, query, keyval, gate, up, lower, outer, mine, send, units_send, out_send, turned, part
):
    low = spot[1]
    for i, w in enumerate((query, keyval)):
        value = w[...].T
        turned[0, pl.ds(i * SHARD, SHARD)] = value[:SHARD]
        turned[1, pl.ds(i * SHARD, SHARD)] = value[SHARD:]
    mine[...] = turned[low]
    send[...] = turned[1 - low]
    units = part.shape[0] // 2
    for k, value in enumerate((gate[...].T, up[...].T, lower[...])):
        part[...] = value
        units_send[pl.ds(k * units, units)] = part[
            pl.ds(pl.multiple_of((1 - low) * units, 64), units)
        ]
    units_send[3 * units :] = outer[...]
    out_send[...] = outer[...]


def prepare(spot, query, keyval, gate, up, lower, outer, ndp):
    cols = gate.shape[1] // ndp
    across = pl.BlockSpec((SHARD, cols), lambda i, s: (0, s[10]))
    count = WIDE // ndp
    dims = ((WIDE, SHARD), (WIDE, SHARD), (3 * cols // 2 + count, SHARD), (count, SHARD))
    return pl.pallas_call(
        prepare_kernel,
        out_shape=tuple(shape(d, BF16) for d in dims),
        grid_spec=pltpu.PrefetchScalarGridSpec(
            num_scalar_prefetch=1,
            grid=(1,),
            in_specs=[whole(query.shape), whole(keyval.shape), across, across]
            + [pl.BlockSpec((cols, SHARD), lambda i, s: (s[10], 0))]
            + [pl.BlockSpec((count, SHARD), lambda i, s: (s[10], 0))],
            out_specs=tuple(whole(d) for d in dims),
            scratch_shapes=[pltpu.VMEM((2, WIDE, SHARD), BF16), pltpu.VMEM((cols, SHARD), BF16)],
        ),
        compiler_params=params(60),
        cost_estimate=cost(0, 4 << 20),
        name="prepare",
    )(spot, query, keyval, gate, up, lower, outer)


def join_rows(spot, mine, got, out):
    out[:, pl.ds(pl.multiple_of(spot[1] * SHARD, 128), SHARD)] = mine[...]
    out[:, pl.ds(pl.multiple_of((1 - spot[1]) * SHARD, 128), SHARD)] = got[...]


def out_rows_kernel(spot, mine, value, out):
    rows = pl.ds(pl.multiple_of(spot[0] * WIDE, 64), WIDE)
    out[rows, pl.ds(pl.multiple_of(spot[1] * SHARD, 128), SHARD)] = mine[...]
    ndp = value.shape[0]
    count = WIDE // ndp
    base = value.shape[1] - 3 * count
    for i in range(ndp):
        for k in (1, 2, 3):
            high, low, _ = peer(spot, k)
            rows = pl.ds(pl.multiple_of(high * WIDE + i * count, 16), count)
            lanes = pl.ds(pl.multiple_of(low * SHARD, 128), SHARD)
            out[rows, lanes] = value[i, pl.ds(base + (k - 1) * count, count)]


def out_rows(spot, mine, value):
    outs = (shape((D, WIDE), BF16),)
    return stage(out_rows_kernel, "out_rows", spot, (mine, value), outs, 0, mib=60)[0]


def unit_rows_kernel(spot, gate, up, lower, other, out, turned):
    low = spot[1]
    units = out.shape[2]
    for k, value in enumerate((gate[...].T, up[...].T, lower[...])):
        turned[k] = value
    for j in range(out.shape[0]):
        for k in range(3):
            rows = pl.ds(pl.multiple_of((2 * j + low) * units, 64), units)
            out[j, k, :, pl.ds(pl.multiple_of(low * SHARD, 128), SHARD)] = turned[k, rows]
            out[j, k, :, pl.ds(pl.multiple_of((1 - low) * SHARD, 128), SHARD)] = other[
                j, pl.ds(k * units, units)
            ]


def unit_rows(spot, gate, up, lower, other, steps=4):
    ndp, rows, _ = other.shape
    cols = gate.shape[1] // steps
    units = gate.shape[1] // (2 * ndp)
    across = pl.BlockSpec((SHARD, cols), lambda i, s: (0, i))
    dims = (ndp, 3, units, WIDE)
    return pl.pallas_call(
        unit_rows_kernel,
        out_shape=shape(dims, BF16),
        grid_spec=pltpu.PrefetchScalarGridSpec(
            num_scalar_prefetch=1,
            grid=(steps,),
            in_specs=[across, across, pl.BlockSpec((cols, SHARD), lambda i, s: (i, 0))]
            + [pl.BlockSpec((ndp // steps, rows, SHARD), lambda i, s: (i, 0, 0))],
            out_specs=pl.BlockSpec((ndp // steps, *dims[1:]), lambda i, s: (i, 0, 0, 0)),
            scratch_shapes=[pltpu.VMEM((3, cols, SHARD), BF16)],
        ),
        compiler_params=params(60),
        cost_estimate=cost(0, 12 << 20),
        name="unit_rows",
    )(spot, gate, up, lower, other)


def qkv_kernel(
    spot, p0, p1, p2, p3, gain, mine, got, mine_oth, got_oth, cosine, sine,
    x, h, inv, q, kv, own, oth, block,
):
    place_pieces(spot, (p0, p1, p2, p3), x)
    cut_pieces(spot, x, (block,))
    join_rows(spot, mine, got, own)
    join_rows(spot, mine_oth, got_oth, oth)
    for i in range(4):
        rows = pl.ds(i * CHUNK, CHUNK)
        value = x[rows].astype(F32)
        inverse = lax.rsqrt((value * value).sum(axis=-1, keepdims=True) / D + EPS)
        inv[rows] = inverse
        h[rows] = (value * inverse * gain[...]).astype(BF16)
    cos, sin = cosine[...], sine[...]
    for i in range(4):
        rows = pl.ds(i * 2 * HD, 2 * HD)
        raw = dot(own[rows], h[:, :WIDE], NT) + dot(oth[rows], h[:, WIDE:], NT)
        out, base = (q, i * 2 * HD) if i < 2 else (kv, (i - 2) * 2 * HD)
        for head in range(2):
            front, behind = raw[head * HD : head * HD + HALF], raw[head * HD + HALF : (head + 1) * HD]
            if i < 2 or head == 0:
                front, behind = turn(front, behind, cos, sin)
            out[pl.ds(base + head * HD, HALF)] = front.astype(BF16)
            out[pl.ds(base + head * HD + HALF, HALF)] = behind.astype(BF16)


def project(spot, pieces, gain, rows, cosine, sine):
    outs = (
        shape((TOKENS, D), BF16),
        shape((TOKENS, D), BF16),
        shape((TOKENS, 1), F32),
        shape((SHARD, TOKENS), BF16),
        shape((SHARD, TOKENS), BF16),
        shape((WIDE, WIDE), BF16),
        shape((WIDE, WIDE), BF16),
        shape((2, QUARTER, SHARD), BF16),
    )
    inputs = (*pieces, gain, *rows, cosine, sine)
    return stage(qkv_kernel, "project", spot, inputs, outs, 2 * TOKENS * D * WIDE, mib=60)


def key_blocks(block):
    return (0, 2) if block == 0 else (0, 1, 2, 3)


def allowed_keys(spot, key, place, low):
    at = spot[4 + key] + lax.broadcasted_iota(jnp.int32, (QUARTER, place.shape[1]), 0)
    return (at >= low) & (at <= place)


def two_heads(ref, group, block):
    lanes = pl.ds(block * QUARTER, QUARTER)
    return jnp.concatenate(
        [ref[pl.ds((2 * group + h) * HD, HD), lanes] for h in range(2)], axis=1
    )


def twice(ref, block):
    row = ref[:, pl.ds(block * QUARTER, QUARTER)]
    return jnp.concatenate([row, row], axis=1)


def half_of(core, first=0):
    return pl.ds(pl.multiple_of(first + core * (SHARD // 2), 64), SHARD // 2)


def forward_kernel(
    spot, q_ref, own_ref, oth_ref, place_ref, low_ref, outt_ref, out_ref, lse_ref, mine_ref, send_ref
):
    factor = SCALE * LOG2E
    for group in range(2):
        keys = []
        vals = []
        for ref in (own_ref, oth_ref):
            for half in range(2):
                lanes = pl.ds(half * QUARTER, QUARTER)
                keys.append(ref[pl.ds(group * 2 * HD, HD), lanes].T)
                vals.append(ref[pl.ds(group * 2 * HD + HD, HD), lanes])
        for block in range(2):
            q = two_heads(q_ref, group, block)
            place, low = twice(place_ref, block), twice(low_ref, block)
            scores = []
            for key in key_blocks(block):
                s = dot(keys[key], q, NN)
                scores.append(jnp.where(allowed_keys(spot, key, place, low), s, NEGATIVE))
            peak = scores[0].max(axis=0, keepdims=True)
            for s in scores[1:]:
                peak = jnp.maximum(peak, s.max(axis=0, keepdims=True))
            shift = peak * factor
            total = jnp.zeros_like(peak)
            acc = jnp.zeros((HD, 2 * QUARTER), F32)
            for key, s in zip(key_blocks(block), scores):
                p = jnp.exp2(s * factor - shift)
                total = total + p.sum(axis=0, keepdims=True)
                acc = acc + dot(vals[key], p.astype(BF16), NN)
            acc = (acc / total).astype(BF16)
            lse = shift + jnp.log2(total)
            for h in range(2):
                lanes = pl.ds(block * QUARTER, QUARTER)
                cut = slice(h * QUARTER, (h + 1) * QUARTER)
                outt_ref[pl.ds((2 * group + h) * HD, HD), lanes] = acc[:, cut]
                lse_ref[pl.ds(2 * group + h, 1), lanes] = lse[:, cut]
    out_ref[...] = outt_ref[...].T
    for ref, core in ((mine_ref, spot[3]), (send_ref, 1 - spot[3])):
        ref[...] = outt_ref[half_of(core)]


def attend(spot, queries, own, other, place, low):
    outs = (
        shape((SHARD, TOKENS), BF16),
        shape((TOKENS, SHARD), BF16),
        shape((4, TOKENS), F32),
        *(shape((SHARD // 2, TOKENS), BF16),) * 2,
    )
    inputs = (queries, own, other, place, low)
    flops = 4 * 4 * HD * QUARTER * QUARTER * 6
    return stage(forward_kernel, "attend_forward", spot, inputs, outs, flops)


def mix_kernel(spot, x, h0, h1, h2, h3, own, oth, gain, mine, h, inv, block, heads, mixed):
    for k, piece in enumerate((h0, h1, h2, h3)):
        _, _, y = peer(spot, k)
        heads[:, pl.ds(pl.multiple_of(y * SHARD, 128), SHARD)] = piece[...]
    for i in range(2):
        rows = pl.ds(i * QUARTER, QUARTER)
        square = jnp.zeros((QUARTER, 1), F32)
        for j, w in enumerate((own, oth)):
            lanes = pl.ds(j * WIDE, WIDE)
            value = x[rows, lanes].astype(F32)
            value = value + dot(heads[rows], w[...], NN)
            mixed[rows, lanes] = value
            square = square + (value * value).sum(axis=-1, keepdims=True)
        inverse = lax.rsqrt(square / D + EPS)
        inv[rows] = inverse
        h[rows] = (mixed[rows] * inverse * gain[...]).astype(BF16)
    cut_pieces(spot, mixed, (block,))
    mine[...] = mixed[pl.ds(pl.multiple_of(spot[2] * CHUNK, CHUNK), CHUNK)]


def mix(spot, x, pieces, own, oth, gain):
    outs = (
        shape((CHUNK, D), F32),
        shape((TOKENS, D), BF16),
        shape((TOKENS, 1), F32),
        shape((2, QUARTER, SHARD), F32),
    )
    inputs = (x, *pieces, own, oth, gain)
    scratch = [pltpu.VMEM((TOKENS, D), BF16), pltpu.VMEM((TOKENS, D), F32)]
    return stage(mix_kernel, "mix", spot, inputs, outs, 2 * TOKENS * D * D, scratch)


def units_of(ref, k):
    return ref[:, k].reshape(-1, WIDE)


def feed_kernel(
    spot, h, pieces, own, oth, top, act, mine, others, dh, acc, stash
):
    step = pl.program_id(0)

    @pl.when(step == 0)
    def _():
        for y in range(4):
            rows = pl.ds((y // 2) * QUARTER, QUARTER)
            for j in range(2):
                lanes = pl.ds((y % 2) * SHARD + j * WIDE, SHARD)
                top[rows, lanes] = pieces[y, pl.ds(j * QUARTER, QUARTER)]
        acc[...] = jnp.zeros_like(acc)

    def hidden(k, columns):
        return dot(units_of(own, k), columns[:, :WIDE], NT) + dot(
            units_of(oth, k), columns[:, WIDE:], NT
        )

    gate, up, grad = hidden(0, h), hidden(1, h), hidden(2, top)
    sigma = jax.nn.sigmoid(gate)
    silu = gate * sigma
    grad_gate = (grad * up * sigma * (1.0 + gate * (1.0 - sigma))).astype(BF16)
    grad_up = (grad * silu).astype(BF16)
    value = (silu * up).astype(BF16)
    act[...] = value
    half = stash.shape[1] // 2
    for k, v in enumerate((grad_gate, grad_up, value)):
        stash[...] = v.reshape(stash.shape)
        for out, core in ((mine, spot[3]), (others, 1 - spot[3])):
            rows = pl.ds(pl.multiple_of(core * half, half), half)
            out[k] = stash[:, rows].reshape(out.shape[1:])
    grad_gate, grad_up = grad_gate.T, grad_up.T
    for j, w in enumerate((own, oth)):
        lanes = pl.ds(j * WIDE, WIDE)
        acc[:, lanes] += dot(grad_gate, units_of(w, 0), NN) + dot(grad_up, units_of(w, 1), NN)

    @pl.when(step == pl.num_programs(0) - 1)
    def _():
        for y in range(4):
            dh[y] = acc[pl.ds(y * CHUNK, CHUNK)].astype(BF16)


def feed(spot, h, pieces, own, oth):
    steps = 4
    ndp, _, units, _ = own.shape
    total = ndp * units
    weights = pl.BlockSpec((ndp // steps, *own.shape[1:]), lambda i, s: (i, 0, 0, 0))
    block = pl.BlockSpec((total // steps, TOKENS), lambda i, s: (i, 0))
    half = pl.BlockSpec((3, total // (2 * steps), TOKENS), lambda i, s: (0, i, 0))
    return pl.pallas_call(
        feed_kernel,
        out_shape=(
            shape((TOKENS, D), BF16),
            shape((total, TOKENS), BF16),
            *(shape((3, total // 2, TOKENS), BF16),) * 2,
            shape((4, CHUNK, D), BF16),
        ),
        grid_spec=pltpu.PrefetchScalarGridSpec(
            num_scalar_prefetch=1,
            grid=(steps,),
            in_specs=[whole((TOKENS, D)), whole(pieces.shape), weights, weights],
            out_specs=(whole((TOKENS, D)), block, half, half, whole((4, CHUNK, D))),
            scratch_shapes=[
                pltpu.VMEM((TOKENS, D), F32),
                pltpu.VMEM((ndp // steps, units, TOKENS), BF16),
            ],
        ),
        compiler_params=params(60),
        cost_estimate=cost(10 * TOKENS * D * total, 20 << 20),
        name="feed",
    )(spot, h, pieces, own, oth)


def down_kernel(spot, act, own, oth, o0, o1, o2, o3, acc):
    step = pl.program_id(0)

    @pl.when(step == 0)
    def _():
        acc[...] = jnp.zeros_like(acc)

    hidden = act[...].T
    for j, w in enumerate((own, oth)):
        acc[:, pl.ds(j * WIDE, WIDE)] += dot(hidden, w[...].reshape(-1, WIDE), NN)

    @pl.when(step == pl.num_programs(0) - 1)
    def _():
        cut_pieces(spot, acc, (o0, o1, o2, o3))


def down(spot, act, own, oth):
    steps = 4
    group = own.shape[0] // steps
    rows = act.shape[0] // steps
    weights = pl.BlockSpec((group, 1, *own.shape[2:]), lambda i, _: (i, 2, 0, 0))
    return pl.pallas_call(
        down_kernel,
        out_shape=(shape((2, QUARTER, SHARD), BF16),) * 4,
        grid_spec=pltpu.PrefetchScalarGridSpec(
            num_scalar_prefetch=1,
            grid=(steps,),
            in_specs=[pl.BlockSpec((rows, TOKENS), lambda i, _: (i, 0)), weights, weights],
            out_specs=(whole((2, QUARTER, SHARD)),) * 4,
            scratch_shapes=[pltpu.VMEM((TOKENS, D), F32)],
        ),
        compiler_params=params(60),
        cost_estimate=cost(2 * TOKENS * D * act.shape[0], 8 << 20),
        name="down",
    )(spot, act, own, oth)


def residual_kernel(spot, pieces, mixed, inv, top, gain, out, part):
    grad = pieces[0].astype(F32)
    for y in range(1, 4):
        grad = grad + pieces[y].astype(F32)
    inverse = inv[...]
    normed = mixed[...] * inverse
    part[...] = (grad * normed).sum(axis=0, keepdims=True)
    scaled = grad * gain[...]
    inner = (scaled * normed).sum(axis=-1, keepdims=True) / D
    out[...] = (top[...].astype(F32) + inverse * (scaled - normed * inner)).astype(BF16)


def residual(spot, pieces, mixed, inv, top, gain):
    mine = lambda width: pl.BlockSpec((CHUNK, width), lambda i, s: (2 * s[0] + s[1], 0))
    return pl.pallas_call(
        residual_kernel,
        out_shape=(shape((CHUNK, D), BF16), shape((1, D), F32)),
        grid_spec=pltpu.PrefetchScalarGridSpec(
            num_scalar_prefetch=1,
            grid=(1,),
            in_specs=[whole((4, CHUNK, D)), whole((CHUNK, D)), mine(1), mine(D), whole((1, D))],
            out_specs=(whole((CHUNK, D)), whole((1, D))),
        ),
        compiler_params=params(16),
        cost_estimate=cost(CHUNK * D * 20, 4 << 20),
        name="residual",
    )(spot, pieces, mixed, inv, top, gain)


def backward_kernel(
    spot, r0, r1, r2, r3, wown, woth, q_ref, own_ref, oth_ref, o_ref, lse_ref, place_ref, low_ref,
    cosine, sine, rows_ref, dq_ref, down_ref, doth_ref, block_ref, do_ref,
):
    for k, piece in enumerate((r0, r1, r2, r3)):
        _, _, y = peer(spot, k)
        rows_ref[pl.ds(pl.multiple_of(y * CHUNK, CHUNK), CHUNK)] = piece[...]
    cut_pieces(spot, rows_ref, (block_ref,))
    do_ref[...] = (
        dot(wown[...], rows_ref[:, :WIDE], NT) + dot(woth[...], rows_ref[:, WIDE:], NT)
    ).astype(BF16)
    factor = SCALE * LOG2E
    for group in range(2):
        keys, vals, keyst = [], [], []
        for ref in (own_ref, oth_ref):
            for half in range(2):
                lanes = pl.ds(half * QUARTER, QUARTER)
                kt = ref[pl.ds(group * 2 * HD, HD), lanes]
                keyst.append(kt)
                keys.append(kt.T)
                vals.append(ref[pl.ds(group * 2 * HD + HD, HD), lanes].T)
        dks = [jnp.zeros((HD, QUARTER), F32) for _ in range(4)]
        dvs = [jnp.zeros((HD, QUARTER), F32) for _ in range(4)]
        for block in range(2):
            lanes = pl.ds(block * QUARTER, QUARTER)
            q = two_heads(q_ref, group, block)
            do = two_heads(do_ref, group, block)
            o = two_heads(o_ref, group, block)
            place, low = twice(place_ref, block), twice(low_ref, block)
            lse = jnp.concatenate(
                [lse_ref[pl.ds(2 * group + h, 1), lanes] for h in range(2)], axis=1
            )
            delta = (do.astype(F32) * o.astype(F32)).sum(axis=0, keepdims=True)
            dq = jnp.zeros((HD, 2 * QUARTER), F32)
            for key in key_blocks(block):
                s = dot(keys[key], q, NN)
                p = jnp.exp2(s * factor - lse)
                p = jnp.where(allowed_keys(spot, key, place, low), p, 0.0)
                dp = dot(vals[key], do, NN)
                ds = (p * (dp - delta)).astype(BF16)
                dvs[key] = dvs[key] + dot(do, p.astype(BF16), NT)
                dks[key] = dks[key] + dot(q, ds, NT)
                dq = dq + dot(keyst[key], ds, NN)
            dq = dq * SCALE
            cos, sin = twice(cosine, block), twice(sine, block)
            front, behind = turn(dq[:HALF], dq[HALF:], cos, -sin)
            for h in range(2):
                cut = slice(h * QUARTER, (h + 1) * QUARTER)
                base = (2 * group + h) * HD
                dq_ref[pl.ds(base, HALF), lanes] = front[:, cut].astype(BF16)
                dq_ref[pl.ds(base + HALF, HALF), lanes] = behind[:, cut].astype(BF16)
        for i, ref in enumerate((down_ref, doth_ref)):
            for half in range(2):
                lanes = pl.ds(half * QUARTER, QUARTER)
                rows = group * 2 * HD
                ref[pl.ds(rows, HD), lanes] = (dks[2 * i + half] * SCALE).astype(ref.dtype)
                ref[pl.ds(rows + HD, HD), lanes] = dvs[2 * i + half].astype(ref.dtype)


def attend_back(spot, pieces, wown, woth, queries, own, other, outs, lse, place, low, cosine, sine):
    weights = pl.BlockSpec((SHARD, WIDE), lambda i, s: (s[2], 0))
    flat = whole((SHARD, TOKENS))
    row = whole((1, TOKENS))
    return pl.pallas_call(
        backward_kernel,
        out_shape=(
            shape((TOKENS, D), BF16),
            shape((SHARD, TOKENS), BF16),
            shape((SHARD, TOKENS), F32),
            shape((SHARD, TOKENS), BF16),
            shape((2, QUARTER, SHARD), BF16),
        ),
        grid_spec=pltpu.PrefetchScalarGridSpec(
            num_scalar_prefetch=1,
            grid=(1,),
            in_specs=[whole((CHUNK, D))] * 4
            + [weights, weights, flat, flat, flat, flat, whole((4, TOKENS)), row, row]
            + [whole((HALF, TOKENS))] * 2,
            out_specs=(whole((TOKENS, D)), flat, flat, flat, whole((2, QUARTER, SHARD))),
            scratch_shapes=[pltpu.VMEM((SHARD, TOKENS), BF16)],
        ),
        compiler_params=params(60),
        cost_estimate=cost(10 * 4 * HD * QUARTER * QUARTER * 6 + 2 * TOKENS * D * SHARD, 8 << 20),
        name="attend_backward",
    )(spot, *pieces, wown, woth, queries, own, other, outs, lse, place, low, cosine, sine)


def input_kernel(
    spot, dq, mine, got, cosine, sine, own, oth, x, inv, here, send, o0, o1, o2, o3, part, acc, raw
):
    raw[:SHARD] = dq[...]
    total = mine[...] + got[...].astype(F32)
    cos, sin = cosine[...], -sine[...]
    for group in range(2):
        base = group * 2 * HD
        front, behind = turn(total[base : base + HALF], total[base + HALF : base + HD], cos, sin)
        raw[pl.ds(SHARD + base, HALF)] = front.astype(BF16)
        raw[pl.ds(SHARD + base + HALF, HALF)] = behind.astype(BF16)
        raw[pl.ds(SHARD + base + HD, HD)] = total[base + HD : base + 2 * HD].astype(BF16)
    for j in range(2):
        span = pl.ds(j * (SHARD // 2), SHARD // 2)
        here[span] = raw[half_of(spot[3], j * SHARD)]
        send[span] = raw[half_of(1 - spot[3], j * SHARD)]
    grads = raw[...].T
    for j, w in enumerate((own, oth)):
        lanes = pl.ds(j * WIDE, WIDE)
        value = dot(grads, w[...], NN)
        acc[:, lanes] = value.astype(BF16)
        part[:, lanes] = (value * (x[:, lanes].astype(F32) * inv[...])).sum(axis=0, keepdims=True)
    cut_pieces(spot, acc, (o0, o1, o2, o3))


def input_grad(spot, dq, mine, got, cosine, sine, own, oth, x, inv):
    outs = (
        *(shape((SHARD, TOKENS), BF16),) * 2,
        *(shape((2, QUARTER, SHARD), BF16),) * 4,
        shape((1, D), F32),
    )
    inputs = (dq, mine, got, cosine, sine, own, oth, x, inv)
    scratch = [pltpu.VMEM((TOKENS, D), BF16), pltpu.VMEM((WIDE, TOKENS), BF16)]
    return stage(input_kernel, "input_grad", spot, inputs, outs, 2 * TOKENS * D * WIDE, scratch)


def units_grad_kernel(spot, mine, got, h, h_oth, top, top_oth, left, *rest):
    rights, stash = rest[:-1], rest[-1]
    half = left.shape[1] // 3
    for k in range(3):
        columns, columns_oth = (top, top_oth) if k == 2 else (h, h_oth)
        for j, out in enumerate((left, stash)):
            here, there = pl.ds(j * WIDE, WIDE), pl.ds((1 - j) * WIDE, WIDE)
            value = dot(mine[k], columns[:, here], NN) + dot(got[k], columns_oth[:, there], NN)
            out[:, pl.ds(k * half, half)] = value.astype(BF16).reshape(-1, half, WIDE)
    nz = len(rights)
    count = left.shape[0] // nz
    for j, right in enumerate(rights):
        for i in range(count):
            right[pl.program_id(0) * count + i] = stash[i * nz + jnp.bitwise_xor(spot[9], j)]


def units_grad(spot, mine, got, h, h_oth, top, top_oth, nx, nz):
    steps = 2
    ndp = nx * nz
    total = mine.shape[1]
    rows = 3 * total // ndp
    block = pl.BlockSpec((3, total // steps, TOKENS), lambda i, s: (0, i, 0))
    return pl.pallas_call(
        units_grad_kernel,
        out_shape=(shape((ndp, rows, WIDE), BF16),) + (shape((nx, rows, WIDE), BF16),) * nz,
        grid_spec=pltpu.PrefetchScalarGridSpec(
            num_scalar_prefetch=1,
            grid=(steps,),
            in_specs=[block, block] + [whole((TOKENS, D))] * 4,
            out_specs=(pl.BlockSpec((ndp // steps, rows, WIDE), lambda i, s: (i, 0, 0)),)
            + (whole((nx, rows, WIDE)),) * nz,
            scratch_shapes=[pltpu.VMEM((ndp // steps, rows, WIDE), BF16)],
        ),
        compiler_params=params(60),
        cost_estimate=cost(12 * TOKENS * D * total, 12 << 20),
        name="units_grad",
    )(spot, mine, got, h, h_oth, top, top_oth)


def heads_grad_kernel(mine, got, heads, heads_got, h, h_oth, rows, rows_oth, gain1, gain2, out):
    count = 3 * SHARD // 2
    first = 0
    for left, left_got, right, right_oth in (
        (mine, got, h, h_oth),
        (heads, heads_got, rows, rows_oth),
    ):
        value = dot(left[...], right[...], NN) + dot(left_got[...], right_oth[...], NN)
        out[pl.ds(first, left.shape[0])] = value.astype(BF16)
        first += left.shape[0]
    out[count:] = jnp.zeros((out.shape[0] - count, WIDE), BF16)
    which = lax.broadcasted_iota(jnp.int32, (16, WIDE), 0)
    value = jnp.where(which == 0, gain1[...], jnp.where(which == 1, gain2[...], 0.0))
    out[pl.ds(count, 16)] = value.astype(BF16)


def heads_grad(*inputs):
    left = [whole(v.shape) for v in inputs[:4]]
    here = pl.BlockSpec((TOKENS, WIDE), lambda i: (0, i))
    there = pl.BlockSpec((TOKENS, WIDE), lambda i: (0, 1 - i))
    gain = pl.BlockSpec((1, WIDE), lambda i: (0, i))
    return pl.pallas_call(
        heads_grad_kernel,
        grid=(2,),
        out_shape=shape((640, D), BF16),
        in_specs=[*left, here, there, here, there, gain, gain],
        out_specs=pl.BlockSpec((640, WIDE), lambda i: (0, i)),
        compiler_params=params(60),
        cost_estimate=cost(6 * TOKENS * D * SHARD, 10 << 20),
        name="heads_grad",
    )(*inputs)


def fold_first_kernel(spot, left, *refs, nx, nz):
    rights, out, outs = refs[:nz], refs[nz], refs[nz + 1 :]
    total = left[:nz].astype(F32)
    for i in range(1, nx):
        total = total + left[i * nz : (i + 1) * nz].astype(F32)
    out[...] = total.astype(BF16)
    for k in range(nx):
        place = jnp.bitwise_xor(spot[8], k)
        total = rights[0][place].astype(F32)
        for right in rights[1:]:
            total = total + right[place].astype(F32)
        outs[k][...] = total.astype(BF16)


def fold_first(spot, left, rights, nx):
    nz = len(rights)
    dims = left.shape[1:]
    outs = (shape((nz, *dims), BF16),) + (shape(dims, BF16),) * nx
    kernel = functools.partial(fold_first_kernel, nx=nx, nz=nz)
    return stage(kernel, "fold_first", spot, (left, *rights), outs, 0, (), 16)


def fold_last_kernel(spot, left, *refs):
    rights, keep, send = refs[:-2], refs[-2], refs[-1]
    total = left[0].astype(F32)
    for i in range(1, left.shape[0]):
        total = total + left[i].astype(F32)
    other = rights[0][...].astype(F32)
    for right in rights[1:]:
        other = other + right[...].astype(F32)
    for j, value in enumerate((total.astype(BF16), other.astype(BF16))):
        low, high = value[:, :SHARD], value[:, SHARD:]

        @pl.when(spot[1] == 0)
        def _():
            keep[j], send[j] = low, high

        @pl.when(spot[1] == 1)
        def _():
            keep[j], send[j] = high, low


def fold_last(spot, left, rights):
    outs = (shape((2, left.shape[1], SHARD), BF16),) * 2
    return stage(fold_last_kernel, "fold_last", spot, (left, *rights), outs, 0, (), 16)


def fold_kernel(spot, value, keep, send):
    total = value[0].astype(F32)
    for i in range(1, value.shape[0]):
        total = total + value[i].astype(F32)
    total = total.astype(BF16)
    for j in range(2):
        low = total[:, j * WIDE : j * WIDE + SHARD]
        high = total[:, j * WIDE + SHARD : (j + 1) * WIDE]

        @pl.when(spot[1] == 0)
        def _():
            keep[j], send[j] = low, high

        @pl.when(spot[1] == 1)
        def _():
            keep[j], send[j] = high, low


def fold(spot, value):
    outs = (shape((2, value.shape[1], SHARD), BF16),) * 2
    return stage(fold_kernel, "fold", spot, (value,), outs, 0, (), 16)


def finish_units_kernel(spot, value, gate, up, lower, both):
    half = both.shape[0] // 4
    for j in range(value.shape[0]):
        span = pl.ds(j * 4 * half, 4 * half)
        for i, out in enumerate((gate, up, lower)):
            for place in range(4):
                low = jnp.bitwise_xor(spot[1], place % 2)
                core = jnp.bitwise_xor(spot[3], place // 2)
                rows = pl.ds(pl.multiple_of((2 * low + core) * half, half), half)
                both[rows] = value[j, place, pl.ds(i * half, half)]
            if i < 2:
                out[:, span] = both[...].astype(F32).T
            else:
                out[span] = both[...].astype(F32)


def finish_units(spot, value, steps):
    ndp = value.shape[0]
    half = value.shape[2] // 3
    cols = 4 * half * ndp // steps
    across = pl.BlockSpec((SHARD, cols), lambda i, s: (0, i))
    return pl.pallas_call(
        finish_units_kernel,
        out_shape=(shape((SHARD, cols * steps), F32),) * 2 + (shape((cols * steps, SHARD), F32),),
        grid_spec=pltpu.PrefetchScalarGridSpec(
            num_scalar_prefetch=1,
            grid=(steps,),
            in_specs=[pl.BlockSpec((ndp // steps, *value.shape[1:]), lambda i, s: (i, 0, 0, 0))],
            out_specs=(across, across, pl.BlockSpec((cols, SHARD), lambda i, s: (i, 0))),
            scratch_shapes=[pltpu.VMEM((4 * half, SHARD), BF16)],
        ),
        compiler_params=params(60),
        cost_estimate=cost(0, 14 << 20),
        name="finish_units",
    )(spot, value)


def finish_heads_kernel(spot, value, query, keyval, out, gains, part, full):
    count = value.shape[2]
    half = SHARD // 2
    total = jnp.zeros((8, SHARD), F32)
    for place in range(4):
        for i in range(value.shape[0]):
            part[pl.ds(i * count, count)] = value[i, place].astype(F32)
        low = jnp.bitwise_xor(spot[1], place % 2)
        core = jnp.bitwise_xor(spot[3], place // 2)
        rows = pl.ds(pl.multiple_of((2 * low + core) * half, half), half)
        for k in range(2):
            full[k, rows] = part[pl.ds(k * half, half)]
        out[rows] = part[pl.ds(2 * half, half)]
        total = total + part[pl.ds(3 * half, 8)]
    query[...] = full[0].T
    keyval[...] = full[1].T
    gains[...] = total


def finish_heads(spot, value):
    dims = ((SHARD, WIDE), (SHARD, WIDE), (WIDE, SHARD), (8, SHARD))
    scratch = [
        pltpu.VMEM((value.shape[0] * value.shape[2], SHARD), F32),
        pltpu.VMEM((2, WIDE, SHARD), F32),
    ]
    outs = tuple(shape(d, F32) for d in dims)
    return stage(finish_heads_kernel, "finish_heads", spot, (value,), outs, 0, scratch, 24)


def body(tokens, gain1, w_query, w_keyval, w_out, gain2, w_gate, w_up, w_down, grad_out, segments):
    core, yh, yl = lax.axis_index("core"), lax.axis_index("yhi"), lax.axis_index("ylo")
    nx, nz = lax.axis_size("x"), lax.axis_size("z")
    dp = lax.axis_index(DP)
    quarter = core ^ yh
    spot = jnp.stack(
        [yh, yl, 2 * yh + yl, core]
        + [place * QUARTER for place in (core, 3 - core, 1 - core, 2 + core)]
        + [lax.axis_index("x"), lax.axis_index("z"), dp]
    ).astype(jnp.int32)

    def pick(first_is_mine, own, other):
        return jnp.where(first_is_mine, own, other), jnp.where(first_is_mine, other, own)

    def halves_of(value):
        own = lax.dynamic_slice_in_dim(value, quarter * QUARTER, QUARTER, 0)
        return own, lax.dynamic_slice_in_dim(value, (1 - quarter) * QUARTER, QUARTER, 0)

    gains = jnp.stack([gain1, gain2])
    gains = jnp.stack([gains, swap(gains, "core")], axis=1)
    gains = jnp.stack(pick(yl == 0, gains, swap(gains, "ylo")), axis=2).reshape(2, 1, D)

    ids = segments[0]
    low_all = jnp.sum((ids[None, :] < ids[:, None]).astype(jnp.int32), axis=1)
    low = jnp.concatenate(
        [
            lax.dynamic_slice_in_dim(low_all, core * QUARTER, QUARTER),
            lax.dynamic_slice_in_dim(low_all, (3 - core) * QUARTER, QUARTER),
        ]
    )
    step = jnp.arange(QUARTER, dtype=jnp.int32)
    place = jnp.concatenate([core * QUARTER + step, (3 - core) * QUARTER + step])
    rates = THETA ** (-jnp.arange(HALF, dtype=F32) * 2.0 / HD)
    angles = rates[:, None] * (place - low).astype(F32)[None, :]
    cosine, sine = jnp.cos(angles), jnp.sin(angles)
    place, low = place[None, :], low[None, :]

    head_mine, head_send, unit_send, out_send = prepare(
        spot, w_query, w_keyval, w_gate, w_up, w_down, w_out, nx * nz
    )
    others = gather_dp(
        jnp.concatenate([swap_y(unit_send, 1), swap_y(out_send, 2), swap_y(out_send, 3)])
    )

    (x_own, x_other), (top_own, top_other) = halves_of(tokens[0]), halves_of(grad_out[0])
    got = swap(jnp.concatenate([x_other, top_other]), "core")
    pieces = peers_y(jnp.concatenate([x_own, got[:QUARTER]]))
    top_pair = jnp.concatenate([top_own, got[QUARTER:]])
    head_got = swap(head_send, "ylo")
    top_pair = jnp.broadcast_to(top_pair[None], (4, *top_pair.shape))
    *pieces, head_got, head_mine, gains, top_pair, cosine, sine, low = together(
        *pieces, head_got, head_mine, gains, top_pair, cosine, sine, low
    )
    head_pieces = (head_mine, head_got, swap(head_mine, "core"), swap(head_got, "core"))

    x, h_one, inv_one, queries, keyval, head_rows, head_rows_oth, x_block = project(
        spot, pieces, gains[0], head_pieces, cosine, sine
    )
    keyval_oth = swap(keyval, "core")
    top_pieces = over_y(after(top_pair, head_pieces[3]))
    others = after(others, queries)
    w_o = out_rows(spot, w_out, others)
    w_f = unit_rows(spot, w_gate, w_up, w_down, after(others, w_o))
    top_pieces, w_f, w_o, low, keyval_oth = together(top_pieces, w_f, w_o, low, keyval_oth)
    w_o_oth, w_f_oth = swap(w_o, "core"), swap(w_f, "core")
    heads_t, heads, lse, heads_mine, heads_send = attend(
        spot, queries, keyval, keyval_oth, place, low
    )
    heads_pieces = peers_y(heads)
    mixed, h_two, inv_two, mixed_block = mix(spot, x, heads_pieces, w_o, w_o_oth, gains[1])
    top, act, mine, send, parts = feed(spot, h_two, top_pieces, w_f, w_f_oth)
    parts = over_y(parts)

    got, h_two_oth, top_oth = swap(send, "core"), swap(h_two, "core"), swap(top, "core")
    left, *rights = units_grad(spot, mine, got, h_two, h_two_oth, top, top_oth, nx, nz)
    outs = down(spot, act, w_f, w_f_oth)
    parts, h_one_oth, left, *both = together(parts, swap(h_one, "core"), left, *rights, *outs)
    rights, outs = both[:nz], both[nz:]
    rows, gain2_part = residual(spot, parts, mixed, inv_two, top, gains[1])
    left = lax.all_to_all(left, "x", 0, 0, tiled=True)
    rights = to_peers(rights, "z")

    row_all, dq, dkv, dkv_oth, row_block = attend_back(
        spot, peers_y(rows), w_o, w_o_oth, queries, keyval, keyval_oth, heads_t, lse, place, low,
        cosine, sine,
    )
    dq, left, *rights = together(dq, left, *rights)
    left, *rights = fold_first(spot, left, rights, nx)
    left = lax.all_to_all(left, "z", 0, 0, tiled=True)
    rights = to_peers(rights, "x")
    raw, send, *parts, gain1_part = input_grad(
        spot, dq, dkv, swap(dkv_oth, "core"), cosine, sine, head_rows, head_rows_oth, x, inv_one
    )
    got = swap(send, "core")
    parts = to_peers_y(parts)

    sums = jnp.concatenate([gain1_part, gain2_part])
    sums = sums + swap(sums, "yhi")
    raw, got, row_all_oth, heads_got = together(
        raw, got, swap(row_all, "core"), swap(heads_send, "core")
    )
    head_parts = heads_grad(
        raw, got, heads_mine, heads_got, h_one, h_one_oth, row_all, row_all_oth,
        sums[:1], sums[1:],
    )
    head_parts, left, *rights = together(head_parts, left, *rights)
    head_parts = scatter_dp(head_parts.reshape(nx * nz, -1, D))
    keep, send = fold_last(spot, left, rights)
    low_got = swap(send, "ylo")

    def over_cores(keep, got):
        other = swap(jnp.stack([keep[1], got[1]]), "core")
        return jnp.stack([keep[0], got[0], other[0], other[1]])

    unit_parts = gather_dp(over_cores(keep, low_got))
    head_parts, *parts = together(head_parts, *parts)
    keep, send = fold(spot, head_parts)
    head_parts = gather_dp_now(over_cores(keep, swap(send, "ylo")))
    *outs, _ = together(*outs, keep)
    outs = to_peers_y(outs)

    got = sum([g.astype(F32) for g in parts])

    def to_home(block):
        return jnp.concatenate(pick(quarter == 0, block[0], swap(block[1], "core")))

    gain = jnp.stack(
        [lax.dynamic_slice(gains[0], (0, j * WIDE + yl * SHARD), (1, SHARD)) for j in range(2)]
    )
    inverse = lax.dynamic_slice_in_dim(inv_one, yh * QUARTER, QUARTER, 0)
    normed = x_block.astype(F32) * inverse
    scaled = got * gain
    inner = (scaled * normed).sum(axis=(0, 2))
    inner = (inner + swap(inner, "ylo"))[:, None] / D
    grad_in = to_home(row_block.astype(F32) + inverse * (scaled - normed * inner))

    output = mixed_block + sum([g.astype(F32) for g in outs])
    output = to_home(output.astype(BF16))

    grad_w_gate, grad_w_up, grad_w_down = finish_units(spot, unit_parts, nx)
    head_parts, grad_w_down = together(head_parts, grad_w_down)
    grad_w_query, grad_w_keyval, grad_w_out, sums = finish_heads(spot, head_parts)
    return (
        output[None],
        grad_in[None],
        sums[0],
        grad_w_query,
        grad_w_keyval,
        grad_w_out,
        sums[1],
        grad_w_gate,
        grad_w_up,
        grad_w_down,
    )


def solution(mesh):
    dp = mesh.shape["dp"]
    side = int(round(dp**0.5))
    fine = Mesh(
        mesh.devices.reshape(side, dp // side, 2, 2, 2), ("x", "z", "ylo", "core", "yhi")
    )
    seq, row, col = DP, ("ylo", "core"), "yhi"
    return jax.shard_map(
        body,
        mesh=fine,
        in_specs=(
            P(seq, col, row),
            P(row),
            P(row, col),
            P(row, col),
            P(col, row),
            P(row),
            P(row, col),
            P(row, col),
            P(col, row),
            P(seq, col, row),
            P(seq, None),
        ),
        out_specs=(
            P(seq, col, row),
            P(seq, col, row),
            P(row),
            P(row, col),
            P(row, col),
            P(col, row),
            P(row),
            P(row, col),
            P(row, col),
            P(col, row),
        ),
        check_vma=False,
    )
```
